32 devices in a mesh: groups: 2 (over x), serve: 16 (over z, y, core).
Axes of the slice: x: 2, y: 2, z: 4, core: 2. Of those that a mesh axis runs over, the one named last changes fastest.
Arguments:
- queries: bfloat16 [4096, 2560], P(('groups', 'serve')), parts along dimension 0, may hold values from -9 to 9
- new_kv: bfloat16 [32, 1, 2, 128, 512], P(('groups', 'serve')), parts along dimension 0, may hold values from -9 to 9
- pool: bfloat16 [512, 2, 128, 512], P(('groups', 'serve')), parts along dimension 0, may hold values from -9 to 9
- page_owner: int32 [32, 48], P(('groups', 'serve')), parts along dimension 0, may hold values from 0 to 15, as said below
- page_slot: int32 [32, 48], P(('groups', 'serve')), parts along dimension 0, may hold values from 0 to 15, as said below
- prefix_len: int32 [32], P(('groups', 'serve')), parts along dimension 0, may hold values from 3713 to 6144, as said below
- store_slot: int32 [32, 1], P(('groups', 'serve')), parts along dimension 0, may hold values from 0 to 15, as said below
Outputs:
- attended: bfloat16 [4096, 2560], P(('groups', 'serve')), parts along dimension 0
- pool_out: bfloat16 [512, 2, 128, 512], P(('groups', 'serve')), parts along dimension 0
The draws below stay inside these ranges and needn't reach their ends.
There are 2 independent parts, one for each index of `groups`. The reference program is written for one: setup_inputs(seed, part) draws one part's arguments, and reference() takes and returns one part's arrays. A program takes and returns all parts, laid end to end along the dimension named above; each array names one. Nothing has to cross between parts.
Inputs may be any that keep to these rules, and one draw needn't show every extreme that they name: `page_owner`: no request names its own index as owner, and a request names one owner at most 4 times among its first ceil(prefix_len / 128) entries; entries past those are 0 and are not read. `page_slot`: entries past a request's pages are 0 and are not read. `prefix_len`: some request has exactly 6144 cached tokens. `store_slot`: the 1 slots of a row are distinct.
All inputs are finite; a program needn't handle non-finite values.
Results may differ from the reference program's by a relative error of at most 0.0047.
Values may be sent and summed in bfloat16 or wider, within the bound.
No kernel may reach another device: no remote copies, remote signals or barrier semaphores. Data moves between devices by JAX's collectives and lax.ppermute only.
A program may use at most 128 MiB of HBM per device.

```python
import jax
import jax.numpy as jnp
from jax import lax

PAGE = 128
KVH = 4
GQ = 5
HD = 128
NEWP = 1
MAXP = 48
SLOTS = 16
HQ = 20
KVW = 512
SPAN = 128
REQUESTS = 16
TOKENS = 2048
POOL = 256


def request_plan(key):
    first, second, third, fourth, fifth = jax.random.split(key, 5)
    longest = jax.random.randint(first, (), 0, REQUESTS)
    low = max(5 * MAXP // 8, 1)
    marker = jnp.arange(REQUESTS) == longest
    counts = jax.random.randint(second, (REQUESTS,), low, MAXP + 1)
    counts = jnp.where(marker, MAXP, counts)
    tails = jax.random.randint(third, (REQUESTS,), 1, PAGE + 1)
    tails = jnp.where(marker, PAGE, tails)
    lengths = (counts - 1) * PAGE + tails
    order_keys = jax.random.split(fourth, REQUESTS)
    orders = jax.vmap(lambda k: jax.random.permutation(k, REQUESTS - 1))(order_keys)
    others = orders[:, jnp.arange(MAXP) % (REQUESTS - 1)]
    owners = others + (others >= jnp.arange(REQUESTS)[:, None]).astype(jnp.int32)
    slots = jax.random.randint(fifth, (REQUESTS, MAXP), 0, SLOTS)
    used = jnp.arange(MAXP)[None, :] < counts[:, None]
    zero = jnp.zeros_like(owners)
    return (jnp.where(used, owners, zero).astype(jnp.int32), jnp.where(used, slots, zero).astype(jnp.int32), lengths.astype(jnp.int32))


def draw_queries(key, part):
    key = jax.random.fold_in(key, 11)
    values = jnp.clip(jax.random.normal(key, (TOKENS, HQ * HD), jnp.float32), -9.0, 9.0)
    return values.astype(jnp.bfloat16)


def draw_new_kv(key, part):
    key = jax.random.fold_in(key, 12)
    values = jnp.clip(jax.random.normal(key, (REQUESTS * NEWP, 2, PAGE, KVW), jnp.float32), -9.0, 9.0)
    return values.reshape(REQUESTS, NEWP, 2, PAGE, KVW).astype(jnp.bfloat16)


def draw_pool(key, part):
    key = jax.random.fold_in(key, 13)
    values = jnp.clip(jax.random.normal(key, (POOL, 2, PAGE, KVW), jnp.float32), -9.0, 9.0)
    return values.astype(jnp.bfloat16)


def draw_page_owner(key, part):
    return request_plan(key)[0]


def draw_page_slot(key, part):
    return request_plan(key)[1]


def draw_prefix_len(key, part):
    return request_plan(key)[2]


def draw_store_slot(key, part):
    key = jax.random.fold_in(key, 14)
    row_keys = jax.random.split(key, REQUESTS)
    orders = jax.vmap(lambda k: jax.random.permutation(k, SLOTS))(row_keys)
    return orders[:, :NEWP].astype(jnp.int32)


def setup_inputs(seed: int = 0, part: int = 0) -> dict:
    seeds = jax.random.split(jax.random.key(seed), 8)
    part_keys = jax.random.split(jax.random.fold_in(seeds[7], part), 8)
    queries = draw_queries(jax.random.fold_in(jax.random.fold_in(seeds[7], part), 71), part)
    new_kv = draw_new_kv(jax.random.fold_in(jax.random.fold_in(seeds[7], part), 71), part)
    pool = draw_pool(jax.random.fold_in(jax.random.fold_in(seeds[7], part), 71), part)
    page_owner = draw_page_owner(jax.random.fold_in(jax.random.fold_in(seeds[7], part), 71), part)
    page_slot = draw_page_slot(jax.random.fold_in(jax.random.fold_in(seeds[7], part), 71), part)
    prefix_len = draw_prefix_len(jax.random.fold_in(jax.random.fold_in(seeds[7], part), 71), part)
    store_slot = draw_store_slot(jax.random.fold_in(jax.random.fold_in(seeds[7], part), 71), part)
    return {"queries": queries, "new_kv": new_kv, "pool": pool, "page_owner": page_owner, "page_slot": page_slot, "prefix_len": prefix_len, "store_slot": store_slot}


def heads_major(rows, heads):
    return rows.reshape(rows.shape[0], heads, HD).transpose(1, 0, 2)


def partial_attend(query_heads, key_heads, value_heads, valid):
    scale = HD ** -0.5

    def one_head(operands):
        query, keys, values = operands
        scores = jnp.dot(query, keys.T, preferred_element_type=jnp.float32) * scale
        scores = jnp.where(valid, scores, -1e30)
        top = jnp.max(scores, axis=1)
        expo = jnp.exp(scores - top[:, None])
        total = jnp.sum(expo, axis=1)
        accum = jnp.dot(expo.astype(jnp.bfloat16), values, preferred_element_type=jnp.float32)
        return top, total, accum

    return lax.map(one_head, (query_heads, key_heads, value_heads))


def merge_parts(first, second):
    top = jnp.maximum(first[0], second[0])
    scale_one = jnp.exp(first[0] - top)
    scale_two = jnp.exp(second[0] - top)
    denom = scale_one * first[1] + scale_two * second[1]
    return (scale_one[..., None] * first[2] + scale_two[..., None] * second[2]) / denom[..., None]


def reference(queries, new_kv, pool, page_owner, page_slot, prefix_len, store_slot):
    rows = GQ * SPAN
    span_valid = jnp.arange(SPAN)[None, :] <= (jnp.arange(rows) % SPAN)[:, None]

    def one_request(index):
        block = lax.dynamic_slice_in_dim(queries, index * SPAN, SPAN, 0)
        query_heads = block.reshape(SPAN, KVH, GQ, HD).transpose(1, 2, 0, 3).reshape(KVH, rows, HD)
        where_pages = page_owner[index] * SLOTS + page_slot[index]
        pages = jnp.take(pool, where_pages.astype(jnp.int32), axis=0)
        prefix_keys = heads_major(pages[:, 0].reshape(MAXP * PAGE, KVW), KVH)
        prefix_values = heads_major(pages[:, 1].reshape(MAXP * PAGE, KVW), KVH)
        prefix_valid = (jnp.arange(MAXP * PAGE) < prefix_len[index])[None, :]
        fresh = new_kv[index]
        span_keys = heads_major(fresh[:, 0].reshape(SPAN, KVW), KVH)
        span_values = heads_major(fresh[:, 1].reshape(SPAN, KVW), KVH)
        first = partial_attend(query_heads, prefix_keys, prefix_values, prefix_valid)
        second = partial_attend(query_heads, span_keys, span_values, span_valid)
        merged = merge_parts(first, second)
        merged = merged.reshape(KVH, GQ, SPAN, HD).transpose(2, 0, 1, 3).reshape(SPAN, HQ * HD)
        return merged.astype(jnp.bfloat16)

    attended = lax.map(one_request, jnp.arange(REQUESTS, dtype=jnp.int32)).reshape(TOKENS, HQ * HD)
    incoming = jnp.roll(new_kv, 1, axis=0).reshape(REQUESTS * NEWP, 2, PAGE, KVW)
    target = (jnp.arange(REQUESTS, dtype=jnp.int32)[:, None] * SLOTS + store_slot).reshape(-1)
    pool_out = pool.at[target.astype(jnp.int32)].set(incoming)
    return attended, pool_out
```

```python
import functools

import jax
import jax.numpy as jnp
from jax import lax
from jax.experimental import pallas as pl
from jax.experimental.pallas import tpu as pltpu
from jax.sharding import PartitionSpec as P

PAGE = 128
KVH = 4
GQ = 5
HD = 128
MAXP = 48
SCALE = HD ** (-0.5)
LOG2E = 1.4426950408889634
LOW = -1e30
CLUSTER = 4
STAT = 16
ROWS = GQ * PAGE + STAT


def swapped(array, axis, bit):
    size = lax.axis_size(axis)
    return lax.ppermute(array, axis, [(i, i ^ bit) for i in range(size)])


def shifted(array, axis, by):
    size = lax.axis_size(axis)
    return lax.ppermute(array, axis, [(i, (i + by) % size) for i in range(size)])


def attend_kernel(
    picks, counts, lasts, mine,
    q_ref, own_ref, side_ref, twin_ref, fresh_ref,
    out_ref,
    pages, scores, tops, acc, sems,
):
    line = pl.program_id(0)
    slots = own_ref.shape[0]

    @pl.when(line == 0)
    def _():
        copies = [
            pltpu.make_async_copy(own_ref, pages.at[pl.ds(0, slots)], sems.at[0]),
            pltpu.make_async_copy(twin_ref.at[0], pages.at[pl.ds(slots, slots)], sems.at[1]),
            pltpu.make_async_copy(side_ref, pages.at[pl.ds(2 * slots, slots)], sems.at[2]),
            pltpu.make_async_copy(twin_ref.at[1], pages.at[pl.ds(3 * slots, slots)], sems.at[3]),
            pltpu.make_async_copy(fresh_ref, pages.at[4 * slots], sems.at[4]),
        ]
        for copy in copies:
            copy.start()
        for copy in copies:
            copy.wait()

    count = counts[line]
    pairs = (count + 1) // 2
    contract_last = (((1,), (1,)), ((), ()))
    tops[...] = jnp.full(tops.shape, LOW, jnp.float32)
    acc[...] = jnp.zeros(acc.shape, jnp.float32)
    own_line = line == mine[0]

    def pair_of(index, part):
        first = pages[picks[line, 2 * index], part]
        second = pages[picks[line, 2 * index + 1], part]
        return jnp.concatenate([first, second], axis=0)

    def score_pair(index, limit):
        keys = pair_of(index, 0)
        for h in range(GQ):
            query = q_ref[0, :, h * HD:(h + 1) * HD]
            s = lax.dot_general(query, keys, contract_last, preferred_element_type=jnp.float32)
            if limit is not None:
                s = jnp.where(lax.broadcasted_iota(jnp.int32, s.shape, 1) < limit, s, LOW)
            scores[index, h] = s
            tops[h] = jnp.maximum(tops[h], jnp.maximum(s[:, :PAGE], s[:, PAGE:]))

    @pl.loop(0, jnp.maximum(pairs - 1, 0))
    def _(index):
        score_pair(index, None)

    @pl.when(pairs > 0)
    def _():
        score_pair(pairs - 1, (count - 2 * pairs + 1) * PAGE + lasts[line])

    @pl.when(own_line)
    def _():
        keys = pages[4 * slots, 0]
        for h in range(GQ):
            query = q_ref[0, :, h * HD:(h + 1) * HD]
            s = lax.dot_general(query, keys, contract_last, preferred_element_type=jnp.float32)
            seen = lax.broadcasted_iota(jnp.int32, s.shape, 1) <= lax.broadcasted_iota(jnp.int32, s.shape, 0)
            s = jnp.where(seen, s, LOW)
            scores[pairs, h, :, :PAGE] = s
            tops[h] = jnp.maximum(tops[h], s)

    for h in range(GQ):
        top = jnp.max(tops[h], axis=1, keepdims=True)
        tops[h] = jnp.broadcast_to(top, (PAGE, PAGE))

    factor = SCALE * LOG2E

    @pl.loop(0, pairs)
    def _(index):
        values = pair_of(index, 1)
        values = jnp.concatenate([values, jnp.ones_like(values)], axis=1)
        for h in range(GQ):
            top = tops[h]
            expo = jnp.exp2((scores[index, h] - jnp.concatenate([top, top], axis=1)) * factor)
            acc[h] += jnp.dot(expo.astype(jnp.bfloat16), values, preferred_element_type=jnp.float32)

    @pl.when(own_line)
    def _():
        values = pages[4 * slots, 1]
        values = jnp.concatenate([values, jnp.ones_like(values)], axis=1)
        for h in range(GQ):
            expo = jnp.exp2((scores[pairs, h, :, :PAGE] - tops[h]) * factor)
            acc[h] += jnp.dot(expo.astype(jnp.bfloat16), values, preferred_element_type=jnp.float32)

    lane = lax.broadcasted_iota(jnp.int32, (PAGE, PAGE), 1)
    stat = jnp.zeros((PAGE, PAGE), jnp.float32)
    for h in range(GQ):
        total = acc[h, :, HD:]
        some = total > 0.0
        total = jnp.where(some, total, 1.0)
        out_ref[0, h * PAGE:(h + 1) * PAGE, :] = (acc[h, :, :HD] / total).astype(jnp.bfloat16)
        level = jnp.where(some, tops[h] * SCALE + jnp.log(total), LOW)
        high = level.astype(jnp.bfloat16).astype(jnp.float32)
        middle = (level - high).astype(jnp.bfloat16).astype(jnp.float32)
        low = level - high - middle
        stat = jnp.where(lane == h, high, stat)
        stat = jnp.where(lane == GQ + h, middle, stat)
        stat = jnp.where(lane == 2 * GQ + h, low, stat)
    out_ref[0, GQ * PAGE:, :] = stat.T[:STAT].astype(jnp.bfloat16)


def attend(picks, counts, lasts, mine, q, own, side, twin, fresh):
    lines = q.shape[0]
    slots = own.shape[0]
    pairs = (picks.shape[1] + 1) // 2
    keys = picks.shape[1] * PAGE
    grid_spec = pltpu.PrefetchScalarGridSpec(
        num_scalar_prefetch=4,
        grid=(lines,),
        in_specs=[
            pl.BlockSpec((1, PAGE, GQ * HD), lambda l, *_: (l, 0, 0)),
            pl.BlockSpec(memory_space=pl.ANY),
            pl.BlockSpec(memory_space=pl.ANY),
            pl.BlockSpec(memory_space=pl.ANY),
            pl.BlockSpec(memory_space=pl.ANY),
        ],
        out_specs=pl.BlockSpec((1, ROWS, HD), lambda l, *_: (l, 0, 0)),
        scratch_shapes=[
            pltpu.VMEM((CLUSTER * slots + 1, 2, PAGE, HD), jnp.bfloat16),
            pltpu.VMEM((pairs + 1, GQ, PAGE, 2 * PAGE), jnp.float32),
            pltpu.VMEM((GQ, PAGE, PAGE), jnp.float32),
            pltpu.VMEM((GQ, PAGE, 2 * HD), jnp.float32),
            pltpu.SemaphoreType.DMA((5,)),
        ],
    )
    return pl.pallas_call(
        attend_kernel,
        grid_spec=grid_spec,
        out_shape=jax.ShapeDtypeStruct((lines, ROWS, HD), jnp.bfloat16),
        compiler_params=pltpu.CompilerParams(vmem_limit_bytes=32 * 2**20),
        cost_estimate=pl.CostEstimate(
            flops=lines * 4 * GQ * PAGE * keys * HD,
            bytes_accessed=(2 * q.size + 8 * own.size + 2 * lines * ROWS * HD),
            transcendentals=lines * GQ * PAGE * keys,
        ),
    )(picks, counts, lasts, mine, q, own, side, twin, fresh)


def merge_kernel(part_ref, out_ref):
    clusters = part_ref.shape[0]
    levels = []
    for i in range(clusters):
        block = part_ref[i, GQ * PAGE:, :].astype(jnp.float32)
        levels.append(block[:GQ] + block[GQ:2 * GQ] + block[2 * GQ:3 * GQ])
    top = functools.reduce(jnp.maximum, levels)
    weights = [jnp.exp(level - top) for level in levels]
    total = functools.reduce(jnp.add, weights)
    weights = [weight / total for weight in weights]
    filler = PAGE - clusters * GQ
    table = jnp.concatenate(weights + [jnp.zeros((filler, PAGE), jnp.float32)], axis=0).T
    for h in range(GQ):
        merged = jnp.zeros((PAGE, HD), jnp.float32)
        for i in range(clusters):
            column = i * GQ + h
            part = part_ref[i, h * PAGE:(h + 1) * PAGE, :].astype(jnp.float32)
            merged += table[:, column:column + 1] * part
        out_ref[:, h * HD:(h + 1) * HD] = merged.astype(jnp.bfloat16)


def merge(parts):
    return pl.pallas_call(
        merge_kernel,
        out_shape=jax.ShapeDtypeStruct((PAGE, GQ * HD), jnp.bfloat16),
        cost_estimate=pl.CostEstimate(
            flops=2 * parts.size, bytes_accessed=2 * parts.size + 2 * PAGE * GQ * HD, transcendentals=0
        ),
    )(parts)


def per_device(queries, new_kv, pool, page_owner, page_slot, prefix_len, store_slot):
    width = lax.axis_size("serve")
    lines = width // CLUSTER
    me = lax.axis_index("serve")
    slots = pool.shape[0]
    capacity = (MAXP + width - 2) // (width - 1)
    limit = min(MAXP, CLUSTER * capacity)
    limit += limit % 2
    groups = [[c * CLUSTER + i for c in range(lines)] for i in range(CLUSTER)]

    table = jnp.concatenate([page_owner[0], page_slot[0], prefix_len])[None]
    tables = lax.all_gather(table, "serve", axis_index_groups=groups, tiled=True)
    owners = tables[:, :MAXP]
    places = tables[:, MAXP:2 * MAXP]
    length = tables[:, 2 * MAXP]
    used = (length + PAGE - 1) // PAGE
    spot = jnp.arange(MAXP)
    here = (spot[None] < used[:, None]) & (owners // CLUSTER == me // CLUSTER)
    hits = here.astype(jnp.int32)
    before = jnp.sum(hits[:, None, :] * (spot[None, None, :] < spot[None, :, None]), axis=2)
    local = ((owners % CLUSTER) ^ (me % CLUSTER)) * slots + places
    chosen = here[:, :, None] & (before[:, :, None] == jnp.arange(limit)[None, None, :])
    picks = jnp.sum(jnp.where(chosen, local[:, :, None], 0), axis=1)
    counts = jnp.sum(hits, axis=1)
    tail = jnp.sum(jnp.where(here & (spot[None] == used[:, None] - 1), 1, 0), axis=1)
    lasts = jnp.where(tail > 0, length - (used - 1) * PAGE, PAGE)
    mine = (me // CLUSTER)[None]

    fresh = new_kv[0, 0]
    outs = []
    for g in range(KVH):
        columns = slice(g * HD, (g + 1) * HD)
        own = pool[:, :, :, columns]
        side = swapped(own, "serve", 2)
        twin = swapped(jnp.stack([own, side]), "serve", 1)
        q = queries[:, g * GQ * HD:(g + 1) * GQ * HD][None]
        q = lax.all_gather(q, "serve", axis_index_groups=groups, tiled=True)
        parts = attend(picks, counts, lasts, mine, q, own, side, twin, fresh[:, :, columns])
        parts = lax.all_to_all(parts, "serve", 0, 0, axis_index_groups=groups, tiled=True)
        outs.append(merge(parts))
    attended = jnp.concatenate(outs, axis=1)
    incoming = shifted(new_kv[0], "serve", 1)
    pool_out = pool.at[store_slot[0]].set(incoming)
    return (attended, pool_out)


def solution(mesh):
    return jax.shard_map(
        per_device,
        mesh=mesh,
        in_specs=(
            P(("groups", "serve"), None),
            P(("groups", "serve"), None, None, None, None),
            P(("groups", "serve"), None, None, None),
            P(("groups", "serve"), None),
            P(("groups", "serve"), None),
            P(("groups", "serve")),
            P(("groups", "serve"), None),
        ),
        out_specs=(P(("groups", "serve"), None), P(("groups", "serve"), None, None, None)),
        check_vma=False,
    )
```

```python
import functools

import jax
import jax.numpy as jnp
from jax import lax
from jax.experimental import pallas as pl
from jax.experimental.pallas import tpu as pltpu
from jax.sharding import PartitionSpec as P

PAGE = 128
KVH = 4
GQ = 5
HD = 128
MAXP = 48
SCALE = HD ** (-0.5)
LOG2E = 1.4426950408889634
LOW = -1e30
CLUSTER = 4
BLOCK = 4
STAT = 16
ROWS = GQ * PAGE + STAT
CHUNK = GQ * HD
CONTRACT_LAST = (((1,), (1,)), ((), ()))


def swapped(array, axis, bit):
    size = lax.axis_size(axis)
    return lax.ppermute(array, axis, [(i, i ^ bit) for i in range(size)])


def shifted(array, axis, by):
    size = lax.axis_size(axis)
    return lax.ppermute(array, axis, [(i, (i + by) % size) for i in range(size)])


def attend_kernel(lines, head, q_head, picks, counts, lasts, mine, *refs):
    own_q, *other_q = refs[:lines]
    own, twin, side, both, fresh = refs[lines:lines + 5]
    outs = refs[lines + 5:2 * lines + 5]
    pages, queries, results, tops, acc, q_sems, page_sems, out_sems = refs[2 * lines + 5:]
    slots = own.shape[0]
    columns = pl.ds(head * HD, HD)
    extra = pages.shape[1] - 1

    q_copies = [pltpu.make_async_copy(own_q.at[:, pl.ds(head * CHUNK, CHUNK)], queries.at[0], q_sems.at[0])]
    for t in range(1, lines):
        q_copies.append(
            pltpu.make_async_copy(other_q[t - 1].at[:, pl.ds(q_head * CHUNK, CHUNK)], queries.at[t], q_sems.at[t])
        )
    for copy in q_copies:
        copy.start()
    pages[...] = jnp.zeros(pages.shape, pages.dtype)
    fresh_copy = pltpu.make_async_copy(fresh.at[:, :, columns], pages.at[0, extra], page_sems.at[0, extra])
    fresh_copy.start()

    def request_of(t):
        return lax.rem(mine[0] - t + lines, lines)

    def page_copy(source, slot, buffer, place):
        if source.shape[-1] == HD:
            origin = source.at[slot]
        else:
            origin = source.at[slot, :, :, columns]
        return pltpu.make_async_copy(origin, pages.at[buffer, place], page_sems.at[buffer, place])

    def fetch(t):
        request = request_of(t)
        buffer = lax.rem(t, 2)

        @pl.loop(0, counts[request])
        def _(place):
            code = picks[request, place]
            rank = lax.div(code, slots)
            slot = lax.rem(code, slots)
            for index, source in enumerate((own, twin, side, both)):
                @pl.when(rank == index)
                def _():
                    page_copy(source, slot, buffer, place).start()

    def arrive(t):
        buffer = lax.rem(t, 2)

        @pl.loop(0, counts[request_of(t)])
        def _(place):
            page_copy(own, 0, buffer, place).wait()

    def update(h, s, values):
        old = tops[h]
        new = jnp.maximum(old, jnp.max(s, axis=1, keepdims=True))
        tops[h] = new
        factor = SCALE * LOG2E
        fade = jnp.exp2((old - new) * factor)
        wide = jnp.concatenate([new] * (s.shape[1] // PAGE), axis=1)
        expo = jnp.exp2((s - wide) * factor).astype(jnp.bfloat16)
        fresh_acc = jnp.dot(expo, values, preferred_element_type=jnp.float32)
        acc[h] = acc[h] * jnp.concatenate([fade, fade], axis=1) + fresh_acc

    def with_ones(values):
        return jnp.concatenate([values, jnp.ones_like(values)], axis=1)

    def attend_block(t, buffer, index, limit):
        block = pages[buffer, pl.ds(index * BLOCK, BLOCK)]
        keys = block[:, 0].reshape(BLOCK * PAGE, HD)
        values = with_ones(block[:, 1].reshape(BLOCK * PAGE, HD))
        for h in range(GQ):
            query = queries[t, :, h * HD:(h + 1) * HD]
            s = lax.dot_general(query, keys, CONTRACT_LAST, preferred_element_type=jnp.float32)
            if limit is not None:
                s = jnp.where(lax.broadcasted_iota(jnp.int32, s.shape, 1) < limit, s, LOW)
            update(h, s, values)

    fetch(0)
    for copy in q_copies:
        copy.wait()
    fresh_copy.wait()

    @pl.loop(0, lines)
    def _(t):
        buffer = lax.rem(t, 2)
        request = request_of(t)
        count = counts[request]
        blocks = lax.div(count + BLOCK - 1, BLOCK)

        @pl.when(t + 1 < lines)
        def _():
            fetch(t + 1)

        tops[...] = jnp.full(tops.shape, LOW, jnp.float32)
        acc[...] = jnp.zeros(acc.shape, jnp.float32)

        @pl.when(t == 0)
        def _():
            keys = pages[0, extra, 0]
            values = with_ones(pages[0, extra, 1])
            for h in range(GQ):
                query = queries[0, :, h * HD:(h + 1) * HD]
                s = lax.dot_general(query, keys, CONTRACT_LAST, preferred_element_type=jnp.float32)
                seen = lax.broadcasted_iota(jnp.int32, s.shape, 1) <= lax.broadcasted_iota(jnp.int32, s.shape, 0)
                update(h, jnp.where(seen, s, LOW), values)

        arrive(t)

        @pl.loop(0, jnp.maximum(blocks - 1, 0))
        def _(index):
            attend_block(t, buffer, index, None)

        @pl.when(blocks > 0)
        def _():
            last = blocks - 1
            attend_block(t, buffer, last, (count - 1 - last * BLOCK) * PAGE + lasts[request])

        lane = lax.broadcasted_iota(jnp.int32, (PAGE, PAGE), 1)
        stat = jnp.zeros((PAGE, PAGE), jnp.float32)
        for h in range(GQ):
            total = acc[h, :, HD:]
            some = total > 0.0
            total = jnp.where(some, total, 1.0)
            results[t, h * PAGE:(h + 1) * PAGE, :] = (acc[h, :, :HD] / total).astype(jnp.bfloat16)
            level = jnp.where(some, tops[h] * SCALE + jnp.log(total), LOW)
            high = level.astype(jnp.bfloat16).astype(jnp.float32)
            middle = (level - high).astype(jnp.bfloat16).astype(jnp.float32)
            low = level - high - middle
            stat = jnp.where(lane == h, high, stat)
            stat = jnp.where(lane == GQ + h, middle, stat)
            stat = jnp.where(lane == 2 * GQ + h, low, stat)
        results[t, GQ * PAGE:, :] = stat.T[:STAT].astype(jnp.bfloat16)
        for index in range(lines):
            @pl.when(t == index)
            def _():
                pltpu.make_async_copy(results.at[index], outs[index], out_sems.at[index]).start()

    for index in range(lines):
        pltpu.make_async_copy(results.at[index], outs[index], out_sems.at[index]).wait()


def attend(head, q_head, tables, queries, pools, fresh):
    picks, counts, lasts, mine = tables
    lines = len(queries)
    places = picks.shape[1]
    keys = places * PAGE * 5 // 8
    grid_spec = pltpu.PrefetchScalarGridSpec(
        num_scalar_prefetch=4,
        grid=(),
        in_specs=[pl.BlockSpec(memory_space=pl.ANY)] * (lines + 5),
        out_specs=[pl.BlockSpec(memory_space=pl.ANY)] * lines,
        scratch_shapes=[
            pltpu.VMEM((2, places + 1, 2, PAGE, HD), jnp.bfloat16),
            pltpu.VMEM((lines, PAGE, CHUNK), jnp.bfloat16),
            pltpu.VMEM((lines, ROWS, HD), jnp.bfloat16),
            pltpu.VMEM((GQ, PAGE, PAGE), jnp.float32),
            pltpu.VMEM((GQ, PAGE, 2 * HD), jnp.float32),
            pltpu.SemaphoreType.DMA((lines,)),
            pltpu.SemaphoreType.DMA((2, places + 1)),
            pltpu.SemaphoreType.DMA((lines,)),
        ],
    )
    return pl.pallas_call(
        functools.partial(attend_kernel, lines, head, q_head),
        grid_spec=grid_spec,
        out_shape=[jax.ShapeDtypeStruct((ROWS, HD), jnp.bfloat16)] * lines,
        compiler_params=pltpu.CompilerParams(vmem_limit_bytes=24 * 2**20),
        cost_estimate=pl.CostEstimate(
            flops=lines * 4 * GQ * PAGE * keys * HD,
            bytes_accessed=lines * keys * 4 * HD + lines * 2 * (CHUNK * PAGE + ROWS * HD),
            transcendentals=lines * GQ * PAGE * keys,
        ),
    )(picks, counts, lasts, mine, *queries, *pools, fresh)


def merge_kernel(lines, head, *refs):
    parts = refs[:lines]
    out, result, sem = refs[-3:]
    levels = []
    for part in parts:
        block = part[GQ * PAGE:, :].astype(jnp.float32)
        levels.append(block[:GQ] + block[GQ:2 * GQ] + block[2 * GQ:3 * GQ])
    top = functools.reduce(jnp.maximum, levels)
    weights = [jnp.exp(level - top) for level in levels]
    total = functools.reduce(jnp.add, weights)
    weights = [weight / total for weight in weights]
    filler = PAGE - lines * GQ
    table = jnp.concatenate(weights + [jnp.zeros((filler, PAGE), jnp.float32)], axis=0).T
    for h in range(GQ):
        merged = jnp.zeros((PAGE, HD), jnp.float32)
        for i, part in enumerate(parts):
            column = i * GQ + h
            merged += table[:, column:column + 1] * part[h * PAGE:(h + 1) * PAGE, :].astype(jnp.float32)
        result[:, h * HD:(h + 1) * HD] = merged.astype(jnp.bfloat16)
    copy = pltpu.make_async_copy(result, out.at[:, pl.ds(head * CHUNK, CHUNK)], sem)
    copy.start()
    copy.wait()


def merge(head, parts, whole):
    lines = len(parts)
    before = [] if whole is None else [whole]
    return pl.pallas_call(
        functools.partial(merge_kernel, lines, head),
        in_specs=[pl.BlockSpec(memory_space=pltpu.VMEM)] * lines + [pl.BlockSpec(memory_space=pl.ANY)] * len(before),
        out_specs=pl.BlockSpec(memory_space=pl.ANY),
        out_shape=jax.ShapeDtypeStruct((PAGE, KVH * CHUNK), jnp.bfloat16),
        scratch_shapes=[pltpu.VMEM((PAGE, CHUNK), jnp.bfloat16), pltpu.SemaphoreType.DMA],
        input_output_aliases={lines: 0} if before else {},
        cost_estimate=pl.CostEstimate(
            flops=2 * lines * ROWS * HD, bytes_accessed=2 * (lines + 1) * ROWS * HD, transcendentals=0
        ),
    )(*parts, *before)


def page_tables(me, width, slots, page_owner, page_slot, prefix_len):
    lines = width // CLUSTER
    capacity = (MAXP + width - 2) // (width - 1)
    limit = min(MAXP, CLUSTER * capacity)
    groups = [[c * CLUSTER + i for c in range(lines)] for i in range(CLUSTER)]
    table = jnp.concatenate([page_owner[0], page_slot[0], prefix_len])[None]
    tables = lax.all_gather(table, "serve", axis_index_groups=groups, tiled=True)
    owners = tables[:, :MAXP]
    places = tables[:, MAXP:2 * MAXP]
    length = tables[:, 2 * MAXP]
    used = (length + PAGE - 1) // PAGE
    spot = jnp.arange(MAXP)
    here = (spot[None] < used[:, None]) & (owners // CLUSTER == me // CLUSTER)
    hits = here.astype(jnp.int32)
    before = jnp.sum(hits[:, None, :] * (spot[None, None, :] < spot[None, :, None]), axis=2)
    local = ((owners % CLUSTER) ^ (me % CLUSTER)) * slots + places
    chosen = here[:, :, None] & (before[:, :, None] == jnp.arange(limit)[None, None, :])
    picks = jnp.sum(jnp.where(chosen, local[:, :, None], 0), axis=1)
    counts = jnp.sum(hits, axis=1)
    tail = jnp.sum(jnp.where(here & (spot[None] == used[:, None] - 1), 1, 0), axis=1)
    lasts = jnp.where(tail > 0, length - (used - 1) * PAGE, PAGE)
    return picks, counts, lasts, (me // CLUSTER)[None]


def per_device(queries, new_kv, pool, page_owner, page_slot, prefix_len, store_slot):
    width = lax.axis_size("serve")
    lines = width // CLUSTER
    me = lax.axis_index("serve")
    slots = pool.shape[0]
    tables = page_tables(me, width, slots, page_owner, page_slot, prefix_len)
    fresh = new_kv[0, 0]
    sides = [swapped(pool[:, :, :, g * HD:(g + 1) * HD], "serve", 2) for g in range(KVH)]
    early = [shifted(queries[:, :CHUNK], "serve", t * CLUSTER) for t in range(1, lines)]
    twin = swapped(pool, "serve", 1)
    later = [shifted(queries[:, CHUNK:], "serve", t * CLUSTER) for t in range(1, lines)]
    incoming = shifted(new_kv[0], "serve", 1)
    attended = None
    for g in range(KVH):
        both = swapped(sides[g], "serve", 1)
        others = early if g == 0 else later
        parts = attend(g, max(g - 1, 0), tables, [queries] + others, (pool, twin, sides[g], both), fresh)
        parts = [part if t == 0 else shifted(part, "serve", -t * CLUSTER) for t, part in enumerate(parts)]
        attended = merge(g, parts, attended)
    pool_out = pool.at[store_slot[0]].set(incoming)
    return (attended, pool_out)


def solution(mesh):
    return jax.shard_map(
        per_device,
        mesh=mesh,
        in_specs=(
            P(("groups", "serve"), None),
            P(("groups", "serve"), None, None, None, None),
            P(("groups", "serve"), None, None, None),
            P(("groups", "serve"), None),
            P(("groups", "serve"), None),
            P(("groups", "serve")),
            P(("groups", "serve"), None),
        ),
        out_specs=(P(("groups", "serve"), None), P(("groups", "serve"), None, None, None)),
        check_vma=False,
    )
```

```python
import functools

import jax
import jax.numpy as jnp
from jax import lax
from jax.experimental import pallas as pl
from jax.experimental.pallas import tpu as pltpu
from jax.sharding import PartitionSpec as P

PAGE = 128
KVH = 4
GQ = 5
HD = 128
MAXP = 48
SCALE = HD ** (-0.5)
LOG2E = 1.4426950408889634
LOW = -1e30
CLUSTER = 4
BLOCK = 4
STAT = 16
ROWS = GQ * PAGE + STAT
CHUNK = GQ * HD
CONTRACT_LAST = (((1,), (1,)), ((), ()))


def swapped(array, axis, bit):
    size = lax.axis_size(axis)
    return lax.ppermute(array, axis, [(i, i ^ bit) for i in range(size)])


def shifted(array, axis, by):
    size = lax.axis_size(axis)
    return lax.ppermute(array, axis, [(i, (i + by) % size) for i in range(size)])


def attend_kernel(lines, head, q_head, picks, counts, lasts, mine, store, *refs):
    q_all, own, twin, side, both, fresh = refs[:6]
    stores = len(refs) == 19
    if stores:
        incoming, out, pool_out = refs[6:9]
        store_sems = refs[-1]
        scratch = refs[9:-1]
    else:
        out = refs[6]
        scratch = refs[7:]
    pages, queries, results, scores, tops, acc, q_sems, page_sems, out_sems = scratch
    slots = own.shape[0]
    columns = pl.ds(head * HD, HD)
    extra = pages.shape[1] - 1

    def request_of(t):
        return lax.rem(mine[0] - t + lines, lines)

    def q_copy(t):
        origin = q_all.at[request_of(t), :, pl.ds(q_head * CHUNK, CHUNK)]
        return pltpu.make_async_copy(origin, queries.at[t], q_sems.at[t])

    def out_copy(t):
        return pltpu.make_async_copy(results.at[t], out.at[request_of(t)], out_sems.at[t])

    def page_copy(source, slot, buffer, place):
        if source.shape[-1] == HD:
            origin = source.at[slot]
        else:
            origin = source.at[slot, :, :, columns]
        return pltpu.make_async_copy(origin, pages.at[buffer, place], page_sems.at[buffer, place])

    def fetch(t):
        request = request_of(t)
        buffer = lax.rem(t, 2)

        @pl.loop(0, counts[request])
        def _(place):
            code = picks[request, place]
            rank = lax.div(code, slots)
            slot = lax.rem(code, slots)
            for index, source in enumerate((own, twin, side, both)):
                @pl.when(rank == index)
                def _():
                    page_copy(source, slot, buffer, place).start()

    def arrive(t):
        buffer = lax.rem(t, 2)

        @pl.loop(0, counts[request_of(t)])
        def _(place):
            page_copy(own, 0, buffer, place).wait()

    def store_copy(slot):
        return pltpu.make_async_copy(own.at[slot], pool_out.at[slot], store_sems.at[slot])

    fresh_copy = pltpu.make_async_copy(fresh.at[:, :, columns], pages.at[0, extra], page_sems.at[0, extra])
    for t in range(lines):
        q_copy(t).start()
    for buffer in range(2):
        pages[buffer, :extra] = jnp.zeros((extra,) + pages.shape[2:], pages.dtype)
    fresh_copy.start()
    fetch(0)
    if lines > 1:
        fetch(1)
    if stores:
        @pl.loop(0, slots)
        def _(slot):
            @pl.when(slot != store[0])
            def _():
                store_copy(slot).start()

        pltpu.make_async_copy(incoming.at[0], pool_out.at[store[0]], store_sems.at[store[0]]).start()

    def soften(h, s, values):
        old = tops[h]
        new = jnp.maximum(old, jnp.max(s, axis=1, keepdims=True))
        tops[h] = new
        factor = SCALE * LOG2E
        fade = jnp.exp2((old - new) * factor)
        wide = jnp.concatenate([new] * (s.shape[1] // PAGE), axis=1)
        expo = jnp.exp2((s - wide) * factor).astype(jnp.bfloat16)
        added = jnp.dot(expo, values, preferred_element_type=jnp.float32)
        acc[h] = acc[h] * jnp.concatenate([fade, fade], axis=1) + added

    def with_ones(values):
        return jnp.concatenate([values, jnp.ones_like(values)], axis=1)

    def score(t, h, keys):
        query = queries[t, :, h * HD:(h + 1) * HD]
        return lax.dot_general(query, keys, CONTRACT_LAST, preferred_element_type=jnp.float32)

    def keys_of(t, index):
        return pages[lax.rem(t, 2), pl.ds(index * BLOCK, BLOCK), 0].reshape(BLOCK * PAGE, HD)

    def values_of(t, index):
        return with_ones(pages[lax.rem(t, 2), pl.ds(index * BLOCK, BLOCK), 1].reshape(BLOCK * PAGE, HD))

    def blocks_of(t):
        return jnp.maximum(lax.div(counts[request_of(t)] + BLOCK - 1, BLOCK), 1)

    def reset():
        tops[...] = jnp.full(tops.shape, LOW, jnp.float32)
        acc[...] = jnp.zeros(acc.shape, jnp.float32)

    def finish(t):
        some = (counts[request_of(t)] > 0) | (t == 0)
        lane = lax.broadcasted_iota(jnp.int32, (PAGE, PAGE), 1)
        stat = jnp.zeros((PAGE, PAGE), jnp.float32)
        for h in range(GQ):
            total = acc[h, :, HD:]
            results[t, h * PAGE:(h + 1) * PAGE, :] = (acc[h, :, :HD] * (1.0 / total)).astype(jnp.bfloat16)
            level = jnp.where(some, tops[h] * SCALE + jnp.log(total), LOW)
            high = level.astype(jnp.bfloat16).astype(jnp.float32)
            middle = (level - high).astype(jnp.bfloat16).astype(jnp.float32)
            low = level - high - middle
            stat = jnp.where(lane == h, high, stat)
            stat = jnp.where(lane == GQ + h, middle, stat)
            stat = jnp.where(lane == 2 * GQ + h, low, stat)
        results[t, GQ * PAGE:, :] = stat.T[:STAT].astype(jnp.bfloat16)
        out_copy(t).start()

    for t in range(lines):
        q_copy(t).wait()
    fresh_copy.wait()
    reset()
    span_values = with_ones(pages[0, extra, 1])
    for h in range(GQ):
        s = score(0, h, pages[0, extra, 0])
        seen = lax.broadcasted_iota(jnp.int32, s.shape, 1) <= lax.broadcasted_iota(jnp.int32, s.shape, 0)
        soften(h, jnp.where(seen, s, LOW), span_values)
    arrive(0)
    first = keys_of(0, 0)
    for h in range(GQ):
        scores[h] = score(0, h, first)

    def step(_, carry):
        t, index = carry
        request = request_of(t)
        ends = index + 1 >= blocks_of(t)
        later_t = jnp.where(ends, t + 1, t)
        later_index = jnp.where(ends, 0, index + 1)
        ahead_t = jnp.minimum(later_t, lines - 1)

        @pl.when(ends & (t + 1 < lines))
        def _():
            arrive(t + 1)

        limit = (counts[request] - 1 - index * BLOCK) * PAGE + lasts[request]
        column = lax.broadcasted_iota(jnp.int32, (PAGE, BLOCK * PAGE), 1)
        values = values_of(t, index)
        keys = keys_of(ahead_t, later_index)
        for h in range(GQ):
            soften(h, jnp.where(column < limit, scores[h], LOW), values)
            scores[h] = score(ahead_t, h, keys)

        @pl.when(ends)
        def _():
            finish(t)
            reset()

            @pl.when(t + 2 < lines)
            def _():
                fetch(t + 2)

        return later_t, later_index

    steps = blocks_of(0)
    for t in range(1, lines):
        steps += blocks_of(t)
    lax.fori_loop(0, steps, step, (jnp.int32(0), jnp.int32(0)))
    for t in range(lines):
        out_copy(t).wait()
    if stores:
        @pl.loop(0, slots)
        def _(slot):
            store_copy(slot).wait()


def attend(head, q_head, tables, q_all, pools, fresh, incoming=None):
    picks, counts, lasts, mine, store = tables
    lines = q_all.shape[0]
    places = picks.shape[1]
    keys = places * PAGE * 5 // 8
    pool = pools[0]
    out_shape = [jax.ShapeDtypeStruct((lines, ROWS, HD), jnp.bfloat16)]
    scratch = [
        pltpu.VMEM((2, places + 1, 2, PAGE, HD), jnp.bfloat16),
        pltpu.VMEM((lines, PAGE, CHUNK), jnp.bfloat16),
        pltpu.VMEM((lines, ROWS, HD), jnp.bfloat16),
        pltpu.VMEM((GQ, PAGE, BLOCK * PAGE), jnp.float32),
        pltpu.VMEM((GQ, PAGE, PAGE), jnp.float32),
        pltpu.VMEM((GQ, PAGE, 2 * HD), jnp.float32),
        pltpu.SemaphoreType.DMA((lines,)),
        pltpu.SemaphoreType.DMA((2, places + 1)),
        pltpu.SemaphoreType.DMA((lines,)),
    ]
    operands = [q_all, *pools, fresh]
    if incoming is not None:
        operands.append(incoming)
        out_shape.append(jax.ShapeDtypeStruct(pool.shape, pool.dtype))
        scratch.append(pltpu.SemaphoreType.DMA((pool.shape[0],)))
    grid_spec = pltpu.PrefetchScalarGridSpec(
        num_scalar_prefetch=5,
        grid=(),
        in_specs=[pl.BlockSpec(memory_space=pl.ANY)] * len(operands),
        out_specs=[pl.BlockSpec(memory_space=pl.ANY)] * len(out_shape),
        scratch_shapes=scratch,
    )
    return pl.pallas_call(
        functools.partial(attend_kernel, lines, head, q_head),
        grid_spec=grid_spec,
        out_shape=out_shape,
        compiler_params=pltpu.CompilerParams(vmem_limit_bytes=24 * 2**20),
        cost_estimate=pl.CostEstimate(
            flops=lines * 4 * GQ * PAGE * keys * HD,
            bytes_accessed=lines * keys * 4 * HD + lines * 2 * (CHUNK * PAGE + ROWS * HD),
            transcendentals=lines * GQ * PAGE * keys,
        ),
    )(picks, counts, lasts, mine, store, *operands)


def merge_kernel(head, parts, *refs):
    lines = parts.shape[0]
    out, result, sem = refs[-3:]
    levels = []
    for i in range(lines):
        block = parts[i, GQ * PAGE:, :].astype(jnp.float32)
        levels.append(block[:GQ] + block[GQ:2 * GQ] + block[2 * GQ:3 * GQ])
    top = functools.reduce(jnp.maximum, levels)
    weights = [jnp.exp(level - top) for level in levels]
    total = functools.reduce(jnp.add, weights)
    weights = [weight / total for weight in weights]
    filler = PAGE - lines * GQ
    table = jnp.concatenate(weights + [jnp.zeros((filler, PAGE), jnp.float32)], axis=0).T
    for h in range(GQ):
        merged = jnp.zeros((PAGE, HD), jnp.float32)
        for i in range(lines):
            column = i * GQ + h
            merged += table[:, column:column + 1] * parts[i, h * PAGE:(h + 1) * PAGE, :].astype(jnp.float32)
        result[:, h * HD:(h + 1) * HD] = merged.astype(jnp.bfloat16)
    copy = pltpu.make_async_copy(result, out.at[:, pl.ds(head * CHUNK, CHUNK)], sem)
    copy.start()
    copy.wait()


def merge(head, parts, whole):
    before = [] if whole is None else [whole]
    return pl.pallas_call(
        functools.partial(merge_kernel, head),
        in_specs=[pl.BlockSpec(memory_space=pltpu.VMEM)] + [pl.BlockSpec(memory_space=pl.ANY)] * len(before),
        out_specs=pl.BlockSpec(memory_space=pl.ANY),
        out_shape=jax.ShapeDtypeStruct((PAGE, KVH * CHUNK), jnp.bfloat16),
        scratch_shapes=[pltpu.VMEM((PAGE, CHUNK), jnp.bfloat16), pltpu.SemaphoreType.DMA],
        input_output_aliases={1: 0} if before else {},
        cost_estimate=pl.CostEstimate(
            flops=2 * parts.size, bytes_accessed=2 * parts.size + 2 * PAGE * CHUNK, transcendentals=0
        ),
    )(parts, *before)


def page_tables(me, width, slots, page_owner, page_slot, prefix_len):
    lines = width // CLUSTER
    capacity = (MAXP + width - 2) // (width - 1)
    limit = min(MAXP, CLUSTER * capacity)
    groups = [[c * CLUSTER + i for c in range(lines)] for i in range(CLUSTER)]
    table = jnp.concatenate([page_owner[0], page_slot[0], prefix_len])[None]
    tables = lax.all_gather(table, "serve", axis_index_groups=groups, tiled=True)
    owners = tables[:, :MAXP]
    places = tables[:, MAXP:2 * MAXP]
    length = tables[:, 2 * MAXP]
    used = (length + PAGE - 1) // PAGE
    spot = jnp.arange(MAXP)
    here = (spot[None] < used[:, None]) & (owners // CLUSTER == me // CLUSTER)
    hits = here.astype(jnp.int32)
    before = jnp.sum(hits[:, None, :] * (spot[None, None, :] < spot[None, :, None]), axis=2)
    local = ((owners % CLUSTER) ^ (me % CLUSTER)) * slots + places
    chosen = here[:, :, None] & (before[:, :, None] == jnp.arange(limit)[None, None, :])
    picks = jnp.sum(jnp.where(chosen, local[:, :, None], 0), axis=1)
    counts = jnp.sum(hits, axis=1)
    tail = jnp.sum(jnp.where(here & (spot[None] == used[:, None] - 1), 1, 0), axis=1)
    lasts = jnp.where(tail > 0, length - (used - 1) * PAGE, PAGE)
    return picks, counts, lasts, (me // CLUSTER)[None]


def exchanged(array, groups):
    return lax.all_to_all(array, "serve", 0, 0, axis_index_groups=groups, tiled=True)


def per_device(queries, new_kv, pool, page_owner, page_slot, prefix_len, store_slot):
    width = lax.axis_size("serve")
    lines = width // CLUSTER
    groups = [[c * CLUSTER + i for c in range(lines)] for i in range(CLUSTER)]
    me = lax.axis_index("serve")
    slots = pool.shape[0]
    first = pool[:, :, :, :HD]
    rest, first = lax.optimization_barrier((pool, first))
    sides = [swapped(first, "serve", 2)]
    sides += [swapped(rest[:, :, :, g * HD:(g + 1) * HD], "serve", 2) for g in range(1, KVH)]
    twin = swapped(pool, "serve", 1)
    early = exchanged(jnp.broadcast_to(queries[None, :, :CHUNK], (lines, PAGE, CHUNK)), groups)
    rest_q, early = lax.optimization_barrier((queries, early))
    later = exchanged(jnp.broadcast_to(rest_q[None, :, CHUNK:], (lines, PAGE, 3 * CHUNK)), groups)
    tables = page_tables(me, width, slots, page_owner, page_slot, prefix_len) + (store_slot[0],)
    fresh = new_kv[0, 0]
    incoming = shifted(new_kv[0], "serve", 1)
    attended = None
    for g in range(KVH):
        both = swapped(sides[g], "serve", 1)
        pools = (pool, twin, sides[g], both)
        q_all = early if g == 0 else later
        if g == 1:
            parts, pool_out = attend(g, max(g - 1, 0), tables, q_all, pools, fresh, incoming)
        else:
            parts = attend(g, max(g - 1, 0), tables, q_all, pools, fresh)[0]
        attended = merge(g, exchanged(parts, groups), attended)
    return (attended, pool_out)


def solution(mesh):
    return jax.shard_map(
        per_device,
        mesh=mesh,
        in_specs=(
            P(("groups", "serve"), None),
            P(("groups", "serve"), None, None, None, None),
            P(("groups", "serve"), None, None, None),
            P(("groups", "serve"), None),
            P(("groups", "serve"), None),
            P(("groups", "serve")),
            P(("groups", "serve"), None),
        ),
        out_specs=(P(("groups", "serve"), None), P(("groups", "serve"), None, None, None)),
        check_vma=False,
    )
```

```python
import functools

import jax
import jax.numpy as jnp
from jax import lax
from jax.experimental import pallas as pl
from jax.experimental.pallas import tpu as pltpu
from jax.sharding import PartitionSpec as P

PAGE = 128
KVH = 4
GQ = 5
HD = 128
MAXP = 48
SCALE = HD ** (-0.5)
LOG2E = 1.4426950408889634
LOW = -1e30
CLUSTER = 4
BLOCK = 4
STAT = 16
HEADS = ((0, 1, 2), (3, 4))
ROWS = GQ * PAGE + STAT
CHUNK = GQ * HD
CONTRACT_LAST = (((1,), (1,)), ((), ()))


def swapped(array, axis, bit):
    size = lax.axis_size(axis)
    return lax.ppermute(array, axis, [(i, i ^ bit) for i in range(size)])


def shifted(array, axis, by):
    size = lax.axis_size(axis)
    return lax.ppermute(array, axis, [(i, (i + by) % size) for i in range(size)])


def attend_kernel(lines, head, q_head, picks, counts, lasts, mine, store, *refs):
    q_all, own, twin, side, both, fresh = refs[:6]
    stores = len(refs) == 19
    if stores:
        incoming, out, pool_out = refs[6:9]
        store_sems = refs[-1]
        scratch = refs[9:-1]
    else:
        out = refs[6]
        scratch = refs[7:]
    pages, queries, results, scores, tops, acc, q_sems, page_sems, out_sems = scratch
    slots = own.shape[0]
    columns = pl.ds(head * HD, HD)
    extra = pages.shape[1] - 1

    def request_of(t):
        return lax.rem(mine[0] - t + lines, lines)

    def q_copy(t, h):
        origin = q_all.at[request_of(t), :, pl.ds((q_head * GQ + h) * HD, HD)]
        return pltpu.make_async_copy(origin, queries.at[t, h], q_sems.at[t, h])

    def out_copy(t):
        return pltpu.make_async_copy(results.at[t], out.at[request_of(t)], out_sems.at[t])

    def page_copy(source, slot, buffer, place):
        if source.shape[-1] == HD:
            origin = source.at[slot]
        else:
            origin = source.at[slot, :, :, columns]
        return pltpu.make_async_copy(origin, pages.at[buffer, place], page_sems.at[buffer, place])

    def fetch(t):
        request = request_of(t)
        buffer = lax.rem(t, 2)

        @pl.loop(0, counts[request])
        def _(place):
            code = picks[request, place]
            rank = lax.div(code, slots)
            slot = lax.rem(code, slots)
            for index, source in enumerate((own, twin, side, both)):
                @pl.when(rank == index)
                def _():
                    page_copy(source, slot, buffer, place).start()

    def arrive(t):
        buffer = lax.rem(t, 2)

        @pl.loop(0, counts[request_of(t)])
        def _(place):
            page_copy(own, 0, buffer, place).wait()

    def store_copy(slot):
        return pltpu.make_async_copy(own.at[slot], pool_out.at[slot], store_sems.at[slot])

    fresh_copy = pltpu.make_async_copy(fresh.at[:, :, columns], pages.at[0, extra], page_sems.at[0, extra])
    for t in range(lines):
        for h in range(GQ):
            q_copy(t, h).start()
    for buffer in range(2):
        pages[buffer, :extra] = jnp.zeros((extra,) + pages.shape[2:], pages.dtype)
    fresh_copy.start()
    fetch(0)
    if lines > 1:
        fetch(1)
    if stores:
        @pl.loop(0, slots)
        def _(slot):
            @pl.when(slot != store[0])
            def _():
                store_copy(slot).start()

        pltpu.make_async_copy(incoming.at[0], pool_out.at[store[0]], store_sems.at[store[0]]).start()

    def soften(heads, scored, values):
        factor = SCALE * LOG2E
        expos = []
        fades = []
        for h in heads:
            s = scored(h)
            old = tops[h]
            new = jnp.maximum(old, jnp.max(s, axis=1, keepdims=True))
            tops[h] = new
            fades.append(jnp.exp2((old - new) * factor))
            wide = jnp.concatenate([new] * (s.shape[1] // PAGE), axis=1)
            expos.append(jnp.exp2((s - wide) * factor).astype(jnp.bfloat16))
        added = jnp.dot(jnp.concatenate(expos, axis=0), values, preferred_element_type=jnp.float32)
        for i, h in enumerate(heads):
            fade = fades[i]
            acc[h] = acc[h] * jnp.concatenate([fade, fade], axis=1) + added[i * PAGE:(i + 1) * PAGE]

    def with_ones(values):
        return jnp.concatenate([values, jnp.ones_like(values)], axis=1)

    def score(t, heads, keys):
        query = queries[t, heads[0]:heads[-1] + 1].reshape(len(heads) * PAGE, HD)
        s = lax.dot_general(query, keys, CONTRACT_LAST, preferred_element_type=jnp.float32)
        return s.reshape(len(heads), PAGE, keys.shape[0])

    def keys_of(t, index):
        return pages[lax.rem(t, 2), pl.ds(index * BLOCK, BLOCK), 0].reshape(BLOCK * PAGE, HD)

    def values_of(t, index):
        return with_ones(pages[lax.rem(t, 2), pl.ds(index * BLOCK, BLOCK), 1].reshape(BLOCK * PAGE, HD))

    def blocks_of(t):
        return jnp.maximum(lax.div(counts[request_of(t)] + BLOCK - 1, BLOCK), 1)

    def reset():
        tops[...] = jnp.full(tops.shape, LOW, jnp.float32)
        acc[...] = jnp.zeros(acc.shape, jnp.float32)

    def finish(t):
        some = (counts[request_of(t)] > 0) | (t == 0)
        lane = lax.broadcasted_iota(jnp.int32, (PAGE, PAGE), 1)
        stat = jnp.zeros((PAGE, PAGE), jnp.float32)
        for h in range(GQ):
            total = acc[h, :, HD:]
            results[t, h * PAGE:(h + 1) * PAGE, :] = (acc[h, :, :HD] * (1.0 / total)).astype(jnp.bfloat16)
            level = jnp.where(some, tops[h] * SCALE + jnp.log(total), LOW)
            high = level.astype(jnp.bfloat16).astype(jnp.float32)
            middle = (level - high).astype(jnp.bfloat16).astype(jnp.float32)
            low = level - high - middle
            stat = jnp.where(lane == h, high, stat)
            stat = jnp.where(lane == GQ + h, middle, stat)
            stat = jnp.where(lane == 2 * GQ + h, low, stat)
        results[t, GQ * PAGE:, :] = stat.T[:STAT].astype(jnp.bfloat16)
        out_copy(t).start()

    for t in range(lines):
        for h in range(GQ):
            q_copy(t, h).wait()
    fresh_copy.wait()
    reset()
    span_values = with_ones(pages[0, extra, 1])
    seen = lax.broadcasted_iota(jnp.int32, (PAGE, PAGE), 1) <= lax.broadcasted_iota(jnp.int32, (PAGE, PAGE), 0)
    for heads in HEADS:
        s = score(0, heads, pages[0, extra, 0])
        soften(heads, lambda h: jnp.where(seen, s[h - heads[0]], LOW), span_values)
    arrive(0)
    first = keys_of(0, 0)
    for heads in HEADS:
        scores[heads[0]:heads[-1] + 1] = score(0, heads, first)

    def step(_, carry):
        t, index = carry
        request = request_of(t)
        ends = index + 1 >= blocks_of(t)
        later_t = jnp.where(ends, t + 1, t)
        later_index = jnp.where(ends, 0, index + 1)
        ahead_t = jnp.minimum(later_t, lines - 1)

        @pl.when(ends & (t + 1 < lines))
        def _():
            arrive(t + 1)

        limit = (counts[request] - 1 - index * BLOCK) * PAGE + lasts[request]
        column = lax.broadcasted_iota(jnp.int32, (PAGE, BLOCK * PAGE), 1)
        values = values_of(t, index)
        keys = keys_of(ahead_t, later_index)
        for heads in HEADS:
            soften(heads, lambda h: jnp.where(column < limit, scores[h], LOW), values)
            scores[heads[0]:heads[-1] + 1] = score(ahead_t, heads, keys)

        @pl.when(ends)
        def _():
            finish(t)
            reset()

            @pl.when(t + 2 < lines)
            def _():
                fetch(t + 2)

        return later_t, later_index

    steps = blocks_of(0)
    for t in range(1, lines):
        steps += blocks_of(t)
    lax.fori_loop(0, steps, step, (jnp.int32(0), jnp.int32(0)))
    for t in range(lines):
        out_copy(t).wait()
    if stores:
        @pl.loop(0, slots)
        def _(slot):
            store_copy(slot).wait()


def attend(head, q_head, tables, q_all, pools, fresh, incoming=None):
    picks, counts, lasts, mine, store = tables
    lines = q_all.shape[0]
    places = picks.shape[1]
    keys = places * PAGE * 5 // 8
    pool = pools[0]
    out_shape = [jax.ShapeDtypeStruct((lines, ROWS, HD), jnp.bfloat16)]
    scratch = [
        pltpu.VMEM((2, places + 1, 2, PAGE, HD), jnp.bfloat16),
        pltpu.VMEM((lines, GQ, PAGE, HD), jnp.bfloat16),
        pltpu.VMEM((lines, ROWS, HD), jnp.bfloat16),
        pltpu.VMEM((GQ, PAGE, BLOCK * PAGE), jnp.float32),
        pltpu.VMEM((GQ, PAGE, PAGE), jnp.float32),
        pltpu.VMEM((GQ, PAGE, 2 * HD), jnp.float32),
        pltpu.SemaphoreType.DMA((lines, GQ)),
        pltpu.SemaphoreType.DMA((2, places + 1)),
        pltpu.SemaphoreType.DMA((lines,)),
    ]
    operands = [q_all, *pools, fresh]
    if incoming is not None:
        operands.append(incoming)
        out_shape.append(jax.ShapeDtypeStruct(pool.shape, pool.dtype))
        scratch.append(pltpu.SemaphoreType.DMA((pool.shape[0],)))
    grid_spec = pltpu.PrefetchScalarGridSpec(
        num_scalar_prefetch=5,
        grid=(),
        in_specs=[pl.BlockSpec(memory_space=pltpu.HBM)] * 3 + [pl.BlockSpec(memory_space=pl.ANY)] * (len(operands) - 3),
        out_specs=[pl.BlockSpec(memory_space=pl.ANY), pl.BlockSpec(memory_space=pltpu.HBM)][:len(out_shape)],
        scratch_shapes=scratch,
    )
    return pl.pallas_call(
        functools.partial(attend_kernel, lines, head, q_head),
        grid_spec=grid_spec,
        out_shape=out_shape,
        compiler_params=pltpu.CompilerParams(vmem_limit_bytes=24 * 2**20),
        cost_estimate=pl.CostEstimate(
            flops=lines * 4 * GQ * PAGE * keys * HD,
            bytes_accessed=lines * keys * 4 * HD + lines * 2 * (CHUNK * PAGE + ROWS * HD),
            transcendentals=lines * GQ * PAGE * keys,
        ),
    )(picks, counts, lasts, mine, store, *operands)


def merge_kernel(head, parts, *refs):
    lines = parts.shape[0]
    out, result, sem = refs[-3:]
    levels = []
    for i in range(lines):
        block = parts[i, GQ * PAGE:, :].astype(jnp.float32)
        levels.append(block[:GQ] + block[GQ:2 * GQ] + block[2 * GQ:3 * GQ])
    top = functools.reduce(jnp.maximum, levels)
    weights = [jnp.exp(level - top) for level in levels]
    total = functools.reduce(jnp.add, weights)
    weights = [weight / total for weight in weights]
    filler = PAGE - lines * GQ
    table = jnp.concatenate(weights + [jnp.zeros((filler, PAGE), jnp.float32)], axis=0).T
    for h in range(GQ):
        merged = jnp.zeros((PAGE, HD), jnp.float32)
        for i in range(lines):
            column = i * GQ + h
            merged += table[:, column:column + 1] * parts[i, h * PAGE:(h + 1) * PAGE, :].astype(jnp.float32)
        result[:, h * HD:(h + 1) * HD] = merged.astype(jnp.bfloat16)
    copy = pltpu.make_async_copy(result, out.at[:, pl.ds(head * CHUNK, CHUNK)], sem)
    copy.start()
    copy.wait()


def merge(head, parts, whole):
    before = [] if whole is None else [whole]
    return pl.pallas_call(
        functools.partial(merge_kernel, head),
        in_specs=[pl.BlockSpec(memory_space=pltpu.VMEM)] + [pl.BlockSpec(memory_space=pl.ANY)] * len(before),
        out_specs=pl.BlockSpec(memory_space=pl.ANY),
        out_shape=jax.ShapeDtypeStruct((PAGE, KVH * CHUNK), jnp.bfloat16),
        scratch_shapes=[pltpu.VMEM((PAGE, CHUNK), jnp.bfloat16), pltpu.SemaphoreType.DMA],
        input_output_aliases={1: 0} if before else {},
        cost_estimate=pl.CostEstimate(
            flops=2 * parts.size, bytes_accessed=2 * parts.size + 2 * PAGE * CHUNK, transcendentals=0
        ),
    )(parts, *before)


def page_tables(me, width, slots, page_owner, page_slot, prefix_len):
    lines = width // CLUSTER
    capacity = (MAXP + width - 2) // (width - 1)
    limit = min(MAXP, CLUSTER * capacity)
    groups = [[c * CLUSTER + i for c in range(lines)] for i in range(CLUSTER)]
    table = jnp.concatenate([page_owner[0], page_slot[0], prefix_len])[None]
    tables = lax.all_gather(table, "serve", axis_index_groups=groups, tiled=True)
    owners = tables[:, :MAXP]
    places = tables[:, MAXP:2 * MAXP]
    length = tables[:, 2 * MAXP]
    used = (length + PAGE - 1) // PAGE
    spot = jnp.arange(MAXP)
    here = (spot[None] < used[:, None]) & (owners // CLUSTER == me // CLUSTER)
    hits = here.astype(jnp.int32)
    before = jnp.sum(hits[:, None, :] * (spot[None, None, :] < spot[None, :, None]), axis=2)
    local = ((owners % CLUSTER) ^ (me % CLUSTER)) * slots + places
    chosen = here[:, :, None] & (before[:, :, None] == jnp.arange(limit)[None, None, :])
    picks = jnp.sum(jnp.where(chosen, local[:, :, None], 0), axis=1)
    counts = jnp.sum(hits, axis=1)
    tail = jnp.sum(jnp.where(here & (spot[None] == used[:, None] - 1), 1, 0), axis=1)
    lasts = jnp.where(tail > 0, length - (used - 1) * PAGE, PAGE)
    return picks, counts, lasts, (me // CLUSTER)[None]


def exchanged(array, groups):
    return lax.all_to_all(array, "serve", 0, 0, axis_index_groups=groups, tiled=True)


def after(array, *others):
    return lax.optimization_barrier((array, *others))[0]


def per_device(queries, new_kv, pool, page_owner, page_slot, prefix_len, store_slot):
    width = lax.axis_size("serve")
    lines = width // CLUSTER
    groups = [[c * CLUSTER + i for c in range(lines)] for i in range(CLUSTER)]
    me = lax.axis_index("serve")
    slots = pool.shape[0]
    first = pool[:, :, :, :HD]
    rest = after(pool, first)
    sides = [swapped(first, "serve", 2)]
    sides += [swapped(rest[:, :, :, g * HD:(g + 1) * HD], "serve", 2) for g in range(1, KVH)]
    tables = page_tables(me, width, slots, page_owner, page_slot, prefix_len) + (store_slot[0],)
    twin = swapped(rest, "serve", 1)
    q_all = jnp.broadcast_to(after(queries, tables[0])[None], (lines, PAGE, KVH * CHUNK))
    q_all = exchanged(q_all, groups)
    fresh = new_kv[0, 0]
    incoming = shifted(after(new_kv[0], tables[0]), "serve", 1)
    attended = None
    parts = None
    for g in range(KVH):
        side = sides[g] if g == 0 else after(sides[g], parts)
        both = swapped(side, "serve", 1)
        pools = (pool, twin, side, both)
        if g == KVH - 2:
            parts, pool_out = attend(g, g, tables, q_all, pools, fresh, incoming)
        else:
            parts = attend(g, g, tables, q_all, pools, fresh)[0]
        attended = merge(g, exchanged(parts, groups), attended)
    return (attended, pool_out)


def solution(mesh):
    return jax.shard_map(
        per_device,
        mesh=mesh,
        in_specs=(
            P(("groups", "serve"), None),
            P(("groups", "serve"), None, None, None, None),
            P(("groups", "serve"), None, None, None),
            P(("groups", "serve"), None),
            P(("groups", "serve"), None),
            P(("groups", "serve")),
            P(("groups", "serve"), None),
        ),
        out_specs=(P(("groups", "serve"), None), P(("groups", "serve"), None, None, None)),
        check_vma=False,
    )
```

```python
import functools

import jax
import jax.numpy as jnp
from jax import lax
from jax.experimental import pallas as pl
from jax.experimental.pallas import tpu as pltpu
from jax.sharding import PartitionSpec as P

PAGE = 128
KVH = 4
GQ = 5
HD = 128
MAXP = 48
SCALE = HD ** (-0.5)
LOG2E = 1.4426950408889634
LOW = -1e30
CLUSTER = 4
BLOCK = 4
STAT = 16
HEADS = ((0, 1, 2), (3, 4))
ROWS = GQ * PAGE + STAT
CHUNK = GQ * HD
CONTRACT_LAST = (((1,), (1,)), ((), ()))


def swapped(array, axis, bit):
    size = lax.axis_size(axis)
    return lax.ppermute(array, axis, [(i, i ^ bit) for i in range(size)])


def shifted(array, axis, by):
    size = lax.axis_size(axis)
    return lax.ppermute(array, axis, [(i, (i + by) % size) for i in range(size)])


def attend_kernel(lines, head, q_head, picks, counts, lasts, mine, store, *refs):
    q_all, own, twin, side, both, fresh = refs[:6]
    stores = len(refs) == 19
    if stores:
        incoming, out, pool_out = refs[6:9]
        store_sems = refs[-1]
        scratch = refs[9:-1]
    else:
        out = refs[6]
        scratch = refs[7:]
    pages, queries, results, scores, tops, acc, q_sems, page_sems, out_sems = scratch
    slots = own.shape[0]
    columns = pl.ds(head * HD, HD)
    extra = pages.shape[1] - 1

    def request_of(t):
        return lax.rem(mine[0] - t + lines, lines)

    def q_copy(t, h):
        origin = q_all.at[request_of(t), :, pl.ds((q_head * GQ + h) * HD, HD)]
        return pltpu.make_async_copy(origin, queries.at[t, h], q_sems.at[t, h])

    def out_copy(t):
        return pltpu.make_async_copy(results.at[t], out.at[request_of(t)], out_sems.at[t])

    def page_copy(source, slot, buffer, place):
        if source.shape[-1] == HD:
            origin = source.at[slot]
        else:
            origin = source.at[slot, :, :, columns]
        return pltpu.make_async_copy(origin, pages.at[buffer, place], page_sems.at[buffer, place])

    def fetch(t):
        request = request_of(t)
        buffer = lax.rem(t, 2)

        @pl.loop(0, counts[request])
        def _(place):
            code = picks[request, place]
            rank = lax.div(code, slots)
            slot = lax.rem(code, slots)
            for index, source in enumerate((own, twin, side, both)):
                @pl.when(rank == index)
                def _():
                    page_copy(source, slot, buffer, place).start()

    def arrive(t):
        buffer = lax.rem(t, 2)

        @pl.loop(0, counts[request_of(t)])
        def _(place):
            page_copy(own, 0, buffer, place).wait()

    def store_copy(slot):
        return pltpu.make_async_copy(own.at[slot], pool_out.at[slot], store_sems.at[slot])

    fresh_copy = pltpu.make_async_copy(fresh.at[:, :, columns], pages.at[0, extra], page_sems.at[0, extra])
    for t in range(lines):
        for h in range(GQ):
            q_copy(t, h).start()
    for buffer in range(2):
        pages[buffer, :extra] = jnp.zeros((extra,) + pages.shape[2:], pages.dtype)
    fresh_copy.start()
    fetch(0)
    if lines > 1:
        fetch(1)
    if stores:
        @pl.loop(0, slots)
        def _(slot):
            @pl.when(slot != store[0])
            def _():
                store_copy(slot).start()

        pltpu.make_async_copy(incoming.at[0], pool_out.at[store[0]], store_sems.at[store[0]]).start()

    def soften(heads, scored, values):
        factor = SCALE * LOG2E
        expos = []
        fades = []
        for h in heads:
            s = scored(h)
            old = tops[h]
            new = jnp.maximum(old, jnp.max(s, axis=1, keepdims=True))
            tops[h] = new
            fades.append(jnp.exp2((old - new) * factor))
            wide = jnp.concatenate([new] * (s.shape[1] // PAGE), axis=1)
            expos.append(jnp.exp2((s - wide) * factor).astype(jnp.bfloat16))
        added = jnp.dot(jnp.concatenate(expos, axis=0), values, preferred_element_type=jnp.float32)
        for i, h in enumerate(heads):
            fade = fades[i]
            acc[h] = acc[h] * jnp.concatenate([fade, fade], axis=1) + added[i * PAGE:(i + 1) * PAGE]

    def with_ones(values):
        return jnp.concatenate([values, jnp.ones_like(values)], axis=1)

    def score(t, heads, keys):
        query = queries[t, heads[0]:heads[-1] + 1].reshape(len(heads) * PAGE, HD)
        s = lax.dot_general(query, keys, CONTRACT_LAST, preferred_element_type=jnp.float32)
        return s.reshape(len(heads), PAGE, keys.shape[0])

    def keys_of(t, index):
        return pages[lax.rem(t, 2), pl.ds(index * BLOCK, BLOCK), 0].reshape(BLOCK * PAGE, HD)

    def values_of(t, index):
        return with_ones(pages[lax.rem(t, 2), pl.ds(index * BLOCK, BLOCK), 1].reshape(BLOCK * PAGE, HD))

    def blocks_of(t):
        return jnp.maximum(lax.div(counts[request_of(t)] + BLOCK - 1, BLOCK), 1)

    def reset():
        tops[...] = jnp.full(tops.shape, LOW, jnp.float32)
        acc[...] = jnp.zeros(acc.shape, jnp.float32)

    def finish(t):
        some = (counts[request_of(t)] > 0) | (t == 0)
        lane = lax.broadcasted_iota(jnp.int32, (PAGE, PAGE), 1)
        stat = jnp.zeros((PAGE, PAGE), jnp.float32)
        for h in range(GQ):
            total = acc[h, :, HD:]
            results[t, h * PAGE:(h + 1) * PAGE, :] = (acc[h, :, :HD] * (1.0 / total)).astype(jnp.bfloat16)
            level = jnp.where(some, tops[h] * SCALE + jnp.log(total), LOW)
            high = level.astype(jnp.bfloat16).astype(jnp.float32)
            middle = (level - high).astype(jnp.bfloat16).astype(jnp.float32)
            low = level - high - middle
            stat = jnp.where(lane == h, high, stat)
            stat = jnp.where(lane == GQ + h, middle, stat)
            stat = jnp.where(lane == 2 * GQ + h, low, stat)
        results[t, GQ * PAGE:, :] = stat.T[:STAT].astype(jnp.bfloat16)
        out_copy(t).start()

    for t in range(lines):
        for h in range(GQ):
            q_copy(t, h).wait()
    fresh_copy.wait()
    reset()
    span_values = with_ones(pages[0, extra, 1])
    seen = lax.broadcasted_iota(jnp.int32, (PAGE, PAGE), 1) <= lax.broadcasted_iota(jnp.int32, (PAGE, PAGE), 0)
    for heads in HEADS:
        s = score(0, heads, pages[0, extra, 0])
        soften(heads, lambda h: jnp.where(seen, s[h - heads[0]], LOW), span_values)
    arrive(0)
    first = keys_of(0, 0)
    for heads in HEADS:
        scores[heads[0]:heads[-1] + 1] = score(0, heads, first)

    def step(_, carry):
        t, index = carry
        request = request_of(t)
        ends = index + 1 >= blocks_of(t)
        later_t = jnp.where(ends, t + 1, t)
        later_index = jnp.where(ends, 0, index + 1)
        ahead_t = jnp.minimum(later_t, lines - 1)

        @pl.when(ends & (t + 1 < lines))
        def _():
            arrive(t + 1)

        limit = (counts[request] - 1 - index * BLOCK) * PAGE + lasts[request]
        column = lax.broadcasted_iota(jnp.int32, (PAGE, BLOCK * PAGE), 1)
        values = values_of(t, index)
        keys = keys_of(ahead_t, later_index)
        for heads in HEADS:
            soften(heads, lambda h: jnp.where(column < limit, scores[h], LOW), values)
            scores[heads[0]:heads[-1] + 1] = score(ahead_t, heads, keys)

        @pl.when(ends)
        def _():
            finish(t)
            reset()

            @pl.when(t + 2 < lines)
            def _():
                fetch(t + 2)

        return later_t, later_index

    steps = blocks_of(0)
    for t in range(1, lines):
        steps += blocks_of(t)
    lax.fori_loop(0, steps, step, (jnp.int32(0), jnp.int32(0)))
    for t in range(lines):
        out_copy(t).wait()
    if stores:
        @pl.loop(0, slots)
        def _(slot):
            store_copy(slot).wait()


def attend(head, q_head, tables, q_all, pools, fresh, incoming=None):
    picks, counts, lasts, mine, store = tables
    lines = q_all.shape[0]
    places = picks.shape[1]
    pool = pools[0]
    out_shape = [jax.ShapeDtypeStruct((lines, ROWS, HD), jnp.bfloat16)]
    scratch = [
        pltpu.VMEM((2, places + 1, 2, PAGE, HD), jnp.bfloat16),
        pltpu.VMEM((lines, GQ, PAGE, HD), jnp.bfloat16),
        pltpu.VMEM((lines, ROWS, HD), jnp.bfloat16),
        pltpu.VMEM((GQ, PAGE, BLOCK * PAGE), jnp.float32),
        pltpu.VMEM((GQ, PAGE, PAGE), jnp.float32),
        pltpu.VMEM((GQ, PAGE, 2 * HD), jnp.float32),
        pltpu.SemaphoreType.DMA((lines, GQ)),
        pltpu.SemaphoreType.DMA((2, places + 1)),
        pltpu.SemaphoreType.DMA((lines,)),
    ]
    operands = [q_all, *pools, fresh]
    if incoming is not None:
        operands.append(incoming)
        out_shape.append(jax.ShapeDtypeStruct(pool.shape, pool.dtype))
        scratch.append(pltpu.SemaphoreType.DMA((pool.shape[0],)))
    grid_spec = pltpu.PrefetchScalarGridSpec(
        num_scalar_prefetch=5,
        grid=(),
        in_specs=[pl.BlockSpec(memory_space=pltpu.HBM)] * 3 + [pl.BlockSpec(memory_space=pl.ANY)] * (len(operands) - 3),
        out_specs=[pl.BlockSpec(memory_space=pl.ANY), pl.BlockSpec(memory_space=pltpu.HBM)][:len(out_shape)],
        scratch_shapes=scratch,
    )
    return pl.pallas_call(
        functools.partial(attend_kernel, lines, head, q_head),
        grid_spec=grid_spec,
        out_shape=out_shape,
        compiler_params=pltpu.CompilerParams(vmem_limit_bytes=24 * 2**20),
        cost_estimate=pl.CostEstimate(flops=1, bytes_accessed=1, transcendentals=0),
    )(picks, counts, lasts, mine, store, *operands)


def merge_kernel(head, parts, *refs):
    lines = parts.shape[0]
    out, result, sem = refs[-3:]
    levels = []
    for i in range(lines):
        block = parts[i, GQ * PAGE:, :].astype(jnp.float32)
        levels.append(block[:GQ] + block[GQ:2 * GQ] + block[2 * GQ:3 * GQ])
    top = functools.reduce(jnp.maximum, levels)
    weights = [jnp.exp(level - top) for level in levels]
    total = functools.reduce(jnp.add, weights)
    weights = [weight / total for weight in weights]
    filler = PAGE - lines * GQ
    table = jnp.concatenate(weights + [jnp.zeros((filler, PAGE), jnp.float32)], axis=0).T
    for h in range(GQ):
        merged = jnp.zeros((PAGE, HD), jnp.float32)
        for i in range(lines):
            column = i * GQ + h
            merged += table[:, column:column + 1] * parts[i, h * PAGE:(h + 1) * PAGE, :].astype(jnp.float32)
        result[:, h * HD:(h + 1) * HD] = merged.astype(jnp.bfloat16)
    copy = pltpu.make_async_copy(result, out.at[:, pl.ds(head * CHUNK, CHUNK)], sem)
    copy.start()
    copy.wait()


def merge(head, parts, whole):
    before = [] if whole is None else [whole]
    return pl.pallas_call(
        functools.partial(merge_kernel, head),
        in_specs=[pl.BlockSpec(memory_space=pltpu.VMEM)] + [pl.BlockSpec(memory_space=pl.ANY)] * len(before),
        out_specs=pl.BlockSpec(memory_space=pl.ANY),
        out_shape=jax.ShapeDtypeStruct((PAGE, KVH * CHUNK), jnp.bfloat16),
        scratch_shapes=[pltpu.VMEM((PAGE, CHUNK), jnp.bfloat16), pltpu.SemaphoreType.DMA],
        input_output_aliases={1: 0} if before else {},
        cost_estimate=pl.CostEstimate(flops=1, bytes_accessed=1, transcendentals=0),
    )(parts, *before)


def page_tables(me, width, slots, page_owner, page_slot, prefix_len):
    lines = width // CLUSTER
    capacity = (MAXP + width - 2) // (width - 1)
    limit = min(MAXP, CLUSTER * capacity)
    groups = [[c * CLUSTER + i for c in range(lines)] for i in range(CLUSTER)]
    table = jnp.concatenate([page_owner[0], page_slot[0], prefix_len])[None]
    tables = lax.all_gather(table, "serve", axis_index_groups=groups, tiled=True)
    owners = tables[:, :MAXP]
    places = tables[:, MAXP:2 * MAXP]
    length = tables[:, 2 * MAXP]
    used = (length + PAGE - 1) // PAGE
    spot = jnp.arange(MAXP)
    here = (spot[None] < used[:, None]) & (owners // CLUSTER == me // CLUSTER)
    hits = here.astype(jnp.int32)
    before = jnp.sum(hits[:, None, :] * (spot[None, None, :] < spot[None, :, None]), axis=2)
    local = ((owners % CLUSTER) ^ (me % CLUSTER)) * slots + places
    chosen = here[:, :, None] & (before[:, :, None] == jnp.arange(limit)[None, None, :])
    picks = jnp.sum(jnp.where(chosen, local[:, :, None], 0), axis=1)
    counts = jnp.sum(hits, axis=1)
    tail = jnp.sum(jnp.where(here & (spot[None] == used[:, None] - 1), 1, 0), axis=1)
    lasts = jnp.where(tail > 0, length - (used - 1) * PAGE, PAGE)
    return picks, counts, lasts, (me // CLUSTER)[None]


def exchanged(array, groups):
    return lax.all_to_all(array, "serve", 0, 0, axis_index_groups=groups, tiled=True)


def after(array, *others):
    return lax.optimization_barrier((array, *others))[0]


def per_device(queries, new_kv, pool, page_owner, page_slot, prefix_len, store_slot):
    width = lax.axis_size("serve")
    lines = width // CLUSTER
    groups = [[c * CLUSTER + i for c in range(lines)] for i in range(CLUSTER)]
    me = lax.axis_index("serve")
    slots = pool.shape[0]
    first = pool[:, :, :, :HD]
    rest = after(pool, first)
    sides = [swapped(first, "serve", 2)]
    sides += [swapped(rest[:, :, :, g * HD:(g + 1) * HD], "serve", 2) for g in range(1, KVH)]
    tables = page_tables(me, width, slots, page_owner, page_slot, prefix_len) + (store_slot[0],)
    twin = swapped(rest, "serve", 1)
    q_parts = []
    last = tables[0]
    for begin, end in ((0, 1), (1, KVH)):
        part = after(queries, last)[None, :, begin * CHUNK:end * CHUNK]
        part = jnp.broadcast_to(part, (lines, PAGE, (end - begin) * CHUNK))
        last = part
        part = exchanged(part, groups)
        q_parts += [(part, i) for i in range(end - begin)]
    fresh = new_kv[0, 0]
    incoming = shifted(after(new_kv[0], tables[0]), "serve", 1)
    attended = None
    parts = None
    for g in range(KVH):
        side = sides[g] if g == 0 else after(sides[g], parts)
        q_all, q_head = q_parts[g]
        both = swapped(side, "serve", 1)
        pools = (pool, twin, side, both)
        if g == KVH - 2:
            parts, pool_out = attend(g, q_head, tables, q_all, pools, fresh, incoming)
        else:
            parts = attend(g, q_head, tables, q_all, pools, fresh)[0]
        attended = merge(g, exchanged(parts, groups), attended)
    return (attended, pool_out)


def solution(mesh):
    return jax.shard_map(
        per_device,
        mesh=mesh,
        in_specs=(
            P(("groups", "serve"), None),
            P(("groups", "serve"), None, None, None, None),
            P(("groups", "serve"), None, None, None),
            P(("groups", "serve"), None),
            P(("groups", "serve"), None),
            P(("groups", "serve")),
            P(("groups", "serve"), None),
        ),
        out_specs=(P(("groups", "serve"), None), P(("groups", "serve"), None, None, None)),
        check_vma=False,
    )
```

```python
import functools

import jax
import jax.numpy as jnp
from jax import lax
from jax.experimental import pallas as pl
from jax.experimental.pallas import tpu as pltpu
from jax.sharding import PartitionSpec as P

PAGE = 128
KVH = 4
GQ = 5
HD = 128
MAXP = 48
SCALE = HD ** (-0.5)
LOG2E = 1.4426950408889634
LOW = -1e30
CLUSTER = 4
BLOCK = 4
STAT = 32
HEADS = ((0, 1, 2), (3, 4))
ROWS = GQ * PAGE + STAT
CHUNK = GQ * HD
CONTRACT_LAST = (((1,), (1,)), ((), ()))


def swapped(array, axis, bit):
    size = lax.axis_size(axis)
    return lax.ppermute(array, axis, [(i, i ^ bit) for i in range(size)])


def shifted(array, axis, by):
    size = lax.axis_size(axis)
    return lax.ppermute(array, axis, [(i, (i + by) % size) for i in range(size)])


def attend_kernel(lines, head, q_head, picks, counts, lasts, mine, store, *refs):
    q_all, own, twin, side, both, fresh = refs[:6]
    stores = len(refs) == 20
    if stores:
        pool, incoming, out, pool_out = refs[6:10]
        store_sems = refs[-1]
        scratch = refs[10:-1]
    else:
        out = refs[6]
        scratch = refs[7:]
    pages, queries, results, scores, tops, acc, q_sems, page_sems, out_sems = scratch
    slots = own.shape[0]
    columns = pl.ds(head * HD, HD)
    extra = pages.shape[1] - 1

    def request_of(t):
        return lax.rem(mine[0] - t + lines, lines)

    def q_copy(t, h):
        origin = q_all.at[request_of(t), pl.ds(0, PAGE), pl.ds((q_head * GQ + h) * HD, HD)]
        return pltpu.make_async_copy(origin, queries.at[t, h], q_sems.at[t, h])

    def out_copy(t):
        return pltpu.make_async_copy(results.at[t], out.at[request_of(t)], out_sems.at[t])

    def page_copy(source, slot, buffer, place):
        if source.shape[-1] == HD:
            origin = source.at[slot]
        else:
            origin = source.at[slot, :, :, columns]
        return pltpu.make_async_copy(origin, pages.at[buffer, place], page_sems.at[buffer, place])

    def fetch(t):
        request = request_of(t)
        buffer = lax.rem(t, 2)

        @pl.loop(0, counts[request])
        def _(place):
            code = picks[request, place]
            rank = lax.div(code, slots)
            slot = lax.rem(code, slots)
            for index, source in enumerate((own, twin, side, both)):
                @pl.when(rank == index)
                def _():
                    page_copy(source, slot, buffer, place).start()

    def arrive(t):
        buffer = lax.rem(t, 2)

        @pl.loop(0, counts[request_of(t)])
        def _(place):
            page_copy(own, 0, buffer, place).wait()

    def store_copy(slot):
        return pltpu.make_async_copy(pool.at[slot], pool_out.at[slot], store_sems.at[slot])

    fresh_copy = pltpu.make_async_copy(fresh.at[:, :, columns], pages.at[0, extra], page_sems.at[0, extra])
    for t in range(lines):
        for h in range(GQ):
            q_copy(t, h).start()
    for buffer in range(2):
        pages[buffer, :extra] = jnp.zeros((extra,) + pages.shape[2:], pages.dtype)
    fresh_copy.start()
    fetch(0)
    if lines > 1:
        fetch(1)
    if stores:
        @pl.loop(0, pool.shape[0])
        def _(slot):
            @pl.when(slot != store[0])
            def _():
                store_copy(slot).start()

        pltpu.make_async_copy(incoming.at[0], pool_out.at[store[0]], store_sems.at[store[0]]).start()

    def soften(heads, scored, values):
        factor = SCALE * LOG2E
        expos = []
        fades = []
        for h in heads:
            s = scored(h)
            old = tops[h]
            new = jnp.maximum(old, jnp.max(s, axis=1, keepdims=True))
            tops[h] = new
            fades.append(jnp.exp2((old - new) * factor))
            wide = jnp.concatenate([new] * (s.shape[1] // PAGE), axis=1)
            expos.append(jnp.exp2((s - wide) * factor).astype(jnp.bfloat16))
        added = jnp.dot(jnp.concatenate(expos, axis=0), values, preferred_element_type=jnp.float32)
        for i, h in enumerate(heads):
            fade = fades[i]
            acc[h] = acc[h] * jnp.concatenate([fade, fade], axis=1) + added[i * PAGE:(i + 1) * PAGE]

    def with_ones(values):
        return jnp.concatenate([values, jnp.ones_like(values)], axis=1)

    def score(t, heads, keys):
        query = queries[t, heads[0]:heads[-1] + 1].reshape(len(heads) * PAGE, HD)
        s = lax.dot_general(query, keys, CONTRACT_LAST, preferred_element_type=jnp.float32)
        return s.reshape(len(heads), PAGE, keys.shape[0])

    def keys_of(t, index):
        return pages[lax.rem(t, 2), pl.ds(index * BLOCK, BLOCK), 0].reshape(BLOCK * PAGE, HD)

    def values_of(t, index):
        return with_ones(pages[lax.rem(t, 2), pl.ds(index * BLOCK, BLOCK), 1].reshape(BLOCK * PAGE, HD))

    def blocks_of(t):
        return jnp.maximum(lax.div(counts[request_of(t)] + BLOCK - 1, BLOCK), 1)

    def reset():
        tops[...] = jnp.full(tops.shape, LOW, jnp.float32)
        acc[...] = jnp.zeros(acc.shape, jnp.float32)

    def finish(t):
        some = (counts[request_of(t)] > 0) | (t == 0)
        lane = lax.broadcasted_iota(jnp.int32, (PAGE, PAGE), 1)
        sums = jnp.ones((PAGE, PAGE), jnp.float32)
        heights = jnp.zeros((PAGE, PAGE), jnp.float32)
        for h in range(GQ):
            total = acc[h, :, HD:]
            results[t, h * PAGE:(h + 1) * PAGE, :] = (acc[h, :, :HD] * (1.0 / total)).astype(jnp.bfloat16)
            sums = jnp.where(lane == h, total, sums)
            heights = jnp.where(lane == h, tops[h], heights)
        level = heights.T[:8] * SCALE + jnp.log(sums.T[:8])
        level = jnp.where(some, level, LOW)
        high = level.astype(jnp.bfloat16).astype(jnp.float32)
        middle = (level - high).astype(jnp.bfloat16).astype(jnp.float32)
        low = level - high - middle
        stat = jnp.concatenate([high, middle, low, jnp.zeros_like(low)], axis=0)
        results[t, GQ * PAGE:, :] = stat.astype(jnp.bfloat16)
        out_copy(t).start()

    for t in range(lines):
        for h in range(GQ):
            q_copy(t, h).wait()
    fresh_copy.wait()
    reset()
    span_values = with_ones(pages[0, extra, 1])
    seen = lax.broadcasted_iota(jnp.int32, (PAGE, PAGE), 1) <= lax.broadcasted_iota(jnp.int32, (PAGE, PAGE), 0)
    for heads in HEADS:
        s = score(0, heads, pages[0, extra, 0])
        soften(heads, lambda h: jnp.where(seen, s[h - heads[0]], LOW), span_values)
    arrive(0)
    first = keys_of(0, 0)
    for heads in HEADS:
        scores[heads[0]:heads[-1] + 1] = score(0, heads, first)

    def step(_, carry):
        t, index = carry
        request = request_of(t)
        ends = index + 1 >= blocks_of(t)
        later_t = jnp.where(ends, t + 1, t)
        later_index = jnp.where(ends, 0, index + 1)
        ahead_t = jnp.minimum(later_t, lines - 1)

        @pl.when(ends & (t + 1 < lines))
        def _():
            arrive(t + 1)

        limit = (counts[request] - 1 - index * BLOCK) * PAGE + lasts[request]
        column = lax.broadcasted_iota(jnp.int32, (PAGE, BLOCK * PAGE), 1)
        values = values_of(t, index)
        keys = keys_of(ahead_t, later_index)
        for heads in HEADS:
            soften(heads, lambda h: jnp.where(column < limit, scores[h], LOW), values)
            scores[heads[0]:heads[-1] + 1] = score(ahead_t, heads, keys)

        @pl.when(ends)
        def _():
            finish(t)
            reset()

            @pl.when(t + 2 < lines)
            def _():
                fetch(t + 2)

        return later_t, later_index

    steps = blocks_of(0)
    for t in range(1, lines):
        steps += blocks_of(t)
    lax.fori_loop(0, steps, step, (jnp.int32(0), jnp.int32(0)))
    for t in range(lines):
        out_copy(t).wait()
    if stores:
        @pl.loop(0, pool.shape[0])
        def _(slot):
            store_copy(slot).wait()


def attend(head, q_head, tables, q_all, pools, fresh, pool=None, incoming=None):
    picks, counts, lasts, mine, store = tables
    lines = q_all.shape[0]
    places = picks.shape[1]
    out_shape = [jax.ShapeDtypeStruct((lines, ROWS, HD), jnp.bfloat16)]
    scratch = [
        pltpu.VMEM((2, places + 1, 2, PAGE, HD), jnp.bfloat16),
        pltpu.VMEM((lines, GQ, PAGE, HD), jnp.bfloat16),
        pltpu.VMEM((lines, ROWS, HD), jnp.bfloat16),
        pltpu.VMEM((GQ, PAGE, BLOCK * PAGE), jnp.float32),
        pltpu.VMEM((GQ, PAGE, PAGE), jnp.float32),
        pltpu.VMEM((GQ, PAGE, 2 * HD), jnp.float32),
        pltpu.SemaphoreType.DMA((lines, GQ)),
        pltpu.SemaphoreType.DMA((2, places + 1)),
        pltpu.SemaphoreType.DMA((lines,)),
    ]
    operands = [q_all, *pools, fresh]
    if incoming is not None:
        operands += [pool, incoming]
        out_shape.append(jax.ShapeDtypeStruct(pool.shape, pool.dtype))
        scratch.append(pltpu.SemaphoreType.DMA((pool.shape[0],)))
    grid_spec = pltpu.PrefetchScalarGridSpec(
        num_scalar_prefetch=5,
        grid=(),
        in_specs=[pl.BlockSpec(memory_space=pl.ANY)] * len(operands),
        out_specs=[pl.BlockSpec(memory_space=pl.ANY), pl.BlockSpec(memory_space=pltpu.HBM)][:len(out_shape)],
        scratch_shapes=scratch,
    )
    return pl.pallas_call(
        functools.partial(attend_kernel, lines, head, q_head),
        grid_spec=grid_spec,
        out_shape=out_shape,
        compiler_params=pltpu.CompilerParams(vmem_limit_bytes=24 * 2**20),
        cost_estimate=pl.CostEstimate(flops=1, bytes_accessed=1, transcendentals=0),
    )(picks, counts, lasts, mine, store, *operands)


def merge_kernel(head, parts, *refs):
    lines = parts.shape[0]
    out, result, sem = refs[-3:]
    levels = []
    for i in range(lines):
        block = parts[i, GQ * PAGE:, :].astype(jnp.float32)
        levels.append(block[:8] + block[8:16] + block[16:24])
    top = functools.reduce(jnp.maximum, levels)
    weights = [jnp.exp(level - top) for level in levels]
    total = functools.reduce(jnp.add, weights)
    weights = [weight / total for weight in weights]
    filler = PAGE - lines * 8
    if filler:
        weights.append(jnp.zeros((filler, PAGE), jnp.float32))
    table = jnp.concatenate(weights, axis=0).T
    for h in range(GQ):
        merged = jnp.zeros((PAGE, HD), jnp.float32)
        for i in range(lines):
            column = i * 8 + h
            merged += table[:, column:column + 1] * parts[i, h * PAGE:(h + 1) * PAGE, :].astype(jnp.float32)
        result[:, h * HD:(h + 1) * HD] = merged.astype(jnp.bfloat16)
    copy = pltpu.make_async_copy(result, out.at[:, pl.ds(head * CHUNK, CHUNK)], sem)
    copy.start()
    copy.wait()


def merge(head, parts, whole):
    before = [] if whole is None else [whole]
    return pl.pallas_call(
        functools.partial(merge_kernel, head),
        in_specs=[pl.BlockSpec(memory_space=pltpu.VMEM)] + [pl.BlockSpec(memory_space=pl.ANY)] * len(before),
        out_specs=pl.BlockSpec(memory_space=pl.ANY),
        out_shape=jax.ShapeDtypeStruct((PAGE, KVH * CHUNK), jnp.bfloat16),
        scratch_shapes=[pltpu.VMEM((PAGE, CHUNK), jnp.bfloat16), pltpu.SemaphoreType.DMA],
        input_output_aliases={1: 0} if before else {},
        cost_estimate=pl.CostEstimate(flops=1, bytes_accessed=1, transcendentals=0),
    )(parts, *before)


def page_rows(me, lines, limit, slots, page_owner, page_slot, prefix_len):
    owners = page_owner[0]
    length = prefix_len[0]
    used = (length + PAGE - 1) // PAGE
    spot = jnp.arange(MAXP)
    here = (spot < used)[None] & (owners[None] // CLUSTER == jnp.arange(lines)[:, None])
    before = jnp.sum(here[:, None, :] & (spot[None, None, :] < spot[None, :, None]), axis=2)
    local = ((owners % CLUSTER) ^ (me % CLUSTER)) * slots + page_slot[0]
    chosen = here[:, :, None] & (before[:, :, None] == jnp.arange(limit)[None, None, :])
    picks = jnp.sum(jnp.where(chosen, local[None, :, None], 0), axis=1)
    counts = jnp.sum(here, axis=1)
    tail = jnp.any(here & (spot == used - 1)[None], axis=1)
    lasts = jnp.where(tail, length - (used - 1) * PAGE, PAGE)
    return jnp.concatenate([picks, counts[:, None], lasts[:, None]], axis=1)


def exchanged(array, groups):
    return lax.all_to_all(array, "serve", 0, 0, axis_index_groups=groups, tiled=True)


def after(array, *others):
    return lax.optimization_barrier((array, *others))[0]


def per_device(queries, new_kv, pool, page_owner, page_slot, prefix_len, store_slot):
    width = lax.axis_size("serve")
    lines = width // CLUSTER
    groups = [[c * CLUSTER + i for c in range(lines)] for i in range(CLUSTER)]
    me = lax.axis_index("serve")
    slots = pool.shape[0]
    capacity = (MAXP + width - 2) // (width - 1)
    limit = min(MAXP, CLUSTER * capacity)
    owns = [pool[:, :, :, :HD]]
    rest = after(pool, owns[0])
    owns += [rest[:, :, :, g * HD:(g + 1) * HD] for g in range(1, KVH)]
    sides = [swapped(own, "serve", 2) for own in owns]
    twin = swapped(rest, "serve", 1)
    incoming = shifted(new_kv[0], "serve", 1)
    rows = page_rows(me, lines, limit, slots, page_owner, page_slot, prefix_len).astype(queries.dtype)
    rows = jnp.pad(rows[:, None], ((0, 0), (0, 15), (0, CHUNK - limit - 2)))
    early = after(queries, owns[1])[:, :CHUNK]
    early = jnp.concatenate([jnp.broadcast_to(early[None], (lines, PAGE, CHUNK)), rows], axis=1)
    early = exchanged(early, groups)
    later = after(queries, sides[0], incoming)[None, :, CHUNK:]
    later = exchanged(jnp.broadcast_to(later, (lines, PAGE, (KVH - 1) * CHUNK)), groups)
    numbers = early[:, PAGE, :limit + 2].astype(jnp.int32)
    tables = (numbers[:, :limit], numbers[:, limit], numbers[:, limit + 1], (me // CLUSTER)[None], store_slot[0])
    fresh = new_kv[0, 0]
    attended = None
    parts = None
    for g in range(KVH):
        side = sides[g] if g == 0 else after(sides[g], parts)
        both = swapped(side, "serve", 1)
        pools = (owns[g], twin, side, both)
        if g == 0:
            parts, pool_out = attend(g, 0, tables, early, pools, fresh, pool, incoming)
        else:
            parts = attend(g, g - 1, tables, later, pools, fresh)[0]
        attended = merge(g, exchanged(parts, groups), attended)
    return (attended, pool_out)


def solution(mesh):
    return jax.shard_map(
        per_device,
        mesh=mesh,
        in_specs=(
            P(("groups", "serve"), None),
            P(("groups", "serve"), None, None, None, None),
            P(("groups", "serve"), None, None, None),
            P(("groups", "serve"), None),
            P(("groups", "serve"), None),
            P(("groups", "serve")),
            P(("groups", "serve"), None),
        ),
        out_specs=(P(("groups", "serve"), None), P(("groups", "serve"), None, None, None)),
        check_vma=False,
    )
```

```python
import functools

import jax
import jax.numpy as jnp
from jax import lax
from jax.experimental import pallas as pl
from jax.experimental.pallas import tpu as pltpu
from jax.sharding import PartitionSpec as P

PAGE = 128
KVH = 4
GQ = 5
HD = 128
MAXP = 48
SCALE = HD ** (-0.5)
LOG2E = 1.4426950408889634
LOW = -1e30
CLUSTER = 4
BLOCK = 4
STAT = 32
HEADS = ((0, 1, 2), (3, 4))
ROWS = GQ * PAGE + STAT
CHUNK = GQ * HD
CONTRACT_LAST = (((1,), (1,)), ((), ()))


def swapped(array, axis, bit):
    size = lax.axis_size(axis)
    return lax.ppermute(array, axis, [(i, i ^ bit) for i in range(size)])


def shifted(array, axis, by):
    size = lax.axis_size(axis)
    return lax.ppermute(array, axis, [(i, (i + by) % size) for i in range(size)])


def attend_kernel(lines, head, limit, numbers, mine, *refs):
    q_all, own, twin, side, both, fresh, out = refs[:7]
    pages, queries, results, scores, tops, acc, q_sems, page_sems, out_sems = refs[7:]
    slots = own.shape[0]
    columns = pl.ds(head * HD, HD)
    extra = pages.shape[1] - 1

    def number(request, place):
        return numbers[request, mine[0] * (limit + 2) + place]

    def count_of(t):
        return number(request_of(t), limit)

    def request_of(t):
        return lax.rem(mine[0] - t + lines, lines)

    def q_copy(t, h):
        origin = q_all.at[request_of(t), pl.ds(0, PAGE), pl.ds((head * GQ + h) * HD, HD)]
        return pltpu.make_async_copy(origin, queries.at[t, h], q_sems.at[t, h])

    def out_copy(t):
        return pltpu.make_async_copy(results.at[t], out.at[request_of(t)], out_sems.at[t])

    def page_copy(source, slot, buffer, place):
        if source.shape[-1] == HD:
            origin = source.at[slot]
        else:
            origin = source.at[slot, :, :, columns]
        return pltpu.make_async_copy(origin, pages.at[buffer, place], page_sems.at[buffer, place])

    def fetch(t):
        request = request_of(t)
        buffer = lax.rem(t, 2)

        @pl.loop(0, count_of(t))
        def _(place):
            code = number(request, place)
            rank = lax.div(code, slots)
            slot = lax.rem(code, slots)
            for index, source in enumerate((own, twin, side, both)):
                @pl.when(rank == index)
                def _():
                    page_copy(source, slot, buffer, place).start()

    def arrive(t):
        buffer = lax.rem(t, 2)

        @pl.loop(0, count_of(t))
        def _(place):
            page_copy(own, 0, buffer, place).wait()

    fresh_copy = pltpu.make_async_copy(fresh.at[:, :, columns], pages.at[0, extra], page_sems.at[0, extra])
    for t in range(lines):
        for h in range(GQ):
            q_copy(t, h).start()
    for buffer in range(2):
        pages[buffer, :extra] = jnp.zeros((extra,) + pages.shape[2:], pages.dtype)
    fresh_copy.start()
    fetch(0)
    if lines > 1:
        fetch(1)
    def soften(heads, scored, values):
        factor = SCALE * LOG2E
        expos = []
        fades = []
        for h in heads:
            s = scored(h)
            old = tops[h]
            new = jnp.maximum(old, jnp.max(s, axis=1, keepdims=True))
            tops[h] = new
            fades.append(jnp.exp2((old - new) * factor))
            wide = jnp.concatenate([new] * (s.shape[1] // PAGE), axis=1)
            expos.append(jnp.exp2((s - wide) * factor).astype(jnp.bfloat16))
        added = jnp.dot(jnp.concatenate(expos, axis=0), values, preferred_element_type=jnp.float32)
        for i, h in enumerate(heads):
            fade = fades[i]
            acc[h] = acc[h] * jnp.concatenate([fade, fade], axis=1) + added[i * PAGE:(i + 1) * PAGE]

    def with_ones(values):
        return jnp.concatenate([values, jnp.ones_like(values)], axis=1)

    def score(t, heads, keys):
        query = queries[t, heads[0]:heads[-1] + 1].reshape(len(heads) * PAGE, HD)
        s = lax.dot_general(query, keys, CONTRACT_LAST, preferred_element_type=jnp.float32)
        return s.reshape(len(heads), PAGE, keys.shape[0])

    def keys_of(t, index):
        return pages[lax.rem(t, 2), pl.ds(index * BLOCK, BLOCK), 0].reshape(BLOCK * PAGE, HD)

    def values_of(t, index):
        return with_ones(pages[lax.rem(t, 2), pl.ds(index * BLOCK, BLOCK), 1].reshape(BLOCK * PAGE, HD))

    def blocks_of(t):
        return jnp.maximum(lax.div(count_of(t) + BLOCK - 1, BLOCK), 1)

    def reset():
        tops[...] = jnp.full(tops.shape, LOW, jnp.float32)
        acc[...] = jnp.zeros(acc.shape, jnp.float32)

    def finish(t):
        some = (count_of(t) > 0) | (t == 0)
        lane = lax.broadcasted_iota(jnp.int32, (PAGE, PAGE), 1)
        sums = jnp.ones((PAGE, PAGE), jnp.float32)
        heights = jnp.zeros((PAGE, PAGE), jnp.float32)
        for h in range(GQ):
            total = acc[h, :, HD:]
            results[t, h * PAGE:(h + 1) * PAGE, :] = (acc[h, :, :HD] * (1.0 / total)).astype(jnp.bfloat16)
            sums = jnp.where(lane == h, total, sums)
            heights = jnp.where(lane == h, tops[h], heights)
        level = heights.T[:8] * SCALE + jnp.log(sums.T[:8])
        level = jnp.where(some, level, LOW)
        high = level.astype(jnp.bfloat16).astype(jnp.float32)
        middle = (level - high).astype(jnp.bfloat16).astype(jnp.float32)
        low = level - high - middle
        stat = jnp.concatenate([high, middle, low, jnp.zeros_like(low)], axis=0)
        results[t, GQ * PAGE:, :] = stat.astype(jnp.bfloat16)
        out_copy(t).start()

    for t in range(lines):
        for h in range(GQ):
            q_copy(t, h).wait()
    fresh_copy.wait()
    reset()
    span_values = with_ones(pages[0, extra, 1])
    seen = lax.broadcasted_iota(jnp.int32, (PAGE, PAGE), 1) <= lax.broadcasted_iota(jnp.int32, (PAGE, PAGE), 0)
    for heads in HEADS:
        s = score(0, heads, pages[0, extra, 0])
        soften(heads, lambda h: jnp.where(seen, s[h - heads[0]], LOW), span_values)
    arrive(0)
    first = keys_of(0, 0)
    for heads in HEADS:
        scores[heads[0]:heads[-1] + 1] = score(0, heads, first)

    def step(_, carry):
        t, index = carry
        request = request_of(t)
        ends = index + 1 >= blocks_of(t)
        later_t = jnp.where(ends, t + 1, t)
        later_index = jnp.where(ends, 0, index + 1)
        ahead_t = jnp.minimum(later_t, lines - 1)

        @pl.when(ends & (t + 1 < lines))
        def _():
            arrive(t + 1)

        seen_here = (count_of(t) - 1 - index * BLOCK) * PAGE + number(request, limit + 1)
        column = lax.broadcasted_iota(jnp.int32, (PAGE, BLOCK * PAGE), 1)
        values = values_of(t, index)
        keys = keys_of(ahead_t, later_index)
        for heads in HEADS:
            soften(heads, lambda h: jnp.where(column < seen_here, scores[h], LOW), values)
            scores[heads[0]:heads[-1] + 1] = score(ahead_t, heads, keys)

        @pl.when(ends)
        def _():
            finish(t)
            reset()

            @pl.when(t + 2 < lines)
            def _():
                fetch(t + 2)

        return later_t, later_index

    steps = blocks_of(0)
    for t in range(1, lines):
        steps += blocks_of(t)
    lax.fori_loop(0, steps, step, (jnp.int32(0), jnp.int32(0)))
    for t in range(lines):
        out_copy(t).wait()


def attend(head, limit, numbers, mine, q_all, pools, fresh):
    lines = q_all.shape[0]
    operands = [q_all, *pools, fresh]
    grid_spec = pltpu.PrefetchScalarGridSpec(
        num_scalar_prefetch=2,
        grid=(),
        in_specs=[pl.BlockSpec(memory_space=pl.ANY)] * len(operands),
        out_specs=pl.BlockSpec(memory_space=pltpu.HBM),
        scratch_shapes=[
            pltpu.VMEM((2, limit + 1, 2, PAGE, HD), jnp.bfloat16),
            pltpu.VMEM((lines, GQ, PAGE, HD), jnp.bfloat16),
            pltpu.VMEM((lines, ROWS, HD), jnp.bfloat16),
            pltpu.VMEM((GQ, PAGE, BLOCK * PAGE), jnp.float32),
            pltpu.VMEM((GQ, PAGE, PAGE), jnp.float32),
            pltpu.VMEM((GQ, PAGE, 2 * HD), jnp.float32),
            pltpu.SemaphoreType.DMA((lines, GQ)),
            pltpu.SemaphoreType.DMA((2, limit + 1)),
            pltpu.SemaphoreType.DMA((lines,)),
        ],
    )
    return pl.pallas_call(
        functools.partial(attend_kernel, lines, head, limit),
        grid_spec=grid_spec,
        out_shape=jax.ShapeDtypeStruct((lines, ROWS, HD), jnp.bfloat16),
        compiler_params=pltpu.CompilerParams(vmem_limit_bytes=16 * 2**20),
        cost_estimate=pl.CostEstimate(flops=1, bytes_accessed=1, transcendentals=0),
    )(numbers, mine, *operands)


def store_kernel(slot, pool, incoming, out, sems):
    pages = pool.shape[0]

    def copy(page):
        return pltpu.make_async_copy(pool.at[page], out.at[page], sems.at[page])

    for page in range(pages):
        @pl.when(slot[0] != page)
        def _():
            copy(page).start()

        @pl.when(slot[0] == page)
        def _():
            pltpu.make_async_copy(incoming.at[0], out.at[page], sems.at[page]).start()

    for page in range(pages):
        copy(page).wait()


def store(slot, pool, incoming):
    grid_spec = pltpu.PrefetchScalarGridSpec(
        num_scalar_prefetch=1,
        grid=(),
        in_specs=[pl.BlockSpec(memory_space=pl.ANY)] * 2,
        out_specs=pl.BlockSpec(memory_space=pltpu.HBM),
        scratch_shapes=[pltpu.SemaphoreType.DMA((pool.shape[0],))],
    )
    return pl.pallas_call(
        store_kernel,
        grid_spec=grid_spec,
        out_shape=jax.ShapeDtypeStruct(pool.shape, pool.dtype),
        compiler_params=pltpu.CompilerParams(vmem_limit_bytes=16 * 2**20),
        cost_estimate=pl.CostEstimate(flops=1, bytes_accessed=1, transcendentals=0),
    )(slot, pool, incoming)


def merge_kernel(head, parts, *refs):
    lines = parts.shape[0]
    out, result, sem = refs[-3:]
    levels = []
    for i in range(lines):
        block = parts[i, GQ * PAGE:, :].astype(jnp.float32)
        levels.append(block[:8] + block[8:16] + block[16:24])
    top = functools.reduce(jnp.maximum, levels)
    weights = [jnp.exp(level - top) for level in levels]
    total = functools.reduce(jnp.add, weights)
    weights = [weight / total for weight in weights]
    filler = PAGE - lines * 8
    if filler:
        weights.append(jnp.zeros((filler, PAGE), jnp.float32))
    table = jnp.concatenate(weights, axis=0).T
    for h in range(GQ):
        merged = jnp.zeros((PAGE, HD), jnp.float32)
        for i in range(lines):
            column = i * 8 + h
            merged += table[:, column:column + 1] * parts[i, h * PAGE:(h + 1) * PAGE, :].astype(jnp.float32)
        result[:, h * HD:(h + 1) * HD] = merged.astype(jnp.bfloat16)
    copy = pltpu.make_async_copy(result, out.at[:, pl.ds(head * CHUNK, CHUNK)], sem)
    copy.start()
    copy.wait()


def merge(head, parts, whole):
    before = [] if whole is None else [whole]
    return pl.pallas_call(
        functools.partial(merge_kernel, head),
        in_specs=[pl.BlockSpec(memory_space=pltpu.VMEM)] + [pl.BlockSpec(memory_space=pl.ANY)] * len(before),
        out_specs=pl.BlockSpec(memory_space=pl.ANY),
        out_shape=jax.ShapeDtypeStruct((PAGE, KVH * CHUNK), jnp.bfloat16),
        scratch_shapes=[pltpu.VMEM((PAGE, CHUNK), jnp.bfloat16), pltpu.SemaphoreType.DMA],
        input_output_aliases={1: 0} if before else {},
        cost_estimate=pl.CostEstimate(flops=1, bytes_accessed=1, transcendentals=0),
    )(parts, *before)


def page_rows(me, lines, limit, slots, page_owner, page_slot, prefix_len):
    owners = page_owner[0]
    length = prefix_len[0]
    used = (length + PAGE - 1) // PAGE
    spot = jnp.arange(MAXP)
    here = (spot < used)[None] & (owners[None] // CLUSTER == jnp.arange(lines)[:, None])
    before = jnp.sum(here[:, None, :] & (spot[None, None, :] < spot[None, :, None]), axis=2)
    local = ((owners % CLUSTER) ^ (me % CLUSTER)) * slots + page_slot[0]
    chosen = here[:, :, None] & (before[:, :, None] == jnp.arange(limit)[None, None, :])
    picks = jnp.sum(jnp.where(chosen, local[None, :, None], 0), axis=1)
    counts = jnp.sum(here, axis=1)
    tail = jnp.any(here & (spot == used - 1)[None], axis=1)
    lasts = jnp.where(tail, length - (used - 1) * PAGE, PAGE)
    return jnp.concatenate([picks, counts[:, None], lasts[:, None]], axis=1)


def exchanged(array, groups):
    return lax.all_to_all(array, "serve", 0, 0, axis_index_groups=groups, tiled=True)


def after(array, *others):
    return lax.optimization_barrier((array, *others))[0]


def per_device(queries, new_kv, pool, page_owner, page_slot, prefix_len, store_slot):
    width = lax.axis_size("serve")
    lines = width // CLUSTER
    groups = [[c * CLUSTER + i for c in range(lines)] for i in range(CLUSTER)]
    me = lax.axis_index("serve")
    slots = pool.shape[0]
    capacity = (MAXP + width - 2) // (width - 1)
    limit = min(MAXP, CLUSTER * capacity)
    owns = [pool[:, :, :, :HD]]
    rest = after(pool, owns[0])
    owns += [rest[:, :, :, g * HD:(g + 1) * HD] for g in range(1, KVH)]
    sides = [swapped(own, "serve", 2) for own in owns]
    twin = swapped(rest, "serve", 1)
    incoming = shifted(new_kv[0], "serve", 1)
    numbers = page_rows(me, lines, limit, slots, page_owner, page_slot, prefix_len).astype(queries.dtype)
    numbers = jnp.pad(numbers.reshape(1, -1), ((0, PAGE - 1), (0, PAGE - lines * (limit + 2))))
    sent = jnp.concatenate([after(queries, owns[1]), numbers], axis=1)
    q_all = lax.all_gather(sent, "serve", axis_index_groups=groups)
    numbers = q_all[:, 0, KVH * CHUNK:].astype(jnp.int32)
    mine = (me // CLUSTER)[None]
    fresh = new_kv[0, 0]
    attended = None
    parts = None
    for g in range(KVH):
        side = sides[g] if g == 0 else after(sides[g], parts)
        both = swapped(side, "serve", 1)
        parts = attend(g, limit, numbers, mine, q_all, (owns[g], twin, side, both), fresh)
        attended = merge(g, exchanged(parts, groups), attended)
    pool_out = store(store_slot[0], pool, after(incoming, parts))
    return (attended, pool_out)


def solution(mesh):
    return jax.shard_map(
        per_device,
        mesh=mesh,
        in_specs=(
            P(("groups", "serve"), None),
            P(("groups", "serve"), None, None, None, None),
            P(("groups", "serve"), None, None, None),
            P(("groups", "serve"), None),
            P(("groups", "serve"), None),
            P(("groups", "serve")),
            P(("groups", "serve"), None),
        ),
        out_specs=(P(("groups", "serve"), None), P(("groups", "serve"), None, None, None)),
        check_vma=False,
    )
```

```python
import functools

import jax
import jax.numpy as jnp
from jax import lax
from jax.experimental import pallas as pl
from jax.experimental.pallas import tpu as pltpu
from jax.sharding import PartitionSpec as P

PAGE = 128
KVH = 4
GQ = 5
HD = 128
MAXP = 48
SCALE = HD ** (-0.5)
LOG2E = 1.4426950408889634
LOW = -1e30
CLUSTER = 4
BLOCK = 4
STAT = 32
HEADS = ((0, 1, 2), (3, 4))
ROWS = GQ * PAGE + STAT
CHUNK = GQ * HD
CONTRACT_LAST = (((1,), (1,)), ((), ()))


def swapped(array, axis, bit):
    size = lax.axis_size(axis)
    return lax.ppermute(array, axis, [(i, i ^ bit) for i in range(size)])


def shifted(array, axis, by):
    size = lax.axis_size(axis)
    return lax.ppermute(array, axis, [(i, (i + by) % size) for i in range(size)])


def attend_kernel(lines, head, q_head, numbers, mine, *refs):
    q_all, pair, other, fresh, out = refs[:5]
    pages, queries, results, scores, tops, acc, found, q_sems, page_sems, out_sems = refs[5:]
    slots = pair.shape[1]
    columns = pl.ds(head * HD, HD)
    extra = pages.shape[1] - 1
    cluster = mine[0]
    core = mine[1]

    def request_of(t):
        return lax.rem(cluster - t + lines, lines)

    def q_copy(t, h):
        origin = q_all.at[request_of(t), pl.ds(0, PAGE), pl.ds((q_head * GQ + h) * HD, HD)]
        return pltpu.make_async_copy(origin, queries.at[t, h], q_sems.at[t, h])

    def out_copy(t):
        return pltpu.make_async_copy(results.at[t], out.at[request_of(t)], out_sems.at[t])

    def page_copy(source, row, slot, buffer, place):
        return pltpu.make_async_copy(source.at[row, slot], pages.at[buffer, place], page_sems.at[buffer, place])

    def fetch(t):
        request = request_of(t)
        buffer = lax.rem(t, 2)

        def look(j, place):
            owner = numbers[request, j]
            here = lax.div(owner, CLUSTER) == cluster
            slot = numbers[request, MAXP + j]
            local = lax.rem(owner, CLUSTER)
            row = lax.div(local, 2)
            same = lax.rem(local, 2) == core

            @pl.when(here & same)
            def _():
                page_copy(pair, row, slot, buffer, place).start()

            @pl.when(here & jnp.logical_not(same))
            def _():
                page_copy(other, row, slot, buffer, place).start()

            return place + here.astype(jnp.int32)

        found[t] = lax.fori_loop(0, numbers[request, 2 * MAXP], look, jnp.int32(0))

    def arrive(t):
        buffer = lax.rem(t, 2)

        @pl.loop(0, found[t])
        def _(place):
            page_copy(pair, 0, 0, buffer, place).wait()

    def tokens_of(t):
        request = request_of(t)
        owner = numbers[request, numbers[request, 2 * MAXP] - 1]
        last = jnp.where(lax.div(owner, CLUSTER) == cluster, numbers[request, 2 * MAXP + 1], PAGE)
        return (found[t] - 1) * PAGE + last

    fresh_copy = pltpu.make_async_copy(fresh.at[:, :, columns], pages.at[0, extra], page_sems.at[0, extra])
    for t in range(lines):
        for h in range(GQ):
            q_copy(t, h).start()
    for buffer in range(2):
        pages[buffer, :extra] = jnp.zeros((extra,) + pages.shape[2:], pages.dtype)
    fresh_copy.start()
    fetch(0)
    if lines > 1:
        fetch(1)
    def soften(heads, scored, values):
        factor = SCALE * LOG2E
        expos = []
        fades = []
        for h in heads:
            s = scored(h)
            old = tops[h]
            new = jnp.maximum(old, jnp.max(s, axis=1, keepdims=True))
            tops[h] = new
            fades.append(jnp.exp2((old - new) * factor))
            wide = jnp.concatenate([new] * (s.shape[1] // PAGE), axis=1)
            expos.append(jnp.exp2((s - wide) * factor).astype(jnp.bfloat16))
        added = jnp.dot(jnp.concatenate(expos, axis=0), values, preferred_element_type=jnp.float32)
        for i, h in enumerate(heads):
            fade = fades[i]
            acc[h] = acc[h] * jnp.concatenate([fade, fade], axis=1) + added[i * PAGE:(i + 1) * PAGE]

    def with_ones(values):
        return jnp.concatenate([values, jnp.ones_like(values)], axis=1)

    def score(t, heads, keys):
        query = queries[t, heads[0]:heads[-1] + 1].reshape(len(heads) * PAGE, HD)
        s = lax.dot_general(query, keys, CONTRACT_LAST, preferred_element_type=jnp.float32)
        return s.reshape(len(heads), PAGE, keys.shape[0])

    def keys_of(t, index):
        return pages[lax.rem(t, 2), pl.ds(index * BLOCK, BLOCK), 0].reshape(BLOCK * PAGE, HD)

    def values_of(t, index):
        return with_ones(pages[lax.rem(t, 2), pl.ds(index * BLOCK, BLOCK), 1].reshape(BLOCK * PAGE, HD))

    def blocks_of(t):
        return jnp.maximum(lax.div(found[t] + BLOCK - 1, BLOCK), 1)

    def reset():
        tops[...] = jnp.full(tops.shape, LOW, jnp.float32)
        acc[...] = jnp.zeros(acc.shape, jnp.float32)

    def finish(t):
        some = (found[t] > 0) | (t == 0)
        lane = lax.broadcasted_iota(jnp.int32, (PAGE, PAGE), 1)
        sums = jnp.ones((PAGE, PAGE), jnp.float32)
        heights = jnp.zeros((PAGE, PAGE), jnp.float32)
        for h in range(GQ):
            total = acc[h, :, HD:]
            results[t, h * PAGE:(h + 1) * PAGE, :] = (acc[h, :, :HD] * (1.0 / total)).astype(jnp.bfloat16)
            sums = jnp.where(lane == h, total, sums)
            heights = jnp.where(lane == h, tops[h], heights)
        level = heights.T[:8] * SCALE + jnp.log(sums.T[:8])
        level = jnp.where(some, level, LOW)
        high = level.astype(jnp.bfloat16).astype(jnp.float32)
        middle = (level - high).astype(jnp.bfloat16).astype(jnp.float32)
        low = level - high - middle
        stat = jnp.concatenate([high, middle, low, jnp.zeros_like(low)], axis=0)
        results[t, GQ * PAGE:, :] = stat.astype(jnp.bfloat16)
        out_copy(t).start()

    for t in range(lines):
        for h in range(GQ):
            q_copy(t, h).wait()
    fresh_copy.wait()
    reset()
    span_values = with_ones(pages[0, extra, 1])
    seen = lax.broadcasted_iota(jnp.int32, (PAGE, PAGE), 1) <= lax.broadcasted_iota(jnp.int32, (PAGE, PAGE), 0)
    for heads in HEADS:
        s = score(0, heads, pages[0, extra, 0])
        soften(heads, lambda h: jnp.where(seen, s[h - heads[0]], LOW), span_values)
    arrive(0)
    first = keys_of(0, 0)
    for heads in HEADS:
        scores[heads[0]:heads[-1] + 1] = score(0, heads, first)

    def step(carry):
        t, index = carry
        ends = index + 1 >= blocks_of(t)
        later_t = jnp.where(ends, t + 1, t)
        later_index = jnp.where(ends, 0, index + 1)
        ahead_t = jnp.minimum(later_t, lines - 1)

        @pl.when(ends & (t + 1 < lines))
        def _():
            arrive(t + 1)

        seen_here = tokens_of(t) - index * BLOCK * PAGE
        column = lax.broadcasted_iota(jnp.int32, (PAGE, BLOCK * PAGE), 1)
        values = values_of(t, index)
        keys = keys_of(ahead_t, later_index)
        for heads in HEADS:
            soften(heads, lambda h: jnp.where(column < seen_here, scores[h], LOW), values)
            scores[heads[0]:heads[-1] + 1] = score(ahead_t, heads, keys)

        @pl.when(ends)
        def _():
            finish(t)
            reset()

            @pl.when(t + 2 < lines)
            def _():
                fetch(t + 2)

        return later_t, later_index

    lax.while_loop(lambda carry: carry[0] < lines, step, (jnp.int32(0), jnp.int32(0)))
    for t in range(lines):
        out_copy(t).wait()


def attend(head, q_head, limit, numbers, mine, q_all, pair, other, fresh):
    lines = q_all.shape[0]
    operands = [q_all, pair, other, fresh]
    grid_spec = pltpu.PrefetchScalarGridSpec(
        num_scalar_prefetch=2,
        grid=(),
        in_specs=[pl.BlockSpec(memory_space=pl.ANY)] * len(operands),
        out_specs=pl.BlockSpec(memory_space=pltpu.HBM),
        scratch_shapes=[
            pltpu.VMEM((2, limit + 1, 2, PAGE, HD), jnp.bfloat16),
            pltpu.VMEM((lines, GQ, PAGE, HD), jnp.bfloat16),
            pltpu.VMEM((lines, ROWS, HD), jnp.bfloat16),
            pltpu.VMEM((GQ, PAGE, BLOCK * PAGE), jnp.float32),
            pltpu.VMEM((GQ, PAGE, PAGE), jnp.float32),
            pltpu.VMEM((GQ, PAGE, 2 * HD), jnp.float32),
            pltpu.SMEM((lines,), jnp.int32),
            pltpu.SemaphoreType.DMA((lines, GQ)),
            pltpu.SemaphoreType.DMA((2, limit + 1)),
            pltpu.SemaphoreType.DMA((lines,)),
        ],
    )
    return pl.pallas_call(
        functools.partial(attend_kernel, lines, head, q_head),
        grid_spec=grid_spec,
        out_shape=jax.ShapeDtypeStruct((lines, ROWS, HD), jnp.bfloat16),
        compiler_params=pltpu.CompilerParams(vmem_limit_bytes=16 * 2**20),
        cost_estimate=pl.CostEstimate(flops=1, bytes_accessed=1, transcendentals=0),
    )(numbers, mine, *operands)


def store_kernel(slot, pool, incoming, out, sems):
    pages = pool.shape[0]

    def copy(page):
        return pltpu.make_async_copy(pool.at[page], out.at[page], sems.at[page])

    for page in range(pages):
        @pl.when(slot[0] != page)
        def _():
            copy(page).start()

        @pl.when(slot[0] == page)
        def _():
            pltpu.make_async_copy(incoming.at[0], out.at[page], sems.at[page]).start()

    for page in range(pages):
        copy(page).wait()


def store(slot, pool, incoming):
    grid_spec = pltpu.PrefetchScalarGridSpec(
        num_scalar_prefetch=1,
        grid=(),
        in_specs=[pl.BlockSpec(memory_space=pl.ANY)] * 2,
        out_specs=pl.BlockSpec(memory_space=pltpu.HBM),
        scratch_shapes=[pltpu.SemaphoreType.DMA((pool.shape[0],))],
    )
    return pl.pallas_call(
        store_kernel,
        grid_spec=grid_spec,
        out_shape=jax.ShapeDtypeStruct(pool.shape, pool.dtype),
        compiler_params=pltpu.CompilerParams(vmem_limit_bytes=16 * 2**20),
        cost_estimate=pl.CostEstimate(flops=1, bytes_accessed=1, transcendentals=0),
    )(slot, pool, incoming)


def merge_kernel(head, parts, *refs):
    lines = parts.shape[0]
    out, result, sem = refs[-3:]
    levels = []
    for i in range(lines):
        block = parts[i, GQ * PAGE:, :].astype(jnp.float32)
        levels.append(block[:8] + block[8:16] + block[16:24])
    top = functools.reduce(jnp.maximum, levels)
    weights = [jnp.exp(level - top) for level in levels]
    total = functools.reduce(jnp.add, weights)
    weights = [weight / total for weight in weights]
    filler = PAGE - lines * 8
    if filler:
        weights.append(jnp.zeros((filler, PAGE), jnp.float32))
    table = jnp.concatenate(weights, axis=0).T
    for h in range(GQ):
        merged = jnp.zeros((PAGE, HD), jnp.float32)
        for i in range(lines):
            column = i * 8 + h
            merged += table[:, column:column + 1] * parts[i, h * PAGE:(h + 1) * PAGE, :].astype(jnp.float32)
        result[:, h * HD:(h + 1) * HD] = merged.astype(jnp.bfloat16)
    copy = pltpu.make_async_copy(result, out.at[:, pl.ds(head * CHUNK, CHUNK)], sem)
    copy.start()
    copy.wait()


def merge(head, parts, whole):
    before = [] if whole is None else [whole]
    return pl.pallas_call(
        functools.partial(merge_kernel, head),
        in_specs=[pl.BlockSpec(memory_space=pltpu.VMEM)] + [pl.BlockSpec(memory_space=pl.ANY)] * len(before),
        out_specs=pl.BlockSpec(memory_space=pl.ANY),
        out_shape=jax.ShapeDtypeStruct((PAGE, KVH * CHUNK), jnp.bfloat16),
        scratch_shapes=[pltpu.VMEM((PAGE, CHUNK), jnp.bfloat16), pltpu.SemaphoreType.DMA],
        input_output_aliases={1: 0} if before else {},
        cost_estimate=pl.CostEstimate(flops=1, bytes_accessed=1, transcendentals=0),
    )(parts, *before)


def exchanged(array, groups):
    return lax.all_to_all(array, "serve", 0, 0, axis_index_groups=groups, tiled=True)


def after(array, *others):
    return lax.optimization_barrier((array, *others))[0]


def per_device(queries, new_kv, pool, page_owner, page_slot, prefix_len, store_slot):
    width = lax.axis_size("serve")
    lines = width // CLUSTER
    groups = [[c * CLUSTER + i for c in range(lines)] for i in range(CLUSTER)]
    me = lax.axis_index("serve")
    capacity = (MAXP + width - 2) // (width - 1)
    limit = min(MAXP, CLUSTER * capacity)
    pairs = [[first, first + 2] for first in range(width) if first % 4 < 2]
    used = (prefix_len + PAGE - 1) // PAGE
    numbers = jnp.concatenate([page_owner[0], page_slot[0], used, prefix_len - (used - 1) * PAGE])
    numbers = jnp.pad(numbers.astype(queries.dtype)[None], ((0, 15), (0, CHUNK - 2 * MAXP - 2)))
    early = jnp.concatenate([queries[:, :CHUNK], numbers], axis=0)
    early = exchanged(jnp.broadcast_to(early[None], (lines,) + early.shape), groups)
    later = after(queries, early)[None, :, CHUNK:]
    later = exchanged(jnp.broadcast_to(later, (lines, PAGE, (KVH - 1) * CHUNK)), groups)
    numbers = early[:, PAGE, :2 * MAXP + 2].astype(jnp.int32)
    mine = jnp.stack([me // CLUSTER, me % 2])
    incoming = shifted(new_kv[0], "serve", 1)
    owns = [pool[:, :, :, :HD]]
    rest = after(pool, owns[0])
    owns += [rest[:, :, :, g * HD:(g + 1) * HD] for g in range(1, KVH)]
    gathered = [lax.all_gather(own, "serve", axis_index_groups=pairs) for own in owns]
    fresh = new_kv[0, 0]
    attended = None
    parts = None
    for g in range(KVH):
        pair = gathered[g] if g == 0 else after(gathered[g], parts)
        other = swapped(pair, "serve", 1)
        q_all, q_head = (early, 0) if g == 0 else (later, g - 1)
        parts = attend(g, q_head, limit, numbers, mine, q_all, pair, other, fresh)
        attended = merge(g, exchanged(parts, groups), attended)
    pool_out = store(store_slot[0], pool, after(incoming, parts))
    return (attended, pool_out)


def solution(mesh):
    return jax.shard_map(
        per_device,
        mesh=mesh,
        in_specs=(
            P(("groups", "serve"), None),
            P(("groups", "serve"), None, None, None, None),
            P(("groups", "serve"), None, None, None),
            P(("groups", "serve"), None),
            P(("groups", "serve"), None),
            P(("groups", "serve")),
            P(("groups", "serve"), None),
        ),
        out_specs=(P(("groups", "serve"), None), P(("groups", "serve"), None, None, None)),
        check_vma=False,
    )
```

```python
import functools

import jax
import jax.numpy as jnp
from jax import lax
from jax.experimental import pallas as pl
from jax.experimental.pallas import tpu as pltpu
from jax.sharding import PartitionSpec as P

PAGE = 128
KVH = 4
GQ = 5
HD = 128
MAXP = 48
SCALE = HD ** (-0.5)
LOG2E = 1.4426950408889634
LOW = -1e30
CLUSTER = 4
BLOCK = 4
STAT = 32
HEADS = ((0, 1, 2), (3, 4))
ROWS = GQ * PAGE + STAT
CHUNK = GQ * HD
CONTRACT_LAST = (((1,), (1,)), ((), ()))


def swapped(array, axis, bit):
    size = lax.axis_size(axis)
    return lax.ppermute(array, axis, [(i, i ^ bit) for i in range(size)])


def shifted(array, axis, by):
    size = lax.axis_size(axis)
    return lax.ppermute(array, axis, [(i, (i + by) % size) for i in range(size)])


def attend_kernel(lines, head, q_head, limit, numbers, mine, *refs):
    q_all, own, twin, side, both, fresh, out = refs[:7]
    pages, queries, results, scores, tops, acc, q_sems, page_sems, out_sems = refs[7:]
    slots = own.shape[0]
    columns = pl.ds(head * HD, HD)
    extra = pages.shape[1] - 1

    def number(request, place):
        return numbers[request, mine[0] * (limit + 2) + place]

    def count_of(t):
        return number(request_of(t), limit)

    def request_of(t):
        return lax.rem(mine[0] - t + lines, lines)

    def q_copy(t, h):
        origin = q_all.at[request_of(t), pl.ds(0, PAGE), pl.ds((q_head * GQ + h) * HD, HD)]
        return pltpu.make_async_copy(origin, queries.at[t, h], q_sems.at[t, h])

    def out_copy(t):
        return pltpu.make_async_copy(results.at[t], out.at[request_of(t)], out_sems.at[t])

    def page_copy(source, slot, buffer, place):
        if source.shape[-1] == HD:
            origin = source.at[slot]
        else:
            origin = source.at[slot, :, :, columns]
        return pltpu.make_async_copy(origin, pages.at[buffer, place], page_sems.at[buffer, place])

    def fetch(t):
        request = request_of(t)
        buffer = lax.rem(t, 2)

        @pl.loop(0, count_of(t))
        def _(place):
            code = number(request, place)
            rank = lax.div(code, slots)
            slot = lax.rem(code, slots)
            for index, source in enumerate((own, twin, side, both)):
                @pl.when(rank == index)
                def _():
                    page_copy(source, slot, buffer, place).start()

    def arrive(t):
        buffer = lax.rem(t, 2)

        @pl.loop(0, count_of(t))
        def _(place):
            page_copy(own, 0, buffer, place).wait()

    fresh_copy = pltpu.make_async_copy(fresh.at[:, :, columns], pages.at[0, extra], page_sems.at[0, extra])
    for t in range(lines):
        for h in range(GQ):
            q_copy(t, h).start()
    for buffer in range(2):
        pages[buffer, :extra] = jnp.zeros((extra,) + pages.shape[2:], pages.dtype)
    fresh_copy.start()
    fetch(0)
    if lines > 1:
        fetch(1)
    def soften(heads, scored, values):
        factor = SCALE * LOG2E
        expos = []
        fades = []
        for h in heads:
            s = scored(h)
            old = tops[h]
            new = jnp.maximum(old, jnp.max(s, axis=1, keepdims=True))
            tops[h] = new
            fades.append(jnp.exp2((old - new) * factor))
            wide = jnp.concatenate([new] * (s.shape[1] // PAGE), axis=1)
            expos.append(jnp.exp2((s - wide) * factor).astype(jnp.bfloat16))
        added = jnp.dot(jnp.concatenate(expos, axis=0), values, preferred_element_type=jnp.float32)
        for i, h in enumerate(heads):
            fade = fades[i]
            acc[h] = acc[h] * jnp.concatenate([fade, fade], axis=1) + added[i * PAGE:(i + 1) * PAGE]

    def with_ones(values):
        return jnp.concatenate([values, jnp.ones_like(values)], axis=1)

    def score(t, heads, keys):
        query = queries[t, heads[0]:heads[-1] + 1].reshape(len(heads) * PAGE, HD)
        s = lax.dot_general(query, keys, CONTRACT_LAST, preferred_element_type=jnp.float32)
        return s.reshape(len(heads), PAGE, keys.shape[0])

    def keys_of(t, index):
        return pages[lax.rem(t, 2), pl.ds(index * BLOCK, BLOCK), 0].reshape(BLOCK * PAGE, HD)

    def values_of(t, index):
        return with_ones(pages[lax.rem(t, 2), pl.ds(index * BLOCK, BLOCK), 1].reshape(BLOCK * PAGE, HD))

    def blocks_of(t):
        return jnp.maximum(lax.div(count_of(t) + BLOCK - 1, BLOCK), 1)

    def reset():
        tops[...] = jnp.full(tops.shape, LOW, jnp.float32)
        acc[...] = jnp.zeros(acc.shape, jnp.float32)

    def finish(t):
        some = (count_of(t) > 0) | (t == 0)
        lane = lax.broadcasted_iota(jnp.int32, (PAGE, PAGE), 1)
        sums = jnp.ones((PAGE, PAGE), jnp.float32)
        heights = jnp.zeros((PAGE, PAGE), jnp.float32)
        for h in range(GQ):
            total = acc[h, :, HD:]
            results[t, h * PAGE:(h + 1) * PAGE, :] = (acc[h, :, :HD] * (1.0 / total)).astype(jnp.bfloat16)
            sums = jnp.where(lane == h, total, sums)
            heights = jnp.where(lane == h, tops[h], heights)
        level = heights.T[:8] * SCALE + jnp.log(sums.T[:8])
        level = jnp.where(some, level, LOW)
        high = level.astype(jnp.bfloat16).astype(jnp.float32)
        middle = (level - high).astype(jnp.bfloat16).astype(jnp.float32)
        low = level - high - middle
        stat = jnp.concatenate([high, middle, low, jnp.zeros_like(low)], axis=0)
        results[t, GQ * PAGE:, :] = stat.astype(jnp.bfloat16)
        out_copy(t).start()

    for t in range(lines):
        for h in range(GQ):
            q_copy(t, h).wait()
    fresh_copy.wait()
    reset()
    span_values = with_ones(pages[0, extra, 1])
    seen = lax.broadcasted_iota(jnp.int32, (PAGE, PAGE), 1) <= lax.broadcasted_iota(jnp.int32, (PAGE, PAGE), 0)
    for heads in HEADS:
        s = score(0, heads, pages[0, extra, 0])
        soften(heads, lambda h: jnp.where(seen, s[h - heads[0]], LOW), span_values)
    arrive(0)
    first = keys_of(0, 0)
    for heads in HEADS:
        scores[heads[0]:heads[-1] + 1] = score(0, heads, first)

    def step(_, carry):
        t, index = carry
        request = request_of(t)
        ends = index + 1 >= blocks_of(t)
        later_t = jnp.where(ends, t + 1, t)
        later_index = jnp.where(ends, 0, index + 1)
        ahead_t = jnp.minimum(later_t, lines - 1)

        @pl.when(ends & (t + 1 < lines))
        def _():
            arrive(t + 1)

        seen_here = (count_of(t) - 1 - index * BLOCK) * PAGE + number(request, limit + 1)
        column = lax.broadcasted_iota(jnp.int32, (PAGE, BLOCK * PAGE), 1)
        values = values_of(t, index)
        keys = keys_of(ahead_t, later_index)
        for heads in HEADS:
            soften(heads, lambda h: jnp.where(column < seen_here, scores[h], LOW), values)
            scores[heads[0]:heads[-1] + 1] = score(ahead_t, heads, keys)

        @pl.when(ends)
        def _():
            finish(t)
            reset()

            @pl.when(t + 2 < lines)
            def _():
                fetch(t + 2)

        return later_t, later_index

    steps = blocks_of(0)
    for t in range(1, lines):
        steps += blocks_of(t)
    lax.fori_loop(0, steps, step, (jnp.int32(0), jnp.int32(0)))
    for t in range(lines):
        out_copy(t).wait()


def attend(head, q_head, limit, numbers, mine, q_all, pools, fresh):
    lines = q_all.shape[0]
    operands = [q_all, *pools, fresh]
    grid_spec = pltpu.PrefetchScalarGridSpec(
        num_scalar_prefetch=2,
        grid=(),
        in_specs=[pl.BlockSpec(memory_space=pl.ANY)] * len(operands),
        out_specs=pl.BlockSpec(memory_space=pltpu.HBM),
        scratch_shapes=[
            pltpu.VMEM((2, limit + 1, 2, PAGE, HD), jnp.bfloat16),
            pltpu.VMEM((lines, GQ, PAGE, HD), jnp.bfloat16),
            pltpu.VMEM((lines, ROWS, HD), jnp.bfloat16),
            pltpu.VMEM((GQ, PAGE, BLOCK * PAGE), jnp.float32),
            pltpu.VMEM((GQ, PAGE, PAGE), jnp.float32),
            pltpu.VMEM((GQ, PAGE, 2 * HD), jnp.float32),
            pltpu.SemaphoreType.DMA((lines, GQ)),
            pltpu.SemaphoreType.DMA((2, limit + 1)),
            pltpu.SemaphoreType.DMA((lines,)),
        ],
    )
    return pl.pallas_call(
        functools.partial(attend_kernel, lines, head, q_head, limit),
        grid_spec=grid_spec,
        out_shape=jax.ShapeDtypeStruct((lines, ROWS, HD), jnp.bfloat16),
        compiler_params=pltpu.CompilerParams(vmem_limit_bytes=16 * 2**20),
        cost_estimate=pl.CostEstimate(flops=1, bytes_accessed=1, transcendentals=0),
    )(numbers, mine, *operands)


def store_kernel(slot, pool, incoming, out, sems):
    pages = pool.shape[0]

    def copy(page):
        return pltpu.make_async_copy(pool.at[page], out.at[page], sems.at[page])

    for page in range(pages):
        @pl.when(slot[0] != page)
        def _():
            copy(page).start()

        @pl.when(slot[0] == page)
        def _():
            pltpu.make_async_copy(incoming.at[0], out.at[page], sems.at[page]).start()

    for page in range(pages):
        copy(page).wait()


def store(slot, pool, incoming):
    grid_spec = pltpu.PrefetchScalarGridSpec(
        num_scalar_prefetch=1,
        grid=(),
        in_specs=[pl.BlockSpec(memory_space=pl.ANY)] * 2,
        out_specs=pl.BlockSpec(memory_space=pltpu.HBM),
        scratch_shapes=[pltpu.SemaphoreType.DMA((pool.shape[0],))],
    )
    return pl.pallas_call(
        store_kernel,
        grid_spec=grid_spec,
        out_shape=jax.ShapeDtypeStruct(pool.shape, pool.dtype),
        compiler_params=pltpu.CompilerParams(vmem_limit_bytes=60 * 2**20),
        cost_estimate=pl.CostEstimate(flops=1, bytes_accessed=1, transcendentals=0),
    )(slot, pool, incoming)


def merge_kernel(head, parts, *refs):
    lines = parts.shape[0]
    out, result, sem = refs[-3:]
    levels = []
    for i in range(lines):
        block = parts[i, GQ * PAGE:, :].astype(jnp.float32)
        levels.append(block[:8] + block[8:16] + block[16:24])
    top = functools.reduce(jnp.maximum, levels)
    weights = [jnp.exp(level - top) for level in levels]
    total = functools.reduce(jnp.add, weights)
    weights = [weight / total for weight in weights]
    filler = PAGE - lines * 8
    if filler:
        weights.append(jnp.zeros((filler, PAGE), jnp.float32))
    table = jnp.concatenate(weights, axis=0).T
    for h in range(GQ):
        merged = jnp.zeros((PAGE, HD), jnp.float32)
        for i in range(lines):
            column = i * 8 + h
            merged += table[:, column:column + 1] * parts[i, h * PAGE:(h + 1) * PAGE, :].astype(jnp.float32)
        result[:, h * HD:(h + 1) * HD] = merged.astype(jnp.bfloat16)
    copy = pltpu.make_async_copy(result, out.at[:, pl.ds(head * CHUNK, CHUNK)], sem)
    copy.start()
    copy.wait()


def merge(head, parts, whole):
    before = [] if whole is None else [whole]
    return pl.pallas_call(
        functools.partial(merge_kernel, head),
        in_specs=[pl.BlockSpec(memory_space=pltpu.VMEM)] + [pl.BlockSpec(memory_space=pl.ANY)] * len(before),
        out_specs=pl.BlockSpec(memory_space=pl.ANY),
        out_shape=jax.ShapeDtypeStruct((PAGE, KVH * CHUNK), jnp.bfloat16),
        scratch_shapes=[pltpu.VMEM((PAGE, CHUNK), jnp.bfloat16), pltpu.SemaphoreType.DMA],
        input_output_aliases={1: 0} if before else {},
        cost_estimate=pl.CostEstimate(flops=1, bytes_accessed=1, transcendentals=0),
    )(parts, *before)


def lists_kernel(lines, limit, slots, owners, places, length, mine, out):
    step = limit + 2
    used = lax.div(length[0] + PAGE - 1, PAGE)

    @pl.loop(0, PAGE)
    def _(i):
        out[0, i] = 0

    for d in range(lines):
        out[0, d * step + limit + 1] = PAGE

    @pl.loop(0, used)
    def _(j):
        owner = owners[0, j]
        base = lax.div(owner, CLUSTER) * step
        place = out[0, base + limit]
        rank = lax.rem(owner, CLUSTER) ^ mine[1]
        out[0, base + place] = rank * slots + places[0, j]
        out[0, base + limit] = place + 1

    final = lax.div(owners[0, used - 1], CLUSTER) * step
    out[0, final + limit + 1] = length[0] - (used - 1) * PAGE


def page_lists(lines, limit, slots, page_owner, page_slot, prefix_len, mine):
    smem = pl.BlockSpec(memory_space=pltpu.SMEM)
    return pl.pallas_call(
        functools.partial(lists_kernel, lines, limit, slots),
        in_specs=[smem] * 4,
        out_specs=smem,
        out_shape=jax.ShapeDtypeStruct((1, PAGE), jnp.int32),
    )(page_owner, page_slot, prefix_len, mine)


def exchanged(array, groups):
    return lax.all_to_all(array, "serve", 0, 0, axis_index_groups=groups, tiled=True)


def after(array, *others):
    return lax.optimization_barrier((array, *others))[0]


def per_device(queries, new_kv, pool, page_owner, page_slot, prefix_len, store_slot):
    width = lax.axis_size("serve")
    lines = width // CLUSTER
    groups = [[c * CLUSTER + i for c in range(lines)] for i in range(CLUSTER)]
    me = lax.axis_index("serve")
    slots = pool.shape[0]
    capacity = (MAXP + width - 2) // (width - 1)
    limit = min(MAXP, CLUSTER * capacity)
    owns = [pool[:, :, :, :HD]]
    rest = after(pool, owns[0])
    owns += [rest[:, :, :, g * HD:(g + 1) * HD] for g in range(1, KVH)]
    sides = [swapped(own, "serve", 2) for own in owns]
    twin = swapped(rest, "serve", 1)
    incoming = shifted(new_kv[0], "serve", 1)
    mine = jnp.stack([me // CLUSTER, me % CLUSTER]).astype(jnp.int32)
    numbers = page_lists(lines, limit, slots, page_owner, page_slot, prefix_len, mine)
    numbers = jnp.pad(numbers.astype(queries.dtype), ((0, PAGE - 1), (0, 0)))
    half = KVH // 2
    early = jnp.concatenate([after(queries, owns[1])[:, :half * CHUNK], numbers], axis=1)
    later = after(queries, early)[:, half * CHUNK:]
    early = lax.all_gather(early, "serve", axis_index_groups=groups)
    later = lax.all_gather(later, "serve", axis_index_groups=groups)
    numbers = early[:, 0, half * CHUNK:].astype(jnp.int32)
    fresh = new_kv[0, 0]
    attended = None
    done = None
    arrived = []
    parts = None
    for g in range(KVH):
        side = sides[g]
        if g > 0:
            side = after(side, parts, *([incoming] if g == 1 else [done]))
        both = swapped(side, "serve", 1)
        q_all, q_head = (early, g) if g < half else (later, g - half)
        parts = attend(g, q_head, limit, numbers, mine, q_all, (owns[g], twin, side, both), fresh)
        if arrived:
            attended = done = merge(g - 1, arrived.pop(), attended)
        arrived.append(exchanged(parts, groups))
    attended = merge(KVH - 1, arrived.pop(), attended)
    pool_out = store(store_slot[0], pool, after(incoming, parts))
    return (attended, pool_out)


def solution(mesh):
    return jax.shard_map(
        per_device,
        mesh=mesh,
        in_specs=(
            P(("groups", "serve"), None),
            P(("groups", "serve"), None, None, None, None),
            P(("groups", "serve"), None, None, None),
            P(("groups", "serve"), None),
            P(("groups", "serve"), None),
            P(("groups", "serve")),
            P(("groups", "serve"), None),
        ),
        out_specs=(P(("groups", "serve"), None), P(("groups", "serve"), None, None, None)),
        check_vma=False,
    )
```

```python
import functools

import jax
import jax.numpy as jnp
from jax import lax
from jax.experimental import pallas as pl
from jax.experimental.pallas import tpu as pltpu
from jax.sharding import PartitionSpec as P

PAGE = 128
KVH = 4
GQ = 5
HD = 128
MAXP = 48
SCALE = HD ** (-0.5)
LOG2E = 1.4426950408889634
LOW = -1e30
CLUSTER = 4
BLOCK = 4
STAT = 32
HEADS = ((0, 1, 2), (3, 4))
ROWS = GQ * PAGE + STAT
CHUNK = GQ * HD
CONTRACT_LAST = (((1,), (1,)), ((), ()))


def swapped(array, axis, bit):
    size = lax.axis_size(axis)
    return lax.ppermute(array, axis, [(i, i ^ bit) for i in range(size)])


def shifted(array, axis, by):
    size = lax.axis_size(axis)
    return lax.ppermute(array, axis, [(i, (i + by) % size) for i in range(size)])


def attend_kernel(lines, head, q_head, picks, counts, lasts, mine, store, *refs):
    q_all, own, twin, side, both, fresh = refs[:6]
    stores = len(refs) == 20
    if stores:
        pool, incoming, out, pool_out = refs[6:10]
        store_sems = refs[-1]
        scratch = refs[10:-1]
    else:
        out = refs[6]
        scratch = refs[7:]
    pages, queries, results, scores, tops, acc, q_sems, page_sems, out_sems = scratch
    slots = own.shape[0]
    columns = pl.ds(head * HD, HD)
    extra = pages.shape[1] - 1

    def request_of(t):
        return lax.rem(mine[0] - t + lines, lines)

    def q_copy(t, h):
        origin = q_all.at[request_of(t), pl.ds(0, PAGE), pl.ds((q_head * GQ + h) * HD, HD)]
        return pltpu.make_async_copy(origin, queries.at[t, h], q_sems.at[t, h])

    def out_copy(t):
        return pltpu.make_async_copy(results.at[t], out.at[request_of(t)], out_sems.at[t])

    def page_copy(source, slot, buffer, place):
        if source.shape[-1] == HD:
            origin = source.at[slot]
        else:
            origin = source.at[slot, :, :, columns]
        return pltpu.make_async_copy(origin, pages.at[buffer, place], page_sems.at[buffer, place])

    def fetch(t):
        request = request_of(t)
        buffer = lax.rem(t, 2)

        @pl.loop(0, counts[request])
        def _(place):
            code = picks[request, place]
            rank = lax.div(code, slots)
            slot = lax.rem(code, slots)
            for index, source in enumerate((own, twin, side, both)):
                @pl.when(rank == index)
                def _():
                    page_copy(source, slot, buffer, place).start()

    def arrive(t):
        buffer = lax.rem(t, 2)

        @pl.loop(0, counts[request_of(t)])
        def _(place):
            page_copy(own, 0, buffer, place).wait()

    def store_copy(slot):
        return pltpu.make_async_copy(pool.at[slot], pool_out.at[slot], store_sems.at[slot])

    fresh_copy = pltpu.make_async_copy(fresh.at[:, :, columns], pages.at[0, extra], page_sems.at[0, extra])
    for t in range(lines):
        for h in range(GQ):
            q_copy(t, h).start()
    for buffer in range(2):
        pages[buffer, :extra] = jnp.zeros((extra,) + pages.shape[2:], pages.dtype)
    fresh_copy.start()
    fetch(0)
    if lines > 1:
        fetch(1)
    if stores:
        @pl.loop(0, pool.shape[0])
        def _(slot):
            @pl.when(slot != store[0])
            def _():
                store_copy(slot).start()

        pltpu.make_async_copy(incoming.at[0], pool_out.at[store[0]], store_sems.at[store[0]]).start()

    def soften(heads, scored, values):
        factor = SCALE * LOG2E
        expos = []
        fades = []
        for h in heads:
            s = scored(h)
            old = tops[h]
            new = jnp.maximum(old, jnp.max(s, axis=1, keepdims=True))
            tops[h] = new
            fades.append(jnp.exp2((old - new) * factor))
            wide = jnp.concatenate([new] * (s.shape[1] // PAGE), axis=1)
            expos.append(jnp.exp2((s - wide) * factor).astype(jnp.bfloat16))
        added = jnp.dot(jnp.concatenate(expos, axis=0), values, preferred_element_type=jnp.float32)
        for i, h in enumerate(heads):
            fade = fades[i]
            acc[h] = acc[h] * jnp.concatenate([fade, fade], axis=1) + added[i * PAGE:(i + 1) * PAGE]

    def with_ones(values):
        return jnp.concatenate([values, jnp.ones_like(values)], axis=1)

    def score(t, heads, keys):
        query = queries[t, heads[0]:heads[-1] + 1].reshape(len(heads) * PAGE, HD)
        s = lax.dot_general(query, keys, CONTRACT_LAST, preferred_element_type=jnp.float32)
        return s.reshape(len(heads), PAGE, keys.shape[0])

    def keys_of(t, index):
        return pages[lax.rem(t, 2), pl.ds(index * BLOCK, BLOCK), 0].reshape(BLOCK * PAGE, HD)

    def values_of(t, index):
        return with_ones(pages[lax.rem(t, 2), pl.ds(index * BLOCK, BLOCK), 1].reshape(BLOCK * PAGE, HD))

    def blocks_of(t):
        return jnp.maximum(lax.div(counts[request_of(t)] + BLOCK - 1, BLOCK), 1)

    def reset():
        tops[...] = jnp.full(tops.shape, LOW, jnp.float32)
        acc[...] = jnp.zeros(acc.shape, jnp.float32)

    def finish(t):
        some = (counts[request_of(t)] > 0) | (t == 0)
        lane = lax.broadcasted_iota(jnp.int32, (PAGE, PAGE), 1)
        sums = jnp.ones((PAGE, PAGE), jnp.float32)
        heights = jnp.zeros((PAGE, PAGE), jnp.float32)
        for h in range(GQ):
            total = acc[h, :, HD:]
            results[t, h * PAGE:(h + 1) * PAGE, :] = (acc[h, :, :HD] * (1.0 / total)).astype(jnp.bfloat16)
            sums = jnp.where(lane == h, total, sums)
            heights = jnp.where(lane == h, tops[h], heights)
        level = heights.T[:8] * SCALE + jnp.log(sums.T[:8])
        level = jnp.where(some, level, LOW)
        high = level.astype(jnp.bfloat16).astype(jnp.float32)
        middle = (level - high).astype(jnp.bfloat16).astype(jnp.float32)
        low = level - high - middle
        stat = jnp.concatenate([high, middle, low, jnp.zeros_like(low)], axis=0)
        results[t, GQ * PAGE:, :] = stat.astype(jnp.bfloat16)
        out_copy(t).start()

    for t in range(lines):
        for h in range(GQ):
            q_copy(t, h).wait()
    fresh_copy.wait()
    reset()
    span_values = with_ones(pages[0, extra, 1])
    seen = lax.broadcasted_iota(jnp.int32, (PAGE, PAGE), 1) <= lax.broadcasted_iota(jnp.int32, (PAGE, PAGE), 0)
    for heads in HEADS:
        s = score(0, heads, pages[0, extra, 0])
        soften(heads, lambda h: jnp.where(seen, s[h - heads[0]], LOW), span_values)
    arrive(0)
    first = keys_of(0, 0)
    for heads in HEADS:
        scores[heads[0]:heads[-1] + 1] = score(0, heads, first)

    def step(_, carry):
        t, index = carry
        request = request_of(t)
        ends = index + 1 >= blocks_of(t)
        later_t = jnp.where(ends, t + 1, t)
        later_index = jnp.where(ends, 0, index + 1)
        ahead_t = jnp.minimum(later_t, lines - 1)

        @pl.when(ends & (t + 1 < lines))
        def _():
            arrive(t + 1)

        limit = (counts[request] - 1 - index * BLOCK) * PAGE + lasts[request]
        column = lax.broadcasted_iota(jnp.int32, (PAGE, BLOCK * PAGE), 1)
        values = values_of(t, index)
        keys = keys_of(ahead_t, later_index)
        for heads in HEADS:
            soften(heads, lambda h: jnp.where(column < limit, scores[h], LOW), values)
            scores[heads[0]:heads[-1] + 1] = score(ahead_t, heads, keys)

        @pl.when(ends)
        def _():
            finish(t)
            reset()

            @pl.when(t + 2 < lines)
            def _():
                fetch(t + 2)

        return later_t, later_index

    steps = blocks_of(0)
    for t in range(1, lines):
        steps += blocks_of(t)
    lax.fori_loop(0, steps, step, (jnp.int32(0), jnp.int32(0)))
    for t in range(lines):
        out_copy(t).wait()
    if stores:
        @pl.loop(0, pool.shape[0])
        def _(slot):
            store_copy(slot).wait()


def attend(head, q_head, tables, q_all, pools, fresh, pool=None, incoming=None):
    picks, counts, lasts, mine, store = tables
    lines = q_all.shape[0]
    places = picks.shape[1]
    out_shape = [jax.ShapeDtypeStruct((lines, ROWS, HD), jnp.bfloat16)]
    scratch = [
        pltpu.VMEM((2, places + 1, 2, PAGE, HD), jnp.bfloat16),
        pltpu.VMEM((lines, GQ, PAGE, HD), jnp.bfloat16),
        pltpu.VMEM((lines, ROWS, HD), jnp.bfloat16),
        pltpu.VMEM((GQ, PAGE, BLOCK * PAGE), jnp.float32),
        pltpu.VMEM((GQ, PAGE, PAGE), jnp.float32),
        pltpu.VMEM((GQ, PAGE, 2 * HD), jnp.float32),
        pltpu.SemaphoreType.DMA((lines, GQ)),
        pltpu.SemaphoreType.DMA((2, places + 1)),
        pltpu.SemaphoreType.DMA((lines,)),
    ]
    operands = [q_all, *pools, fresh]
    if incoming is not None:
        operands += [pool, incoming]
        out_shape.append(jax.ShapeDtypeStruct(pool.shape, pool.dtype))
        scratch.append(pltpu.SemaphoreType.DMA((pool.shape[0],)))
    grid_spec = pltpu.PrefetchScalarGridSpec(
        num_scalar_prefetch=5,
        grid=(),
        in_specs=[pl.BlockSpec(memory_space=pl.ANY)] * len(operands),
        out_specs=[pl.BlockSpec(memory_space=pltpu.HBM)] * len(out_shape),
        scratch_shapes=scratch,
    )
    return pl.pallas_call(
        functools.partial(attend_kernel, lines, head, q_head),
        grid_spec=grid_spec,
        out_shape=out_shape,
        compiler_params=pltpu.CompilerParams(vmem_limit_bytes=16 * 2**20),
        cost_estimate=pl.CostEstimate(flops=1, bytes_accessed=1, transcendentals=0),
    )(picks, counts, lasts, mine, store, *operands)


def merge_kernel(head, parts, *refs):
    lines = parts.shape[0]
    out, result, sem = refs[-3:]
    levels = []
    for i in range(lines):
        block = parts[i, GQ * PAGE:, :].astype(jnp.float32)
        levels.append(block[:8] + block[8:16] + block[16:24])
    top = functools.reduce(jnp.maximum, levels)
    weights = [jnp.exp(level - top) for level in levels]
    total = functools.reduce(jnp.add, weights)
    weights = [weight / total for weight in weights]
    filler = PAGE - lines * 8
    if filler:
        weights.append(jnp.zeros((filler, PAGE), jnp.float32))
    table = jnp.concatenate(weights, axis=0).T
    for h in range(GQ):
        merged = jnp.zeros((PAGE, HD), jnp.float32)
        for i in range(lines):
            column = i * 8 + h
            merged += table[:, column:column + 1] * parts[i, h * PAGE:(h + 1) * PAGE, :].astype(jnp.float32)
        result[:, h * HD:(h + 1) * HD] = merged.astype(jnp.bfloat16)
    copy = pltpu.make_async_copy(result, out.at[:, pl.ds(head * CHUNK, CHUNK)], sem)
    copy.start()
    copy.wait()


def merge(head, parts, whole):
    before = [] if whole is None else [whole]
    return pl.pallas_call(
        functools.partial(merge_kernel, head),
        in_specs=[pl.BlockSpec(memory_space=pltpu.VMEM)] + [pl.BlockSpec(memory_space=pl.ANY)] * len(before),
        out_specs=pl.BlockSpec(memory_space=pl.ANY),
        out_shape=jax.ShapeDtypeStruct((PAGE, KVH * CHUNK), jnp.bfloat16),
        scratch_shapes=[pltpu.VMEM((PAGE, CHUNK), jnp.bfloat16), pltpu.SemaphoreType.DMA],
        input_output_aliases={1: 0} if before else {},
        cost_estimate=pl.CostEstimate(flops=1, bytes_accessed=1, transcendentals=0),
    )(parts, *before)


def page_rows(me, lines, limit, slots, page_owner, page_slot, prefix_len):
    owners = page_owner[0]
    length = prefix_len[0]
    used = (length + PAGE - 1) // PAGE
    spot = jnp.arange(MAXP)
    here = (spot < used)[None] & (owners[None] // CLUSTER == jnp.arange(lines)[:, None])
    before = jnp.sum(here[:, None, :] & (spot[None, None, :] < spot[None, :, None]), axis=2)
    local = ((owners % CLUSTER) ^ (me % CLUSTER)) * slots + page_slot[0]
    chosen = here[:, :, None] & (before[:, :, None] == jnp.arange(limit)[None, None, :])
    picks = jnp.sum(jnp.where(chosen, local[None, :, None], 0), axis=1)
    counts = jnp.sum(here, axis=1)
    tail = jnp.any(here & (spot == used - 1)[None], axis=1)
    lasts = jnp.where(tail, length - (used - 1) * PAGE, PAGE)
    return jnp.concatenate([picks, counts[:, None], lasts[:, None]], axis=1)


def exchanged(array, groups):
    return lax.all_to_all(array, "serve", 0, 0, axis_index_groups=groups, tiled=True)


def after(array, *others):
    return lax.optimization_barrier((array, *others))[0]


def per_device(queries, new_kv, pool, page_owner, page_slot, prefix_len, store_slot):
    width = lax.axis_size("serve")
    lines = width // CLUSTER
    groups = [[c * CLUSTER + i for c in range(lines)] for i in range(CLUSTER)]
    me = lax.axis_index("serve")
    slots = pool.shape[0]
    capacity = (MAXP + width - 2) // (width - 1)
    limit = min(MAXP, CLUSTER * capacity)
    owns = [pool[:, :, :, :HD]]
    rest = after(pool, owns[0])
    owns += [rest[:, :, :, g * HD:(g + 1) * HD] for g in range(1, KVH)]
    sides = [swapped(own, "serve", 2) for own in owns]
    twin = swapped(rest, "serve", 1)
    incoming = shifted(new_kv[0], "serve", 1)
    rows = page_rows(me, lines, limit, slots, page_owner, page_slot, prefix_len).astype(queries.dtype)
    rows = jnp.pad(rows[:, None], ((0, 0), (0, 15), (0, CHUNK - limit - 2)))
    early = after(queries, owns[1], twin)[:, :CHUNK]
    early = jnp.concatenate([jnp.broadcast_to(early[None], (lines, PAGE, CHUNK)), rows], axis=1)
    early = exchanged(early, groups)
    later = after(queries, sides[0], incoming)[None, :, CHUNK:]
    later = exchanged(jnp.broadcast_to(later, (lines, PAGE, (KVH - 1) * CHUNK)), groups)
    numbers = early[:, PAGE, :limit + 2].astype(jnp.int32)
    tables = (numbers[:, :limit], numbers[:, limit], numbers[:, limit + 1], (me // CLUSTER)[None], store_slot[0])
    fresh = new_kv[0, 0]
    attended = None
    parts = None
    for g in range(KVH):
        side = sides[g] if g == 0 else after(sides[g], parts)
        both = swapped(side, "serve", 1)
        pools = (owns[g], twin, side, both)
        if g == 0:
            parts, pool_out = attend(g, 0, tables, early, pools, fresh, pool, incoming)
        else:
            parts = attend(g, g - 1, tables, later, pools, fresh)[0]
        attended = merge(g, exchanged(parts, groups), attended)
    return (attended, pool_out)


def solution(mesh):
    return jax.shard_map(
        per_device,
        mesh=mesh,
        in_specs=(
            P(("groups", "serve"), None),
            P(("groups", "serve"), None, None, None, None),
            P(("groups", "serve"), None, None, None),
            P(("groups", "serve"), None),
            P(("groups", "serve"), None),
            P(("groups", "serve")),
            P(("groups", "serve"), None),
        ),
        out_specs=(P(("groups", "serve"), None), P(("groups", "serve"), None, None, None)),
        check_vma=False,
    )
```

```python
import functools

import jax
import jax.numpy as jnp
from jax import lax
from jax.experimental import pallas as pl
from jax.experimental.pallas import tpu as pltpu
from jax.sharding import PartitionSpec as P

PAGE = 128
KVH = 4
GQ = 5
HD = 128
MAXP = 48
SCALE = HD ** (-0.5)
LOG2E = 1.4426950408889634
LOW = -1e30
CLUSTER = 4
BLOCK = 4
STAT = 32
HEADS = ((0, 1, 2), (3, 4))
ROWS = GQ * PAGE + STAT
CHUNK = GQ * HD
CONTRACT_LAST = (((1,), (1,)), ((), ()))


def swapped(array, axis, bit):
    size = lax.axis_size(axis)
    return lax.ppermute(array, axis, [(i, i ^ bit) for i in range(size)])


def shifted(array, axis, by):
    size = lax.axis_size(axis)
    return lax.ppermute(array, axis, [(i, (i + by) % size) for i in range(size)])


def attend_kernel(lines, head, q_head, picks, counts, lasts, mine, store, *refs):
    q_all, own, twin, side, both, fresh = refs[:6]
    stores = len(refs) == 20
    if stores:
        pool, incoming, out, pool_out = refs[6:10]
        store_sems = refs[-1]
        scratch = refs[10:-1]
    else:
        out = refs[6]
        scratch = refs[7:]
    pages, queries, results, scores, tops, acc, q_sems, page_sems, out_sems = scratch
    slots = own.shape[0]
    columns = pl.ds(head * HD, HD)
    extra = pages.shape[1] - 1

    def request_of(t):
        return lax.rem(mine[0] - t + lines, lines)

    def q_copy(t, h):
        origin = q_all.at[request_of(t), pl.ds(0, PAGE), pl.ds((q_head * GQ + h) * HD, HD)]
        return pltpu.make_async_copy(origin, queries.at[t, h], q_sems.at[t, h])

    def out_copy(t):
        return pltpu.make_async_copy(results.at[t], out.at[request_of(t)], out_sems.at[t])

    def page_copy(source, slot, buffer, place):
        if source.shape[-1] == HD:
            origin = source.at[slot]
        else:
            origin = source.at[slot, :, :, columns]
        return pltpu.make_async_copy(origin, pages.at[buffer, place], page_sems.at[buffer, place])

    def fetch(t):
        request = request_of(t)
        buffer = lax.rem(t, 2)

        @pl.loop(0, counts[request])
        def _(place):
            code = picks[request, place]
            rank = lax.div(code, slots)
            slot = lax.rem(code, slots)
            for index, source in enumerate((own, twin, side, both)):
                @pl.when(rank == index)
                def _():
                    page_copy(source, slot, buffer, place).start()

    def arrive(t):
        buffer = lax.rem(t, 2)

        @pl.loop(0, counts[request_of(t)])
        def _(place):
            page_copy(own, 0, buffer, place).wait()

    def store_copy(slot):
        return pltpu.make_async_copy(pool.at[slot], pool_out.at[slot], store_sems.at[slot])

    fresh_copy = pltpu.make_async_copy(fresh.at[:, :, columns], pages.at[0, extra], page_sems.at[0, extra])
    for t in range(lines):
        for h in range(GQ):
            q_copy(t, h).start()
    for buffer in range(2):
        pages[buffer, :extra] = jnp.zeros((extra,) + pages.shape[2:], pages.dtype)
    fresh_copy.start()
    fetch(0)
    if lines > 1:
        fetch(1)
    if stores:
        @pl.loop(0, pool.shape[0])
        def _(slot):
            @pl.when(slot != store[0])
            def _():
                store_copy(slot).start()

        pltpu.make_async_copy(incoming.at[0], pool_out.at[store[0]], store_sems.at[store[0]]).start()

    def soften(heads, scored, values):
        factor = SCALE * LOG2E
        expos = []
        fades = []
        for h in heads:
            s = scored(h)
            old = tops[h]
            new = jnp.maximum(old, jnp.max(s, axis=1, keepdims=True))
            tops[h] = new
            fades.append(jnp.exp2((old - new) * factor))
            wide = jnp.concatenate([new] * (s.shape[1] // PAGE), axis=1)
            expos.append(jnp.exp2((s - wide) * factor).astype(jnp.bfloat16))
        added = jnp.dot(jnp.concatenate(expos, axis=0), values, preferred_element_type=jnp.float32)
        for i, h in enumerate(heads):
            fade = fades[i]
            acc[h] = acc[h] * jnp.concatenate([fade, fade], axis=1) + added[i * PAGE:(i + 1) * PAGE]

    def with_ones(values):
        return jnp.concatenate([values, jnp.ones_like(values)], axis=1)

    def score(t, heads, keys):
        query = queries[t, heads[0]:heads[-1] + 1].reshape(len(heads) * PAGE, HD)
        s = lax.dot_general(query, keys, CONTRACT_LAST, preferred_element_type=jnp.float32)
        return s.reshape(len(heads), PAGE, keys.shape[0])

    def keys_of(t, index):
        return pages[lax.rem(t, 2), pl.ds(index * BLOCK, BLOCK), 0].reshape(BLOCK * PAGE, HD)

    def values_of(t, index):
        return with_ones(pages[lax.rem(t, 2), pl.ds(index * BLOCK, BLOCK), 1].reshape(BLOCK * PAGE, HD))

    def blocks_of(t):
        return jnp.maximum(lax.div(counts[request_of(t)] + BLOCK - 1, BLOCK), 1)

    def reset():
        tops[...] = jnp.full(tops.shape, LOW, jnp.float32)
        acc[...] = jnp.zeros(acc.shape, jnp.float32)

    def finish(t):
        some = (counts[request_of(t)] > 0) | (t == 0)
        lane = lax.broadcasted_iota(jnp.int32, (PAGE, PAGE), 1)
        sums = jnp.ones((PAGE, PAGE), jnp.float32)
        heights = jnp.zeros((PAGE, PAGE), jnp.float32)
        for h in range(GQ):
            total = acc[h, :, HD:]
            results[t, h * PAGE:(h + 1) * PAGE, :] = (acc[h, :, :HD] * (1.0 / total)).astype(jnp.bfloat16)
            sums = jnp.where(lane == h, total, sums)
            heights = jnp.where(lane == h, tops[h], heights)
        level = heights.T[:8] * SCALE + jnp.log(sums.T[:8])
        level = jnp.where(some, level, LOW)
        high = level.astype(jnp.bfloat16).astype(jnp.float32)
        middle = (level - high).astype(jnp.bfloat16).astype(jnp.float32)
        low = level - high - middle
        stat = jnp.concatenate([high, middle, low, jnp.zeros_like(low)], axis=0)
        results[t, GQ * PAGE:, :] = stat.astype(jnp.bfloat16)
        out_copy(t).start()

    for t in range(lines):
        for h in range(GQ):
            q_copy(t, h).wait()
    fresh_copy.wait()
    reset()
    span_values = with_ones(pages[0, extra, 1])
    seen = lax.broadcasted_iota(jnp.int32, (PAGE, PAGE), 1) <= lax.broadcasted_iota(jnp.int32, (PAGE, PAGE), 0)
    for heads in HEADS:
        s = score(0, heads, pages[0, extra, 0])
        soften(heads, lambda h: jnp.where(seen, s[h - heads[0]], LOW), span_values)
    arrive(0)
    first = keys_of(0, 0)
    for heads in HEADS:
        scores[heads[0]:heads[-1] + 1] = score(0, heads, first)

    def step(_, carry):
        t, index = carry
        request = request_of(t)
        ends = index + 1 >= blocks_of(t)
        later_t = jnp.where(ends, t + 1, t)
        later_index = jnp.where(ends, 0, index + 1)
        ahead_t = jnp.minimum(later_t, lines - 1)

        @pl.when(ends & (t + 1 < lines))
        def _():
            arrive(t + 1)

        limit = (counts[request] - 1 - index * BLOCK) * PAGE + lasts[request]
        column = lax.broadcasted_iota(jnp.int32, (PAGE, BLOCK * PAGE), 1)
        values = values_of(t, index)
        keys = keys_of(ahead_t, later_index)
        for heads in HEADS:
            soften(heads, lambda h: jnp.where(column < limit, scores[h], LOW), values)
            scores[heads[0]:heads[-1] + 1] = score(ahead_t, heads, keys)

        @pl.when(ends)
        def _():
            finish(t)
            reset()

            @pl.when(t + 2 < lines)
            def _():
                fetch(t + 2)

        return later_t, later_index

    steps = blocks_of(0)
    for t in range(1, lines):
        steps += blocks_of(t)
    lax.fori_loop(0, steps, step, (jnp.int32(0), jnp.int32(0)))
    for t in range(lines):
        out_copy(t).wait()
    if stores:
        @pl.loop(0, pool.shape[0])
        def _(slot):
            store_copy(slot).wait()


def attend(head, q_head, tables, q_all, pools, fresh, pool=None, incoming=None):
    picks, counts, lasts, mine, store = tables
    lines = q_all.shape[0]
    places = picks.shape[1]
    out_shape = [jax.ShapeDtypeStruct((lines, ROWS, HD), jnp.bfloat16)]
    scratch = [
        pltpu.VMEM((2, places + 1, 2, PAGE, HD), jnp.bfloat16),
        pltpu.VMEM((lines, GQ, PAGE, HD), jnp.bfloat16),
        pltpu.VMEM((lines, ROWS, HD), jnp.bfloat16),
        pltpu.VMEM((GQ, PAGE, BLOCK * PAGE), jnp.float32),
        pltpu.VMEM((GQ, PAGE, PAGE), jnp.float32),
        pltpu.VMEM((GQ, PAGE, 2 * HD), jnp.float32),
        pltpu.SemaphoreType.DMA((lines, GQ)),
        pltpu.SemaphoreType.DMA((2, places + 1)),
        pltpu.SemaphoreType.DMA((lines,)),
    ]
    operands = [q_all, *pools, fresh]
    if incoming is not None:
        operands += [pool, incoming]
        out_shape.append(jax.ShapeDtypeStruct(pool.shape, pool.dtype))
        scratch.append(pltpu.SemaphoreType.DMA((pool.shape[0],)))
    grid_spec = pltpu.PrefetchScalarGridSpec(
        num_scalar_prefetch=5,
        grid=(),
        in_specs=[pl.BlockSpec(memory_space=pl.ANY)] * len(operands),
        out_specs=[pl.BlockSpec(memory_space=pltpu.HBM)] * len(out_shape),
        scratch_shapes=scratch,
    )
    return pl.pallas_call(
        functools.partial(attend_kernel, lines, head, q_head),
        grid_spec=grid_spec,
        out_shape=out_shape,
        compiler_params=pltpu.CompilerParams(vmem_limit_bytes=16 * 2**20),
        cost_estimate=pl.CostEstimate(flops=1, bytes_accessed=1, transcendentals=0),
    )(picks, counts, lasts, mine, store, *operands)


def merge_kernel(head, parts, *refs):
    lines = parts.shape[0]
    out, result, sem = refs[-3:]
    levels = []
    for i in range(lines):
        block = parts[i, GQ * PAGE:, :].astype(jnp.float32)
        levels.append(block[:8] + block[8:16] + block[16:24])
    top = functools.reduce(jnp.maximum, levels)
    weights = [jnp.exp(level - top) for level in levels]
    total = functools.reduce(jnp.add, weights)
    weights = [weight / total for weight in weights]
    filler = PAGE - lines * 8
    if filler:
        weights.append(jnp.zeros((filler, PAGE), jnp.float32))
    table = jnp.concatenate(weights, axis=0).T
    for h in range(GQ):
        merged = jnp.zeros((PAGE, HD), jnp.float32)
        for i in range(lines):
            column = i * 8 + h
            merged += table[:, column:column + 1] * parts[i, h * PAGE:(h + 1) * PAGE, :].astype(jnp.float32)
        result[:, h * HD:(h + 1) * HD] = merged.astype(jnp.bfloat16)
    copy = pltpu.make_async_copy(result, out.at[:, pl.ds(head * CHUNK, CHUNK)], sem)
    copy.start()
    copy.wait()


def merge(head, parts, whole):
    before = [] if whole is None else [whole]
    return pl.pallas_call(
        functools.partial(merge_kernel, head),
        in_specs=[pl.BlockSpec(memory_space=pltpu.VMEM)] + [pl.BlockSpec(memory_space=pl.ANY)] * len(before),
        out_specs=pl.BlockSpec(memory_space=pl.ANY),
        out_shape=jax.ShapeDtypeStruct((PAGE, KVH * CHUNK), jnp.bfloat16),
        scratch_shapes=[pltpu.VMEM((PAGE, CHUNK), jnp.bfloat16), pltpu.SemaphoreType.DMA],
        input_output_aliases={1: 0} if before else {},
        cost_estimate=pl.CostEstimate(flops=1, bytes_accessed=1, transcendentals=0),
    )(parts, *before)


def page_rows(me, lines, limit, slots, page_owner, page_slot, prefix_len):
    owners = page_owner[0]
    length = prefix_len[0]
    used = (length + PAGE - 1) // PAGE
    spot = jnp.arange(MAXP)
    here = (spot < used)[None] & (owners[None] // CLUSTER == jnp.arange(lines)[:, None])
    before = jnp.sum(here[:, None, :] & (spot[None, None, :] < spot[None, :, None]), axis=2)
    local = ((owners % CLUSTER) ^ (me % CLUSTER)) * slots + page_slot[0]
    chosen = here[:, :, None] & (before[:, :, None] == jnp.arange(limit)[None, None, :])
    picks = jnp.sum(jnp.where(chosen, local[None, :, None], 0), axis=1)
    counts = jnp.sum(here, axis=1)
    tail = jnp.any(here & (spot == used - 1)[None], axis=1)
    lasts = jnp.where(tail, length - (used - 1) * PAGE, PAGE)
    return jnp.concatenate([picks, counts[:, None], lasts[:, None]], axis=1)


def exchanged(array, groups):
    return lax.all_to_all(array, "serve", 0, 0, axis_index_groups=groups, tiled=True)


def after(array, *others):
    return lax.optimization_barrier((array, *others))[0]


def per_device(queries, new_kv, pool, page_owner, page_slot, prefix_len, store_slot):
    width = lax.axis_size("serve")
    lines = width // CLUSTER
    groups = [[c * CLUSTER + i for c in range(lines)] for i in range(CLUSTER)]
    me = lax.axis_index("serve")
    slots = pool.shape[0]
    capacity = (MAXP + width - 2) // (width - 1)
    limit = min(MAXP, CLUSTER * capacity)
    owns = [pool[:, :, :, :HD]]
    rest = after(pool, owns[0])
    owns += [rest[:, :, :, g * HD:(g + 1) * HD] for g in range(1, KVH)]
    sides = [swapped(own, "serve", 2) for own in owns]
    twin = swapped(rest, "serve", 1)
    incoming = shifted(new_kv[0], "serve", 1)
    rows = page_rows(me, lines, limit, slots, page_owner, page_slot, prefix_len).astype(queries.dtype)
    rows = jnp.pad(rows[:, None], ((0, 0), (0, PAGE - 1), (0, PAGE - limit - 2)))
    q_all = jnp.broadcast_to(queries[None], (lines, PAGE, KVH * CHUNK))
    q_all = exchanged(jnp.concatenate([q_all, rows], axis=2), groups)
    numbers = q_all[:, 0, KVH * CHUNK:KVH * CHUNK + limit + 2].astype(jnp.int32)
    tables = (numbers[:, :limit], numbers[:, limit], numbers[:, limit + 1], (me // CLUSTER)[None], store_slot[0])
    fresh = new_kv[0, 0]
    attended = None
    parts = []
    for g in range(KVH):
        side = sides[g]
        if g == 1:
            side = after(side, incoming)
        if g > 1:
            side = after(side, parts[g - 2])
        both = swapped(side, "serve", 1)
        pools = (owns[g], twin, side, both)
        if g == 0:
            part, pool_out = attend(g, g, tables, q_all, pools, fresh, pool, incoming)
        else:
            part = attend(g, g, tables, q_all, pools, fresh)[0]
        parts.append(part)
        attended = merge(g, exchanged(part, groups), attended)
    return (attended, pool_out)


def solution(mesh):
    return jax.shard_map(
        per_device,
        mesh=mesh,
        in_specs=(
            P(("groups", "serve"), None),
            P(("groups", "serve"), None, None, None, None),
            P(("groups", "serve"), None, None, None),
            P(("groups", "serve"), None),
            P(("groups", "serve"), None),
            P(("groups", "serve")),
            P(("groups", "serve"), None),
        ),
        out_specs=(P(("groups", "serve"), None), P(("groups", "serve"), None, None, None)),
        check_vma=False,
    )
```

```python
import functools

import jax
import jax.numpy as jnp
from jax import lax
from jax.experimental import pallas as pl
from jax.experimental.pallas import tpu as pltpu
from jax.sharding import PartitionSpec as P

PAGE = 128
KVH = 4
GQ = 5
HD = 128
MAXP = 48
SCALE = HD ** (-0.5)
LOG2E = 1.4426950408889634
LOW = -1e30
CLUSTER = 4
BLOCK = 4
STAT = 32
HEADS = ((0, 1, 2), (3, 4))
ROWS = GQ * PAGE + STAT
CHUNK = GQ * HD
CONTRACT_LAST = (((1,), (1,)), ((), ()))


def swapped(array, axis, bit):
    size = lax.axis_size(axis)
    return lax.ppermute(array, axis, [(i, i ^ bit) for i in range(size)])


def shifted(array, axis, by):
    size = lax.axis_size(axis)
    return lax.ppermute(array, axis, [(i, (i + by) % size) for i in range(size)])


def attend_kernel(lines, head, q_head, picks, counts, lasts, mine, store, *refs):
    q_all, own, twin, side, both, fresh = refs[:6]
    stores = len(refs) == 20
    if stores:
        pool, incoming, out, pool_out = refs[6:10]
        store_sems = refs[-1]
        scratch = refs[10:-1]
    else:
        out = refs[6]
        scratch = refs[7:]
    pages, queries, results, scores, tops, acc, q_sems, page_sems, out_sems = scratch
    slots = own.shape[0]
    columns = pl.ds(head * HD, HD)
    extra = pages.shape[1] - 1

    def request_of(t):
        return lax.rem(mine[0] - t + lines, lines)

    def q_copy(t, h):
        origin = q_all.at[request_of(t), pl.ds(0, PAGE), pl.ds((q_head * GQ + h) * HD, HD)]
        return pltpu.make_async_copy(origin, queries.at[t, h], q_sems.at[t, h])

    def out_copy(t):
        return pltpu.make_async_copy(results.at[t], out.at[request_of(t)], out_sems.at[t])

    def page_copy(source, slot, buffer, place):
        if source.shape[-1] == HD:
            origin = source.at[slot]
        else:
            origin = source.at[slot, :, :, columns]
        return pltpu.make_async_copy(origin, pages.at[buffer, place], page_sems.at[buffer, place])

    def fetch(t):
        request = request_of(t)
        buffer = lax.rem(t, 2)

        @pl.loop(0, counts[request])
        def _(place):
            code = picks[request, place]
            rank = lax.div(code, slots)
            slot = lax.rem(code, slots)
            for index, source in enumerate((own, twin, side, both)):
                @pl.when(rank == index)
                def _():
                    page_copy(source, slot, buffer, place).start()

    def arrive(t):
        buffer = lax.rem(t, 2)

        @pl.loop(0, counts[request_of(t)])
        def _(place):
            page_copy(own, 0, buffer, place).wait()

    def store_copy(slot):
        return pltpu.make_async_copy(pool.at[slot], pool_out.at[slot], store_sems.at[slot])

    fresh_copy = pltpu.make_async_copy(fresh.at[:, :, columns], pages.at[0, extra], page_sems.at[0, extra])
    for t in range(lines):
        for h in range(GQ):
            q_copy(t, h).start()
    for buffer in range(2):
        pages[buffer, :extra] = jnp.zeros((extra,) + pages.shape[2:], pages.dtype)
    fresh_copy.start()
    fetch(0)
    if lines > 1:
        fetch(1)
    if stores:
        @pl.loop(0, pool.shape[0])
        def _(slot):
            @pl.when(slot != store[0])
            def _():
                store_copy(slot).start()

        pltpu.make_async_copy(incoming.at[0], pool_out.at[store[0]], store_sems.at[store[0]]).start()

    def soften(heads, scored, values):
        factor = SCALE * LOG2E
        expos = []
        fades = []
        for h in heads:
            s = scored(h)
            old = tops[h]
            new = jnp.maximum(old, jnp.max(s, axis=1, keepdims=True))
            tops[h] = new
            fades.append(jnp.exp2((old - new) * factor))
            wide = jnp.concatenate([new] * (s.shape[1] // PAGE), axis=1)
            expos.append(jnp.exp2((s - wide) * factor).astype(jnp.bfloat16))
        added = jnp.dot(jnp.concatenate(expos, axis=0), values, preferred_element_type=jnp.float32)
        for i, h in enumerate(heads):
            fade = fades[i]
            acc[h] = acc[h] * jnp.concatenate([fade, fade], axis=1) + added[i * PAGE:(i + 1) * PAGE]

    def with_ones(values):
        return jnp.concatenate([values, jnp.ones_like(values)], axis=1)

    def score(t, heads, keys):
        query = queries[t, heads[0]:heads[-1] + 1].reshape(len(heads) * PAGE, HD)
        s = lax.dot_general(query, keys, CONTRACT_LAST, preferred_element_type=jnp.float32)
        return s.reshape(len(heads), PAGE, keys.shape[0])

    def keys_of(t, index):
        return pages[lax.rem(t, 2), pl.ds(index * BLOCK, BLOCK), 0].reshape(BLOCK * PAGE, HD)

    def values_of(t, index):
        return with_ones(pages[lax.rem(t, 2), pl.ds(index * BLOCK, BLOCK), 1].reshape(BLOCK * PAGE, HD))

    def blocks_of(t):
        return jnp.maximum(lax.div(counts[request_of(t)] + BLOCK - 1, BLOCK), 1)

    def reset():
        tops[...] = jnp.full(tops.shape, LOW, jnp.float32)
        acc[...] = jnp.zeros(acc.shape, jnp.float32)

    def finish(t):
        some = (counts[request_of(t)] > 0) | (t == 0)
        lane = lax.broadcasted_iota(jnp.int32, (PAGE, PAGE), 1)
        sums = jnp.ones((PAGE, PAGE), jnp.float32)
        heights = jnp.zeros((PAGE, PAGE), jnp.float32)
        for h in range(GQ):
            total = acc[h, :, HD:]
            results[t, h * PAGE:(h + 1) * PAGE, :] = (acc[h, :, :HD] * (1.0 / total)).astype(jnp.bfloat16)
            sums = jnp.where(lane == h, total, sums)
            heights = jnp.where(lane == h, tops[h], heights)
        level = heights.T[:8] * SCALE + jnp.log(sums.T[:8])
        level = jnp.where(some, level, LOW)
        high = level.astype(jnp.bfloat16).astype(jnp.float32)
        middle = (level - high).astype(jnp.bfloat16).astype(jnp.float32)
        low = level - high - middle
        stat = jnp.concatenate([high, middle, low, jnp.zeros_like(low)], axis=0)
        results[t, GQ * PAGE:, :] = stat.astype(jnp.bfloat16)
        out_copy(t).start()

    for t in range(lines):
        for h in range(GQ):
            q_copy(t, h).wait()
    fresh_copy.wait()
    reset()
    span_values = with_ones(pages[0, extra, 1])
    seen = lax.broadcasted_iota(jnp.int32, (PAGE, PAGE), 1) <= lax.broadcasted_iota(jnp.int32, (PAGE, PAGE), 0)
    for heads in HEADS:
        s = score(0, heads, pages[0, extra, 0])
        soften(heads, lambda h: jnp.where(seen, s[h - heads[0]], LOW), span_values)
    arrive(0)
    first = keys_of(0, 0)
    for heads in HEADS:
        scores[heads[0]:heads[-1] + 1] = score(0, heads, first)

    def step(_, carry):
        t, index = carry
        request = request_of(t)
        ends = index + 1 >= blocks_of(t)
        later_t = jnp.where(ends, t + 1, t)
        later_index = jnp.where(ends, 0, index + 1)
        ahead_t = jnp.minimum(later_t, lines - 1)

        @pl.when(ends & (t + 1 < lines))
        def _():
            arrive(t + 1)

        limit = (counts[request] - 1 - index * BLOCK) * PAGE + lasts[request]
        column = lax.broadcasted_iota(jnp.int32, (PAGE, BLOCK * PAGE), 1)
        values = values_of(t, index)
        keys = keys_of(ahead_t, later_index)
        for heads in HEADS:
            soften(heads, lambda h: jnp.where(column < limit, scores[h], LOW), values)
            scores[heads[0]:heads[-1] + 1] = score(ahead_t, heads, keys)

        @pl.when(ends)
        def _():
            finish(t)
            reset()

            @pl.when(t + 2 < lines)
            def _():
                fetch(t + 2)

        return later_t, later_index

    steps = blocks_of(0)
    for t in range(1, lines):
        steps += blocks_of(t)
    lax.fori_loop(0, steps, step, (jnp.int32(0), jnp.int32(0)))
    for t in range(lines):
        out_copy(t).wait()
    if stores:
        @pl.loop(0, pool.shape[0])
        def _(slot):
            store_copy(slot).wait()


def attend(head, q_head, tables, q_all, pools, fresh, pool=None, incoming=None):
    picks, counts, lasts, mine, store = tables
    lines = q_all.shape[0]
    places = picks.shape[1]
    out_shape = [jax.ShapeDtypeStruct((lines, ROWS, HD), jnp.bfloat16)]
    scratch = [
        pltpu.VMEM((2, places + 1, 2, PAGE, HD), jnp.bfloat16),
        pltpu.VMEM((lines, GQ, PAGE, HD), jnp.bfloat16),
        pltpu.VMEM((lines, ROWS, HD), jnp.bfloat16),
        pltpu.VMEM((GQ, PAGE, BLOCK * PAGE), jnp.float32),
        pltpu.VMEM((GQ, PAGE, PAGE), jnp.float32),
        pltpu.VMEM((GQ, PAGE, 2 * HD), jnp.float32),
        pltpu.SemaphoreType.DMA((lines, GQ)),
        pltpu.SemaphoreType.DMA((2, places + 1)),
        pltpu.SemaphoreType.DMA((lines,)),
    ]
    operands = [q_all, *pools, fresh]
    if incoming is not None:
        operands += [pool, incoming]
        out_shape.append(jax.ShapeDtypeStruct(pool.shape, pool.dtype))
        scratch.append(pltpu.SemaphoreType.DMA((pool.shape[0],)))
    grid_spec = pltpu.PrefetchScalarGridSpec(
        num_scalar_prefetch=5,
        grid=(),
        in_specs=[pl.BlockSpec(memory_space=pl.ANY)] * len(operands),
        out_specs=[pl.BlockSpec(memory_space=pltpu.HBM)] * len(out_shape),
        scratch_shapes=scratch,
    )
    return pl.pallas_call(
        functools.partial(attend_kernel, lines, head, q_head),
        grid_spec=grid_spec,
        out_shape=out_shape,
        compiler_params=pltpu.CompilerParams(vmem_limit_bytes=32 * 2**20),
        cost_estimate=pl.CostEstimate(flops=1, bytes_accessed=1, transcendentals=0),
    )(picks, counts, lasts, mine, store, *operands)


def merge_kernel(head, parts, *refs):
    lines = parts.shape[0]
    out, result, sem = refs[-3:]
    levels = []
    for i in range(lines):
        block = parts[i, GQ * PAGE:, :].astype(jnp.float32)
        levels.append(block[:8] + block[8:16] + block[16:24])
    top = functools.reduce(jnp.maximum, levels)
    weights = [jnp.exp(level - top) for level in levels]
    total = functools.reduce(jnp.add, weights)
    weights = [weight / total for weight in weights]
    filler = PAGE - lines * 8
    if filler:
        weights.append(jnp.zeros((filler, PAGE), jnp.float32))
    table = jnp.concatenate(weights, axis=0).T
    for h in range(GQ):
        merged = jnp.zeros((PAGE, HD), jnp.float32)
        for i in range(lines):
            column = i * 8 + h
            merged += table[:, column:column + 1] * parts[i, h * PAGE:(h + 1) * PAGE, :].astype(jnp.float32)
        result[:, h * HD:(h + 1) * HD] = merged.astype(jnp.bfloat16)
    copy = pltpu.make_async_copy(result, out.at[:, pl.ds(head * CHUNK, CHUNK)], sem)
    copy.start()
    copy.wait()


def merge(head, parts, whole):
    before = [] if whole is None else [whole]
    return pl.pallas_call(
        functools.partial(merge_kernel, head),
        in_specs=[pl.BlockSpec(memory_space=pltpu.VMEM)] + [pl.BlockSpec(memory_space=pl.ANY)] * len(before),
        out_specs=pl.BlockSpec(memory_space=pl.ANY),
        out_shape=jax.ShapeDtypeStruct((PAGE, KVH * CHUNK), jnp.bfloat16),
        scratch_shapes=[pltpu.VMEM((PAGE, CHUNK), jnp.bfloat16), pltpu.SemaphoreType.DMA],
        input_output_aliases={1: 0} if before else {},
        cost_estimate=pl.CostEstimate(flops=1, bytes_accessed=1, transcendentals=0),
    )(parts, *before)


def page_rows(me, lines, limit, slots, page_owner, page_slot, prefix_len):
    owners = page_owner[0]
    length = prefix_len[0]
    used = (length + PAGE - 1) // PAGE
    spot = jnp.arange(MAXP)
    here = (spot < used)[None] & (owners[None] // CLUSTER == jnp.arange(lines)[:, None])
    before = jnp.sum(here[:, None, :] & (spot[None, None, :] < spot[None, :, None]), axis=2)
    local = ((owners % CLUSTER) ^ (me % CLUSTER)) * slots + page_slot[0]
    chosen = here[:, :, None] & (before[:, :, None] == jnp.arange(limit)[None, None, :])
    picks = jnp.sum(jnp.where(chosen, local[None, :, None], 0), axis=1)
    counts = jnp.sum(here, axis=1)
    tail = jnp.any(here & (spot == used - 1)[None], axis=1)
    lasts = jnp.where(tail, length - (used - 1) * PAGE, PAGE)
    return jnp.concatenate([picks, counts[:, None], lasts[:, None]], axis=1)


def exchanged(array, groups):
    return lax.all_to_all(array, "serve", 0, 0, axis_index_groups=groups, tiled=True)


def after(array, *others):
    return lax.optimization_barrier((array, *others))[0]


def per_device(queries, new_kv, pool, page_owner, page_slot, prefix_len, store_slot):
    width = lax.axis_size("serve")
    lines = width // CLUSTER
    groups = [[c * CLUSTER + i for c in range(lines)] for i in range(CLUSTER)]
    me = lax.axis_index("serve")
    slots = pool.shape[0]
    capacity = (MAXP + width - 2) // (width - 1)
    limit = min(MAXP, CLUSTER * capacity)
    incoming = shifted(new_kv[0], "serve", 1)
    owns = [after(pool, incoming)[:, :, :, :HD]]
    rest = after(pool, owns[0])
    owns += [rest[:, :, :, g * HD:(g + 1) * HD] for g in range(1, KVH)]
    sides = [swapped(own, "serve", 2) for own in owns]
    twin = swapped(rest, "serve", 1)
    rows = page_rows(me, lines, limit, slots, page_owner, page_slot, prefix_len).astype(queries.dtype)
    rows = jnp.pad(rows[:, None], ((0, 0), (0, PAGE - 1), (0, PAGE - limit - 2)))
    early = jnp.broadcast_to(queries[None, :, :CHUNK], (lines, PAGE, CHUNK))
    early = exchanged(jnp.concatenate([early, rows], axis=2), groups)
    later = after(queries, early)[None, :, CHUNK:]
    later = exchanged(jnp.broadcast_to(later, (lines, PAGE, (KVH - 1) * CHUNK)), groups)
    numbers = early[:, 0, CHUNK:CHUNK + limit + 2].astype(jnp.int32)
    tables = (numbers[:, :limit], numbers[:, limit], numbers[:, limit + 1], (me // CLUSTER)[None], store_slot[0])
    fresh = new_kv[0, 0]
    attended = None
    parts = []
    for g in range(KVH):
        side = sides[g]
        if g > 1:
            side = after(side, parts[g - 2])
        both = swapped(side, "serve", 1)
        pools = (owns[g], twin, side, both)
        if g == 0:
            part, pool_out = attend(g, 0, tables, early, pools, fresh, pool, incoming)
        else:
            part = attend(g, g - 1, tables, later, pools, fresh)[0]
        parts.append(part)
        attended = merge(g, exchanged(part, groups), attended)
    return (attended, pool_out)


def solution(mesh):
    return jax.shard_map(
        per_device,
        mesh=mesh,
        in_specs=(
            P(("groups", "serve"), None),
            P(("groups", "serve"), None, None, None, None),
            P(("groups", "serve"), None, None, None),
            P(("groups", "serve"), None),
            P(("groups", "serve"), None),
            P(("groups", "serve")),
            P(("groups", "serve"), None),
        ),
        out_specs=(P(("groups", "serve"), None), P(("groups", "serve"), None, None, None)),
        check_vma=False,
    )
```

```python
import functools

import jax
import jax.numpy as jnp
from jax import lax
from jax.experimental import pallas as pl
from jax.experimental.pallas import tpu as pltpu
from jax.sharding import PartitionSpec as P

PAGE = 128
KVH = 4
GQ = 5
HD = 128
MAXP = 48
SCALE = HD ** (-0.5)
LOG2E = 1.4426950408889634
LOW = -1e30
CLUSTER = 4
BLOCK = 4
STAT = 32
ROWS = GQ * PAGE + STAT
CHUNK = GQ * HD
CONTRACT_LAST = (((1,), (1,)), ((), ()))


def swapped(array, axis, bit):
    size = lax.axis_size(axis)
    return lax.ppermute(array, axis, [(i, i ^ bit) for i in range(size)])


def shifted(array, axis, by):
    size = lax.axis_size(axis)
    return lax.ppermute(array, axis, [(i, (i + by) % size) for i in range(size)])


def attend_kernel(lines, head, q_head, picks, counts, lasts, mine, store, *refs):
    q_all, own, twin, side, both, fresh = refs[:6]
    stores = len(refs) == 20
    if stores:
        pool, incoming, out, pool_out = refs[6:10]
        store_sems = refs[-1]
        scratch = refs[10:-1]
    else:
        out = refs[6]
        scratch = refs[7:]
    pages, queries, results, scores, tops, acc, q_sems, page_sems, out_sems = scratch
    slots = own.shape[0]
    columns = pl.ds(head * HD, HD)
    extra = pages.shape[1] - 1

    def request_of(t):
        return lax.rem(mine[0] - t + lines, lines)

    def q_copy(t, h):
        origin = q_all.at[request_of(t), pl.ds(0, PAGE), pl.ds((q_head * GQ + h) * HD, HD)]
        return pltpu.make_async_copy(origin, queries.at[t, h], q_sems.at[t, h])

    def out_copy(t):
        return pltpu.make_async_copy(results.at[t], out.at[request_of(t)], out_sems.at[t])

    def page_copy(source, slot, buffer, place):
        if source.shape[-1] == HD:
            origin = source.at[slot]
        else:
            origin = source.at[slot, :, :, columns]
        return pltpu.make_async_copy(origin, pages.at[buffer, place], page_sems.at[buffer, place])

    def fetch(t):
        request = request_of(t)
        buffer = lax.rem(t, 2)

        @pl.loop(0, counts[request])
        def _(place):
            code = picks[request, place]
            rank = lax.div(code, slots)
            slot = lax.rem(code, slots)
            for index, source in enumerate((own, twin, side, both)):
                @pl.when(rank == index)
                def _():
                    page_copy(source, slot, buffer, place).start()

    def arrive(t):
        buffer = lax.rem(t, 2)

        @pl.loop(0, counts[request_of(t)])
        def _(place):
            page_copy(own, 0, buffer, place).wait()

    def store_copy(slot):
        return pltpu.make_async_copy(pool.at[slot], pool_out.at[slot], store_sems.at[slot])

    fresh_copy = pltpu.make_async_copy(fresh.at[:, :, columns], pages.at[0, extra], page_sems.at[0, extra])
    for t in range(lines):
        for h in range(GQ):
            q_copy(t, h).start()
    for buffer in range(2):
        pages[buffer, :extra] = jnp.zeros((extra,) + pages.shape[2:], pages.dtype)
    fresh_copy.start()
    fetch(0)
    if lines > 1:
        fetch(1)
    if stores:
        @pl.loop(0, pool.shape[0])
        def _(slot):
            @pl.when(slot != store[0])
            def _():
                store_copy(slot).start()

        pltpu.make_async_copy(incoming.at[0], pool_out.at[store[0]], store_sems.at[store[0]]).start()

    def soften(h, scored, values):
        factor = SCALE * LOG2E
        old = tops[h]
        new = jnp.maximum(old, jnp.max(scored(), axis=1, keepdims=True))
        tops[h] = new
        fade = jnp.exp2((old - new) * factor)
        s = scored()
        wide = jnp.concatenate([new] * (s.shape[1] // PAGE), axis=1)
        expo = jnp.exp2((s - wide) * factor).astype(jnp.bfloat16)
        added = jnp.dot(expo, values, preferred_element_type=jnp.float32)
        acc[h] = acc[h] * jnp.concatenate([fade, fade], axis=1) + added

    def with_ones(values):
        return jnp.concatenate([values, jnp.ones_like(values)], axis=1)

    def score(t, h, keys):
        return lax.dot_general(queries[t, h], keys, CONTRACT_LAST, preferred_element_type=jnp.float32)

    def seen_of(t, index):
        request = request_of(t)
        return (counts[request] - 1 - index * BLOCK) * PAGE + lasts[request]

    def score_block(t, index, h, keys):
        column = lax.broadcasted_iota(jnp.int32, (PAGE, BLOCK * PAGE), 1)
        scores[h] = jnp.where(column < seen_of(t, index), score(t, h, keys), LOW)

    def keys_of(t, index):
        return pages[lax.rem(t, 2), pl.ds(index * BLOCK, BLOCK), 0].reshape(BLOCK * PAGE, HD)

    def values_of(t, index):
        return with_ones(pages[lax.rem(t, 2), pl.ds(index * BLOCK, BLOCK), 1].reshape(BLOCK * PAGE, HD))

    def blocks_of(t):
        return jnp.maximum(lax.div(counts[request_of(t)] + BLOCK - 1, BLOCK), 1)

    def reset():
        tops[...] = jnp.full(tops.shape, LOW, jnp.float32)
        acc[...] = jnp.zeros(acc.shape, jnp.float32)

    def finish(t):
        some = (counts[request_of(t)] > 0) | (t == 0)
        lane = lax.broadcasted_iota(jnp.int32, (PAGE, PAGE), 1)
        sums = jnp.ones((PAGE, PAGE), jnp.float32)
        heights = jnp.zeros((PAGE, PAGE), jnp.float32)
        for h in range(GQ):
            total = acc[h, :, HD:]
            results[t, h * PAGE:(h + 1) * PAGE, :] = (acc[h, :, :HD] * (1.0 / total)).astype(jnp.bfloat16)
            sums = jnp.where(lane == h, total, sums)
            heights = jnp.where(lane == h, tops[h], heights)
        level = heights.T[:8] * SCALE + jnp.log(sums.T[:8])
        level = jnp.where(some, level, LOW)
        high = level.astype(jnp.bfloat16).astype(jnp.float32)
        middle = (level - high).astype(jnp.bfloat16).astype(jnp.float32)
        low = level - high - middle
        stat = jnp.concatenate([high, middle, low, jnp.zeros_like(low)], axis=0)
        results[t, GQ * PAGE:, :] = stat.astype(jnp.bfloat16)
        out_copy(t).start()

    for t in range(lines):
        for h in range(GQ):
            q_copy(t, h).wait()
    fresh_copy.wait()
    reset()
    span_values = with_ones(pages[0, extra, 1])
    seen = lax.broadcasted_iota(jnp.int32, (PAGE, PAGE), 1) <= lax.broadcasted_iota(jnp.int32, (PAGE, PAGE), 0)
    for h in range(GQ):
        s = jnp.where(seen, score(0, h, pages[0, extra, 0]), LOW)
        soften(h, lambda: s, span_values)
    arrive(0)
    first = keys_of(0, 0)
    for h in range(GQ):
        score_block(0, 0, h, first)

    def step(_, carry):
        t, index = carry
        ends = index + 1 >= blocks_of(t)
        later_t = jnp.where(ends, t + 1, t)
        later_index = jnp.where(ends, 0, index + 1)
        ahead_t = jnp.minimum(later_t, lines - 1)

        @pl.when(ends & (t + 1 < lines))
        def _():
            arrive(t + 1)

        values = values_of(t, index)
        keys = keys_of(ahead_t, later_index)
        for h in range(GQ):
            soften(h, lambda: scores[h], values)
            score_block(ahead_t, later_index, h, keys)

        @pl.when(ends)
        def _():
            finish(t)
            reset()

            @pl.when(t + 2 < lines)
            def _():
                fetch(t + 2)

        return later_t, later_index

    steps = blocks_of(0)
    for t in range(1, lines):
        steps += blocks_of(t)
    lax.fori_loop(0, steps, step, (jnp.int32(0), jnp.int32(0)))
    for t in range(lines):
        out_copy(t).wait()
    if stores:
        @pl.loop(0, pool.shape[0])
        def _(slot):
            store_copy(slot).wait()


def attend(head, q_head, tables, q_all, pools, fresh, pool=None, incoming=None):
    picks, counts, lasts, mine, store = tables
    lines = q_all.shape[0]
    places = picks.shape[1]
    out_shape = [jax.ShapeDtypeStruct((lines, ROWS, HD), jnp.bfloat16)]
    scratch = [
        pltpu.VMEM((2, places + 1, 2, PAGE, HD), jnp.bfloat16),
        pltpu.VMEM((lines, GQ, PAGE, HD), jnp.bfloat16),
        pltpu.VMEM((lines, ROWS, HD), jnp.bfloat16),
        pltpu.VMEM((GQ, PAGE, BLOCK * PAGE), jnp.float32),
        pltpu.VMEM((GQ, PAGE, PAGE), jnp.float32),
        pltpu.VMEM((GQ, PAGE, 2 * HD), jnp.float32),
        pltpu.SemaphoreType.DMA((lines, GQ)),
        pltpu.SemaphoreType.DMA((2, places + 1)),
        pltpu.SemaphoreType.DMA((lines,)),
    ]
    operands = [q_all, *pools, fresh]
    if incoming is not None:
        operands += [pool, incoming]
        out_shape.append(jax.ShapeDtypeStruct(pool.shape, pool.dtype))
        scratch.append(pltpu.SemaphoreType.DMA((pool.shape[0],)))
    grid_spec = pltpu.PrefetchScalarGridSpec(
        num_scalar_prefetch=5,
        grid=(),
        in_specs=[pl.BlockSpec(memory_space=pl.ANY)] * len(operands),
        out_specs=[pl.BlockSpec(memory_space=pltpu.HBM)] * len(out_shape),
        scratch_shapes=scratch,
    )
    return pl.pallas_call(
        functools.partial(attend_kernel, lines, head, q_head),
        grid_spec=grid_spec,
        out_shape=out_shape,
        compiler_params=pltpu.CompilerParams(vmem_limit_bytes=24 * 2**20),
        cost_estimate=pl.CostEstimate(flops=1, bytes_accessed=1, transcendentals=0),
    )(picks, counts, lasts, mine, store, *operands)


def merge_kernel(head, parts, *refs):
    lines = parts.shape[0]
    out, result, sem = refs[-3:]
    levels = []
    for i in range(lines):
        block = parts[i, GQ * PAGE:, :].astype(jnp.float32)
        levels.append(block[:8] + block[8:16] + block[16:24])
    top = functools.reduce(jnp.maximum, levels)
    weights = [jnp.exp(level - top) for level in levels]
    total = functools.reduce(jnp.add, weights)
    weights = [weight / total for weight in weights]
    filler = PAGE - lines * 8
    if filler:
        weights.append(jnp.zeros((filler, PAGE), jnp.float32))
    table = jnp.concatenate(weights, axis=0).T
    for h in range(GQ):
        merged = jnp.zeros((PAGE, HD), jnp.float32)
        for i in range(lines):
            column = i * 8 + h
            merged += table[:, column:column + 1] * parts[i, h * PAGE:(h + 1) * PAGE, :].astype(jnp.float32)
        result[:, h * HD:(h + 1) * HD] = merged.astype(jnp.bfloat16)
    copy = pltpu.make_async_copy(result, out.at[:, pl.ds(head * CHUNK, CHUNK)], sem)
    copy.start()
    copy.wait()


def merge(head, parts, whole):
    before = [] if whole is None else [whole]
    return pl.pallas_call(
        functools.partial(merge_kernel, head),
        in_specs=[pl.BlockSpec(memory_space=pltpu.VMEM)] + [pl.BlockSpec(memory_space=pl.ANY)] * len(before),
        out_specs=pl.BlockSpec(memory_space=pl.ANY),
        out_shape=jax.ShapeDtypeStruct((PAGE, KVH * CHUNK), jnp.bfloat16),
        scratch_shapes=[pltpu.VMEM((PAGE, CHUNK), jnp.bfloat16), pltpu.SemaphoreType.DMA],
        input_output_aliases={1: 0} if before else {},
        cost_estimate=pl.CostEstimate(flops=1, bytes_accessed=1, transcendentals=0),
    )(parts, *before)


def page_rows(me, lines, limit, slots, page_owner, page_slot, prefix_len):
    owners = page_owner[0]
    length = prefix_len[0]
    used = (length + PAGE - 1) // PAGE
    spot = jnp.arange(MAXP)
    here = (spot < used)[None] & (owners[None] // CLUSTER == jnp.arange(lines)[:, None])
    before = jnp.sum(here[:, None, :] & (spot[None, None, :] < spot[None, :, None]), axis=2)
    local = ((owners % CLUSTER) ^ (me % CLUSTER)) * slots + page_slot[0]
    chosen = here[:, :, None] & (before[:, :, None] == jnp.arange(limit)[None, None, :])
    picks = jnp.sum(jnp.where(chosen, local[None, :, None], 0), axis=1)
    counts = jnp.sum(here, axis=1)
    tail = jnp.any(here & (spot == used - 1)[None], axis=1)
    lasts = jnp.where(tail, length - (used - 1) * PAGE, PAGE)
    return jnp.concatenate([picks, counts[:, None], lasts[:, None]], axis=1)


def exchanged(array, groups):
    return lax.all_to_all(array, "serve", 0, 0, axis_index_groups=groups, tiled=True)


def after(array, *others):
    return lax.optimization_barrier((array, *others))[0]


def per_device(queries, new_kv, pool, page_owner, page_slot, prefix_len, store_slot):
    width = lax.axis_size("serve")
    lines = width // CLUSTER
    groups = [[c * CLUSTER + i for c in range(lines)] for i in range(CLUSTER)]
    me = lax.axis_index("serve")
    slots = pool.shape[0]
    capacity = (MAXP + width - 2) // (width - 1)
    limit = min(MAXP, CLUSTER * capacity)
    incoming = shifted(new_kv[0], "serve", 1)
    owns = [after(pool, incoming)[:, :, :, :HD]]
    rest = after(pool, owns[0])
    owns += [rest[:, :, :, g * HD:(g + 1) * HD] for g in range(1, KVH)]
    sides = [swapped(own, "serve", 2) for own in owns]
    twin = swapped(rest, "serve", 1)
    rows = page_rows(me, lines, limit, slots, page_owner, page_slot, prefix_len).astype(queries.dtype)
    rows = jnp.pad(rows[:, None], ((0, 0), (0, PAGE - 1), (0, PAGE - limit - 2)))
    q_all = jnp.broadcast_to(queries[None], (lines, PAGE, KVH * CHUNK))
    q_all = exchanged(jnp.concatenate([q_all, rows], axis=2), groups)
    numbers = q_all[:, 0, KVH * CHUNK:KVH * CHUNK + limit + 2].astype(jnp.int32)
    tables = (numbers[:, :limit], numbers[:, limit], numbers[:, limit + 1], (me // CLUSTER)[None], store_slot[0])
    fresh = new_kv[0, 0]
    attended = None
    parts = []
    for g in range(KVH):
        side = sides[g]
        if g > 1:
            side = after(side, parts[g - 2])
        both = swapped(side, "serve", 1)
        pools = (owns[g], twin, side, both)
        if g == 0:
            part, pool_out = attend(g, g, tables, q_all, pools, fresh, pool, incoming)
        else:
            part = attend(g, g, tables, q_all, pools, fresh)[0]
        parts.append(part)
        attended = merge(g, exchanged(part, groups), attended)
    return (attended, pool_out)


def solution(mesh):
    return jax.shard_map(
        per_device,
        mesh=mesh,
        in_specs=(
            P(("groups", "serve"), None),
            P(("groups", "serve"), None, None, None, None),
            P(("groups", "serve"), None, None, None),
            P(("groups", "serve"), None),
            P(("groups", "serve"), None),
            P(("groups", "serve")),
            P(("groups", "serve"), None),
        ),
        out_specs=(P(("groups", "serve"), None), P(("groups", "serve"), None, None, None)),
        check_vma=False,
    )
```

```python
import functools

import jax
import jax.numpy as jnp
from jax import lax
from jax.experimental import pallas as pl
from jax.experimental.pallas import tpu as pltpu
from jax.sharding import PartitionSpec as P

PAGE = 128
KVH = 4
GQ = 5
HD = 128
MAXP = 48
SCALE = HD ** (-0.5)
LOG2E = 1.4426950408889634
LOW = -1e30
CLUSTER = 4
BLOCK = 4
STAT = 32
ROWS = GQ * PAGE + STAT
CHUNK = GQ * HD
CONTRACT_LAST = (((1,), (1,)), ((), ()))


def swapped(array, axis, bit):
    size = lax.axis_size(axis)
    return lax.ppermute(array, axis, [(i, i ^ bit) for i in range(size)])


def shifted(array, axis, by):
    size = lax.axis_size(axis)
    return lax.ppermute(array, axis, [(i, (i + by) % size) for i in range(size)])


def attend_kernel(lines, head, q_head, picks, counts, lasts, mine, store, *refs):
    q_all, own, twin, side, both, fresh = refs[:6]
    stores = len(refs) == 20
    if stores:
        pool, incoming, out, pool_out = refs[6:10]
        store_sems = refs[-1]
        scratch = refs[10:-1]
    else:
        out = refs[6]
        scratch = refs[7:]
    pages, queries, results, scores, tops, acc, q_sems, page_sems, out_sems = scratch
    slots = own.shape[0]
    columns = pl.ds(head * HD, HD)
    extra = pages.shape[1] - 1

    def request_of(t):
        return lax.rem(mine[0] - t + lines, lines)

    def q_copy(t, h):
        origin = q_all.at[request_of(t), pl.ds(0, PAGE), pl.ds((q_head * GQ + h) * HD, HD)]
        return pltpu.make_async_copy(origin, queries.at[t, h], q_sems.at[t, h])

    def out_copy(t):
        return pltpu.make_async_copy(results.at[t], out.at[request_of(t)], out_sems.at[t])

    def page_copy(source, slot, buffer, place):
        if source.shape[-1] == HD:
            origin = source.at[slot]
        else:
            origin = source.at[slot, :, :, columns]
        return pltpu.make_async_copy(origin, pages.at[buffer, place], page_sems.at[buffer, place])

    def fetch(t):
        request = request_of(t)
        buffer = lax.rem(t, 2)

        @pl.loop(0, counts[request])
        def _(place):
            code = picks[request, place]
            rank = lax.div(code, slots)
            slot = lax.rem(code, slots)
            for index, source in enumerate((own, twin, side, both)):
                @pl.when(rank == index)
                def _():
                    page_copy(source, slot, buffer, place).start()

    def arrive(t):
        buffer = lax.rem(t, 2)

        @pl.loop(0, counts[request_of(t)])
        def _(place):
            page_copy(own, 0, buffer, place).wait()

    def store_copy(slot):
        return pltpu.make_async_copy(pool.at[slot], pool_out.at[slot], store_sems.at[slot])

    fresh_copy = pltpu.make_async_copy(fresh.at[:, :, columns], pages.at[0, extra], page_sems.at[0, extra])
    for t in range(lines):
        for h in range(GQ):
            q_copy(t, h).start()
    for buffer in range(2):
        pages[buffer, :extra] = jnp.zeros((extra,) + pages.shape[2:], pages.dtype)
    fresh_copy.start()
    fetch(0)
    if lines > 1:
        fetch(1)
    if stores:
        @pl.loop(0, pool.shape[0])
        def _(slot):
            @pl.when(slot != store[0])
            def _():
                store_copy(slot).start()

        pltpu.make_async_copy(incoming.at[0], pool_out.at[store[0]], store_sems.at[store[0]]).start()

    def soften(h, scored, values):
        factor = SCALE * LOG2E
        old = tops[h]
        new = jnp.maximum(old, jnp.max(scored(), axis=1, keepdims=True))
        tops[h] = new
        fade = jnp.exp2((old - new) * factor)
        s = scored()
        wide = jnp.concatenate([new] * (s.shape[1] // PAGE), axis=1)
        expo = jnp.exp2((s - wide) * factor).astype(jnp.bfloat16)
        added = jnp.dot(expo, values, preferred_element_type=jnp.float32)
        acc[h] = acc[h] * jnp.concatenate([fade, fade], axis=1) + added

    def with_ones(values):
        return jnp.concatenate([values, jnp.ones_like(values)], axis=1)

    def score(t, h, keys):
        return lax.dot_general(queries[t, h], keys, CONTRACT_LAST, preferred_element_type=jnp.float32)

    def seen_of(t, index):
        request = request_of(t)
        return (counts[request] - 1 - index * BLOCK) * PAGE + lasts[request]

    def score_block(t, index, h, keys):
        column = lax.broadcasted_iota(jnp.int32, (PAGE, BLOCK * PAGE), 1)
        scores[h] = jnp.where(column < seen_of(t, index), score(t, h, keys), LOW)

    def keys_of(t, index):
        return pages[lax.rem(t, 2), pl.ds(index * BLOCK, BLOCK), 0].reshape(BLOCK * PAGE, HD)

    def values_of(t, index):
        return with_ones(pages[lax.rem(t, 2), pl.ds(index * BLOCK, BLOCK), 1].reshape(BLOCK * PAGE, HD))

    def blocks_of(t):
        return jnp.maximum(lax.div(counts[request_of(t)] + BLOCK - 1, BLOCK), 1)

    def reset():
        tops[...] = jnp.full(tops.shape, LOW, jnp.float32)
        acc[...] = jnp.zeros(acc.shape, jnp.float32)

    def finish(t):
        some = (counts[request_of(t)] > 0) | (t == 0)
        lane = lax.broadcasted_iota(jnp.int32, (PAGE, PAGE), 1)
        sums = jnp.ones((PAGE, PAGE), jnp.float32)
        heights = jnp.zeros((PAGE, PAGE), jnp.float32)
        for h in range(GQ):
            total = acc[h, :, HD:]
            results[t, h * PAGE:(h + 1) * PAGE, :] = (acc[h, :, :HD] * (1.0 / total)).astype(jnp.bfloat16)
            sums = jnp.where(lane == h, total, sums)
            heights = jnp.where(lane == h, tops[h], heights)
        level = heights.T[:8] * SCALE + jnp.log(sums.T[:8])
        level = jnp.where(some, level, LOW)
        high = level.astype(jnp.bfloat16).astype(jnp.float32)
        middle = (level - high).astype(jnp.bfloat16).astype(jnp.float32)
        low = level - high - middle
        stat = jnp.concatenate([high, middle, low, jnp.zeros_like(low)], axis=0)
        results[t, GQ * PAGE:, :] = stat.astype(jnp.bfloat16)
        out_copy(t).start()

    for t in range(lines):
        for h in range(GQ):
            q_copy(t, h).wait()
    fresh_copy.wait()
    reset()
    span_values = with_ones(pages[0, extra, 1])
    seen = lax.broadcasted_iota(jnp.int32, (PAGE, PAGE), 1) <= lax.broadcasted_iota(jnp.int32, (PAGE, PAGE), 0)
    for h in range(GQ):
        s = jnp.where(seen, score(0, h, pages[0, extra, 0]), LOW)
        soften(h, lambda: s, span_values)
    arrive(0)
    first = keys_of(0, 0)
    for h in range(GQ):
        score_block(0, 0, h, first)

    def step(_, carry):
        t, index = carry
        ends = index + 1 >= blocks_of(t)
        later_t = jnp.where(ends, t + 1, t)
        later_index = jnp.where(ends, 0, index + 1)
        ahead_t = jnp.minimum(later_t, lines - 1)

        @pl.when(ends & (t + 1 < lines))
        def _():
            arrive(t + 1)

        values = values_of(t, index)
        keys = keys_of(ahead_t, later_index)
        for h in range(GQ):
            soften(h, lambda: scores[h], values)
            score_block(ahead_t, later_index, h, keys)

        @pl.when(ends)
        def _():
            finish(t)
            reset()

            @pl.when(t + 2 < lines)
            def _():
                fetch(t + 2)

        return later_t, later_index

    steps = blocks_of(0)
    for t in range(1, lines):
        steps += blocks_of(t)
    lax.fori_loop(0, steps, step, (jnp.int32(0), jnp.int32(0)))
    for t in range(lines):
        out_copy(t).wait()
    if stores:
        @pl.loop(0, pool.shape[0])
        def _(slot):
            store_copy(slot).wait()


def attend(head, q_head, tables, q_all, pools, fresh, pool=None, incoming=None):
    picks, counts, lasts, mine, store = tables
    lines = q_all.shape[0]
    places = picks.shape[1]
    out_shape = [jax.ShapeDtypeStruct((lines, ROWS, HD), jnp.bfloat16)]
    scratch = [
        pltpu.VMEM((2, places + 1, 2, PAGE, HD), jnp.bfloat16),
        pltpu.VMEM((lines, GQ, PAGE, HD), jnp.bfloat16),
        pltpu.VMEM((lines, ROWS, HD), jnp.bfloat16),
        pltpu.VMEM((GQ, PAGE, BLOCK * PAGE), jnp.float32),
        pltpu.VMEM((GQ, PAGE, PAGE), jnp.float32),
        pltpu.VMEM((GQ, PAGE, 2 * HD), jnp.float32),
        pltpu.SemaphoreType.DMA((lines, GQ)),
        pltpu.SemaphoreType.DMA((2, places + 1)),
        pltpu.SemaphoreType.DMA((lines,)),
    ]
    operands = [q_all, *pools, fresh]
    if incoming is not None:
        operands += [pool, incoming]
        out_shape.append(jax.ShapeDtypeStruct(pool.shape, pool.dtype))
        scratch.append(pltpu.SemaphoreType.DMA((pool.shape[0],)))
    grid_spec = pltpu.PrefetchScalarGridSpec(
        num_scalar_prefetch=5,
        grid=(),
        in_specs=[pl.BlockSpec(memory_space=pl.ANY)] * len(operands),
        out_specs=[pl.BlockSpec(memory_space=pltpu.HBM)] * len(out_shape),
        scratch_shapes=scratch,
    )
    return pl.pallas_call(
        functools.partial(attend_kernel, lines, head, q_head),
        grid_spec=grid_spec,
        out_shape=out_shape,
        compiler_params=pltpu.CompilerParams(vmem_limit_bytes=24 * 2**20),
        cost_estimate=pl.CostEstimate(flops=1, bytes_accessed=1, transcendentals=0),
    )(picks, counts, lasts, mine, store, *operands)


def merge_kernel(head, parts, *refs):
    lines = parts.shape[0]
    out, result, sem = refs[-3:]
    levels = []
    for i in range(lines):
        block = parts[i, GQ * PAGE:, :].astype(jnp.float32)
        levels.append(block[:8] + block[8:16] + block[16:24])
    top = functools.reduce(jnp.maximum, levels)
    weights = [jnp.exp(level - top) for level in levels]
    total = functools.reduce(jnp.add, weights)
    weights = [weight / total for weight in weights]
    filler = PAGE - lines * 8
    if filler:
        weights.append(jnp.zeros((filler, PAGE), jnp.float32))
    table = jnp.concatenate(weights, axis=0).T
    for h in range(GQ):
        merged = jnp.zeros((PAGE, HD), jnp.float32)
        for i in range(lines):
            column = i * 8 + h
            merged += table[:, column:column + 1] * parts[i, h * PAGE:(h + 1) * PAGE, :].astype(jnp.float32)
        result[:, h * HD:(h + 1) * HD] = merged.astype(jnp.bfloat16)
    copy = pltpu.make_async_copy(result, out.at[:, pl.ds(head * CHUNK, CHUNK)], sem)
    copy.start()
    copy.wait()


def merge(head, parts, whole):
    before = [] if whole is None else [whole]
    return pl.pallas_call(
        functools.partial(merge_kernel, head),
        in_specs=[pl.BlockSpec(memory_space=pltpu.VMEM)] + [pl.BlockSpec(memory_space=pl.ANY)] * len(before),
        out_specs=pl.BlockSpec(memory_space=pl.ANY),
        out_shape=jax.ShapeDtypeStruct((PAGE, KVH * CHUNK), jnp.bfloat16),
        scratch_shapes=[pltpu.VMEM((PAGE, CHUNK), jnp.bfloat16), pltpu.SemaphoreType.DMA],
        input_output_aliases={1: 0} if before else {},
        cost_estimate=pl.CostEstimate(flops=1, bytes_accessed=1, transcendentals=0),
    )(parts, *before)


def page_rows(me, lines, limit, slots, page_owner, page_slot, prefix_len):
    owners = page_owner[0]
    length = prefix_len[0]
    used = (length + PAGE - 1) // PAGE
    spot = jnp.arange(MAXP)
    here = (spot < used)[None] & (owners[None] // CLUSTER == jnp.arange(lines)[:, None])
    before = jnp.sum(here[:, None, :] & (spot[None, None, :] < spot[None, :, None]), axis=2)
    local = ((owners % CLUSTER) ^ (me % CLUSTER)) * slots + page_slot[0]
    chosen = here[:, :, None] & (before[:, :, None] == jnp.arange(limit)[None, None, :])
    picks = jnp.sum(jnp.where(chosen, local[None, :, None], 0), axis=1)
    counts = jnp.sum(here, axis=1)
    tail = jnp.any(here & (spot == used - 1)[None], axis=1)
    lasts = jnp.where(tail, length - (used - 1) * PAGE, PAGE)
    return jnp.concatenate([picks, counts[:, None], lasts[:, None]], axis=1)


def exchanged(array, groups):
    return lax.all_to_all(array, "serve", 0, 0, axis_index_groups=groups, tiled=True)


def after(array, *others):
    return lax.optimization_barrier((array, *others))[0]


def per_device(queries, new_kv, pool, page_owner, page_slot, prefix_len, store_slot):
    width = lax.axis_size("serve")
    lines = width // CLUSTER
    groups = [[c * CLUSTER + i for c in range(lines)] for i in range(CLUSTER)]
    me = lax.axis_index("serve")
    slots = pool.shape[0]
    capacity = (MAXP + width - 2) // (width - 1)
    limit = min(MAXP, CLUSTER * capacity)
    incoming = shifted(new_kv[0], "serve", 1)
    owns = [pool[:, :, :, :HD]]
    rest = after(pool, owns[0])
    owns += [rest[:, :, :, g * HD:(g + 1) * HD] for g in range(1, KVH)]
    sides = [swapped(own, "serve", 2) for own in owns]
    twin = swapped(rest, "serve", 1)
    rows = page_rows(me, lines, limit, slots, page_owner, page_slot, prefix_len).astype(queries.dtype)
    rows = jnp.pad(rows[:, None], ((0, 0), (0, PAGE - 1), (0, PAGE - limit - 2)))
    q_all = jnp.broadcast_to(after(queries, incoming)[None], (lines, PAGE, KVH * CHUNK))
    q_all = exchanged(jnp.concatenate([q_all, rows], axis=2), groups)
    numbers = q_all[:, 0, KVH * CHUNK:KVH * CHUNK + limit + 2].astype(jnp.int32)
    tables = (numbers[:, :limit], numbers[:, limit], numbers[:, limit + 1], (me // CLUSTER)[None], store_slot[0])
    fresh = new_kv[0, 0]
    attended = None
    parts = []
    for g in range(KVH):
        side = sides[g]
        if g > 1:
            side = after(side, parts[g - 2])
        both = swapped(side, "serve", 1)
        pools = (owns[g], twin, side, both)
        if g == 0:
            part, pool_out = attend(g, g, tables, q_all, pools, fresh, pool, incoming)
        else:
            part = attend(g, g, tables, q_all, pools, fresh)[0]
        parts.append(part)
        attended = merge(g, exchanged(part, groups), attended)
    return (attended, pool_out)


def solution(mesh):
    return jax.shard_map(
        per_device,
        mesh=mesh,
        in_specs=(
            P(("groups", "serve"), None),
            P(("groups", "serve"), None, None, None, None),
            P(("groups", "serve"), None, None, None),
            P(("groups", "serve"), None),
            P(("groups", "serve"), None),
            P(("groups", "serve")),
            P(("groups", "serve"), None),
        ),
        out_specs=(P(("groups", "serve"), None), P(("groups", "serve"), None, None, None)),
        check_vma=False,
    )
```

```python
import functools

import jax
import jax.numpy as jnp
from jax import lax
from jax.experimental import pallas as pl
from jax.experimental.pallas import tpu as pltpu
from jax.sharding import PartitionSpec as P

PAGE = 128
KVH = 4
GQ = 5
HD = 128
MAXP = 48
SCALE = HD ** (-0.5)
LOG2E = 1.4426950408889634
LOW = -1e30
CLUSTER = 4
BLOCK = 4
STAT = 32
ROWS = GQ * PAGE + STAT
CHUNK = GQ * HD
CONTRACT_LAST = (((1,), (1,)), ((), ()))


def swapped(array, axis, bit):
    size = lax.axis_size(axis)
    return lax.ppermute(array, axis, [(i, i ^ bit) for i in range(size)])


def shifted(array, axis, by):
    size = lax.axis_size(axis)
    return lax.ppermute(array, axis, [(i, (i + by) % size) for i in range(size)])


def attend_kernel(lines, head, q_head, picks, counts, lasts, mine, store, *refs):
    q_all, own, twin, side, both, fresh = refs[:6]
    stores = len(refs) == 20
    if stores:
        pool, incoming, out, pool_out = refs[6:10]
        store_sems = refs[-1]
        scratch = refs[10:-1]
    else:
        out = refs[6]
        scratch = refs[7:]
    pages, queries, results, scores, tops, acc, q_sems, page_sems, out_sems = scratch
    slots = own.shape[0]
    columns = pl.ds(head * HD, HD)
    extra = pages.shape[1] - 1

    def request_of(t):
        return lax.rem(mine[0] - t + lines, lines)

    def q_copy(t, h):
        origin = q_all.at[request_of(t), pl.ds(0, PAGE), pl.ds((q_head * GQ + h) * HD, HD)]
        return pltpu.make_async_copy(origin, queries.at[t, h], q_sems.at[t, h])

    def out_copy(t):
        return pltpu.make_async_copy(results.at[t], out.at[request_of(t)], out_sems.at[t])

    def page_copy(source, slot, buffer, place):
        if source.shape[-1] == HD:
            origin = source.at[slot]
        else:
            origin = source.at[slot, :, :, columns]
        return pltpu.make_async_copy(origin, pages.at[buffer, place], page_sems.at[buffer, place])

    def fetch(t):
        request = request_of(t)
        buffer = lax.rem(t, 2)

        @pl.loop(0, counts[request])
        def _(place):
            code = picks[request, place]
            rank = lax.div(code, slots)
            slot = lax.rem(code, slots)
            for index, source in enumerate((own, twin, side, both)):
                @pl.when(rank == index)
                def _():
                    page_copy(source, slot, buffer, place).start()

    def arrive(t):
        buffer = lax.rem(t, 2)

        @pl.loop(0, counts[request_of(t)])
        def _(place):
            page_copy(own, 0, buffer, place).wait()

    def store_copy(slot):
        return pltpu.make_async_copy(pool.at[slot], pool_out.at[slot], store_sems.at[slot])

    fresh_copy = pltpu.make_async_copy(fresh.at[:, :, columns], pages.at[0, extra], page_sems.at[0, extra])
    for t in range(lines):
        for h in range(GQ):
            q_copy(t, h).start()
    for buffer in range(2):
        pages[buffer, :extra] = jnp.zeros((extra,) + pages.shape[2:], pages.dtype)
    fresh_copy.start()
    fetch(0)
    if lines > 1:
        fetch(1)
    if stores:
        @pl.loop(0, pool.shape[0])
        def _(slot):
            @pl.when(slot != store[0])
            def _():
                store_copy(slot).start()

        pltpu.make_async_copy(incoming.at[0], pool_out.at[store[0]], store_sems.at[store[0]]).start()

    def soften(h, scored, values):
        factor = SCALE * LOG2E
        old = tops[h]
        new = jnp.maximum(old, jnp.max(scored(), axis=1, keepdims=True))
        tops[h] = new
        fade = jnp.exp2((old - new) * factor)
        s = scored()
        wide = jnp.concatenate([new] * (s.shape[1] // PAGE), axis=1)
        expo = jnp.exp2((s - wide) * factor).astype(jnp.bfloat16)
        added = jnp.dot(expo, values, preferred_element_type=jnp.float32)
        acc[h] = acc[h] * jnp.concatenate([fade, fade], axis=1) + added

    def with_ones(values):
        return jnp.concatenate([values, jnp.ones_like(values)], axis=1)

    def score(t, h, keys):
        return lax.dot_general(queries[t, h], keys, CONTRACT_LAST, preferred_element_type=jnp.float32)

    def seen_of(t, index):
        request = request_of(t)
        return (counts[request] - 1 - index * BLOCK) * PAGE + lasts[request]

    def score_block(t, index, h, keys):
        column = lax.broadcasted_iota(jnp.int32, (PAGE, BLOCK * PAGE), 1)
        scores[h] = jnp.where(column < seen_of(t, index), score(t, h, keys), LOW)

    def keys_of(t, index):
        return pages[lax.rem(t, 2), pl.ds(index * BLOCK, BLOCK), 0].reshape(BLOCK * PAGE, HD)

    def values_of(t, index):
        return with_ones(pages[lax.rem(t, 2), pl.ds(index * BLOCK, BLOCK), 1].reshape(BLOCK * PAGE, HD))

    def blocks_of(t):
        return jnp.maximum(lax.div(counts[request_of(t)] + BLOCK - 1, BLOCK), 1)

    def reset():
        tops[...] = jnp.full(tops.shape, LOW, jnp.float32)
        acc[...] = jnp.zeros(acc.shape, jnp.float32)

    def finish(t):
        some = (counts[request_of(t)] > 0) | (t == 0)
        lane = lax.broadcasted_iota(jnp.int32, (PAGE, PAGE), 1)
        sums = jnp.ones((PAGE, PAGE), jnp.float32)
        heights = jnp.zeros((PAGE, PAGE), jnp.float32)
        for h in range(GQ):
            total = acc[h, :, HD:]
            results[t, h * PAGE:(h + 1) * PAGE, :] = (acc[h, :, :HD] * (1.0 / total)).astype(jnp.bfloat16)
            sums = jnp.where(lane == h, total, sums)
            heights = jnp.where(lane == h, tops[h], heights)
        level = heights.T[:8] * SCALE + jnp.log(sums.T[:8])
        level = jnp.where(some, level, LOW)
        high = level.astype(jnp.bfloat16).astype(jnp.float32)
        middle = (level - high).astype(jnp.bfloat16).astype(jnp.float32)
        low = level - high - middle
        stat = jnp.concatenate([high, middle, low, jnp.zeros_like(low)], axis=0)
        results[t, GQ * PAGE:, :] = stat.astype(jnp.bfloat16)
        out_copy(t).start()

    for t in range(lines):
        for h in range(GQ):
            q_copy(t, h).wait()
    fresh_copy.wait()
    reset()
    span_values = with_ones(pages[0, extra, 1])
    seen = lax.broadcasted_iota(jnp.int32, (PAGE, PAGE), 1) <= lax.broadcasted_iota(jnp.int32, (PAGE, PAGE), 0)
    for h in range(GQ):
        s = jnp.where(seen, score(0, h, pages[0, extra, 0]), LOW)
        soften(h, lambda: s, span_values)
    arrive(0)
    first = keys_of(0, 0)
    for h in range(GQ):
        score_block(0, 0, h, first)

    def step(_, carry):
        t, index = carry
        ends = index + 1 >= blocks_of(t)
        later_t = jnp.where(ends, t + 1, t)
        later_index = jnp.where(ends, 0, index + 1)
        ahead_t = jnp.minimum(later_t, lines - 1)

        @pl.when(ends & (t + 1 < lines))
        def _():
            arrive(t + 1)

        values = values_of(t, index)
        keys = keys_of(ahead_t, later_index)
        for h in range(GQ):
            soften(h, lambda: scores[h], values)
            score_block(ahead_t, later_index, h, keys)

        @pl.when(ends)
        def _():
            finish(t)
            reset()

            @pl.when(t + 2 < lines)
            def _():
                fetch(t + 2)

        return later_t, later_index

    steps = blocks_of(0)
    for t in range(1, lines):
        steps += blocks_of(t)
    lax.fori_loop(0, steps, step, (jnp.int32(0), jnp.int32(0)))
    for t in range(lines):
        out_copy(t).wait()
    if stores:
        @pl.loop(0, pool.shape[0])
        def _(slot):
            store_copy(slot).wait()


def attend(head, q_head, tables, q_all, pools, fresh, pool=None, incoming=None):
    picks, counts, lasts, mine, store = tables
    lines = q_all.shape[0]
    places = picks.shape[1]
    out_shape = [jax.ShapeDtypeStruct((lines, ROWS, HD), jnp.bfloat16)]
    scratch = [
        pltpu.VMEM((2, places + 1, 2, PAGE, HD), jnp.bfloat16),
        pltpu.VMEM((lines, GQ, PAGE, HD), jnp.bfloat16),
        pltpu.VMEM((lines, ROWS, HD), jnp.bfloat16),
        pltpu.VMEM((GQ, PAGE, BLOCK * PAGE), jnp.float32),
        pltpu.VMEM((GQ, PAGE, PAGE), jnp.float32),
        pltpu.VMEM((GQ, PAGE, 2 * HD), jnp.float32),
        pltpu.SemaphoreType.DMA((lines, GQ)),
        pltpu.SemaphoreType.DMA((2, places + 1)),
        pltpu.SemaphoreType.DMA((lines,)),
    ]
    operands = [q_all, *pools, fresh]
    if incoming is not None:
        operands += [pool, incoming]
        out_shape.append(jax.ShapeDtypeStruct(pool.shape, pool.dtype))
        scratch.append(pltpu.SemaphoreType.DMA((pool.shape[0],)))
    grid_spec = pltpu.PrefetchScalarGridSpec(
        num_scalar_prefetch=5,
        grid=(),
        in_specs=[pl.BlockSpec(memory_space=pl.ANY)] * len(operands),
        out_specs=[pl.BlockSpec(memory_space=pltpu.HBM)] * len(out_shape),
        scratch_shapes=scratch,
    )
    return pl.pallas_call(
        functools.partial(attend_kernel, lines, head, q_head),
        grid_spec=grid_spec,
        out_shape=out_shape,
        compiler_params=pltpu.CompilerParams(vmem_limit_bytes=24 * 2**20),
        cost_estimate=pl.CostEstimate(flops=1, bytes_accessed=1, transcendentals=0),
    )(picks, counts, lasts, mine, store, *operands)


def merge_kernel(head, parts, *refs):
    lines = parts.shape[0]
    out, result, sem = refs[-3:]
    levels = []
    for i in range(lines):
        block = parts[i, GQ * PAGE:, :].astype(jnp.float32)
        levels.append(block[:8] + block[8:16] + block[16:24])
    top = functools.reduce(jnp.maximum, levels)
    weights = [jnp.exp(level - top) for level in levels]
    total = functools.reduce(jnp.add, weights)
    weights = [weight / total for weight in weights]
    filler = PAGE - lines * 8
    if filler:
        weights.append(jnp.zeros((filler, PAGE), jnp.float32))
    table = jnp.concatenate(weights, axis=0).T
    for h in range(GQ):
        merged = jnp.zeros((PAGE, HD), jnp.float32)
        for i in range(lines):
            column = i * 8 + h
            merged += table[:, column:column + 1] * parts[i, h * PAGE:(h + 1) * PAGE, :].astype(jnp.float32)
        result[:, h * HD:(h + 1) * HD] = merged.astype(jnp.bfloat16)
    copy = pltpu.make_async_copy(result, out.at[:, pl.ds(head * CHUNK, CHUNK)], sem)
    copy.start()
    copy.wait()


def merge(head, parts, whole):
    before = [] if whole is None else [whole]
    return pl.pallas_call(
        functools.partial(merge_kernel, head),
        in_specs=[pl.BlockSpec(memory_space=pltpu.VMEM)] + [pl.BlockSpec(memory_space=pl.ANY)] * len(before),
        out_specs=pl.BlockSpec(memory_space=pl.ANY),
        out_shape=jax.ShapeDtypeStruct((PAGE, KVH * CHUNK), jnp.bfloat16),
        scratch_shapes=[pltpu.VMEM((PAGE, CHUNK), jnp.bfloat16), pltpu.SemaphoreType.DMA],
        input_output_aliases={1: 0} if before else {},
        cost_estimate=pl.CostEstimate(flops=1, bytes_accessed=1, transcendentals=0),
    )(parts, *before)


def page_rows(me, lines, limit, slots, page_owner, page_slot, prefix_len):
    owners = page_owner[0]
    length = prefix_len[0]
    used = (length + PAGE - 1) // PAGE
    spot = jnp.arange(MAXP)
    here = (spot < used)[None] & (owners[None] // CLUSTER == jnp.arange(lines)[:, None])
    before = jnp.sum(here[:, None, :] & (spot[None, None, :] < spot[None, :, None]), axis=2)
    local = ((owners % CLUSTER) ^ (me % CLUSTER)) * slots + page_slot[0]
    chosen = here[:, :, None] & (before[:, :, None] == jnp.arange(limit)[None, None, :])
    picks = jnp.sum(jnp.where(chosen, local[None, :, None], 0), axis=1)
    counts = jnp.sum(here, axis=1)
    tail = jnp.any(here & (spot == used - 1)[None], axis=1)
    lasts = jnp.where(tail, length - (used - 1) * PAGE, PAGE)
    return jnp.concatenate([picks, counts[:, None], lasts[:, None]], axis=1)


def exchanged(array, groups):
    return lax.all_to_all(array, "serve", 0, 0, axis_index_groups=groups, tiled=True)


def after(array, *others):
    return lax.optimization_barrier((array, *others))[0]


def per_device(queries, new_kv, pool, page_owner, page_slot, prefix_len, store_slot):
    width = lax.axis_size("serve")
    lines = width // CLUSTER
    groups = [[c * CLUSTER + i for c in range(lines)] for i in range(CLUSTER)]
    me = lax.axis_index("serve")
    slots = pool.shape[0]
    capacity = (MAXP + width - 2) // (width - 1)
    limit = min(MAXP, CLUSTER * capacity)
    incoming = shifted(new_kv[0], "serve", 1)
    owns = [pool[:, :, :, :HD]]
    rest = after(pool, owns[0])
    owns += [rest[:, :, :, g * HD:(g + 1) * HD] for g in range(1, KVH)]
    sides = [swapped(own, "serve", 2) for own in owns]
    twin = swapped(rest, "serve", 1)
    rows = page_rows(me, lines, limit, slots, page_owner, page_slot, prefix_len).astype(queries.dtype)
    rows = jnp.pad(rows[:, None], ((0, 0), (0, PAGE - 1), (0, PAGE - limit - 2)))
    half = KVH // 2 * CHUNK
    early = jnp.broadcast_to(after(queries, incoming)[None, :, :half], (lines, PAGE, half))
    early = exchanged(jnp.concatenate([early, rows], axis=2), groups)
    later = after(queries, sides[0])[None, :, half:]
    later = exchanged(jnp.broadcast_to(later, (lines, PAGE, KVH * CHUNK - half)), groups)
    numbers = early[:, 0, half:half + limit + 2].astype(jnp.int32)
    tables = (numbers[:, :limit], numbers[:, limit], numbers[:, limit + 1], (me // CLUSTER)[None], store_slot[0])
    fresh = new_kv[0, 0]
    attended = None
    parts = []
    for g in range(KVH):
        side = sides[g]
        if g > 0:
            side = after(side, parts[g - 1])
        q_all, q_head = (early, g) if g < KVH // 2 else (later, g - KVH // 2)
        both = swapped(side, "serve", 1)
        pools = (owns[g], twin, side, both)
        if g == 0:
            part, pool_out = attend(g, q_head, tables, q_all, pools, fresh, pool, incoming)
        else:
            part = attend(g, q_head, tables, q_all, pools, fresh)[0]
        parts.append(part)
        attended = merge(g, exchanged(part, groups), attended)
    return (attended, pool_out)


def solution(mesh):
    return jax.shard_map(
        per_device,
        mesh=mesh,
        in_specs=(
            P(("groups", "serve"), None),
            P(("groups", "serve"), None, None, None, None),
            P(("groups", "serve"), None, None, None),
            P(("groups", "serve"), None),
            P(("groups", "serve"), None),
            P(("groups", "serve")),
            P(("groups", "serve"), None),
        ),
        out_specs=(P(("groups", "serve"), None), P(("groups", "serve"), None, None, None)),
        check_vma=False,
    )
```

```python
import functools

import jax
import jax.numpy as jnp
from jax import lax
from jax.experimental import pallas as pl
from jax.experimental.pallas import tpu as pltpu
from jax.sharding import PartitionSpec as P

PAGE = 128
KVH = 4
GQ = 5
HD = 128
MAXP = 48
SCALE = HD ** (-0.5)
LOG2E = 1.4426950408889634
LOW = -1e30
CLUSTER = 4
BLOCK = 4
STAT = 32
ROWS = GQ * PAGE + STAT
CHUNK = GQ * HD
CONTRACT_LAST = (((1,), (1,)), ((), ()))


def swapped(array, axis, bit):
    size = lax.axis_size(axis)
    return lax.ppermute(array, axis, [(i, i ^ bit) for i in range(size)])


def shifted(array, axis, by):
    size = lax.axis_size(axis)
    return lax.ppermute(array, axis, [(i, (i + by) % size) for i in range(size)])


def attend_kernel(lines, head, q_head, picks, counts, lasts, mine, store, *refs):
    q_all, own, twin, side, both, fresh = refs[:6]
    stores = len(refs) == 20
    if stores:
        pool, incoming, out, pool_out = refs[6:10]
        store_sems = refs[-1]
        scratch = refs[10:-1]
    else:
        out = refs[6]
        scratch = refs[7:]
    pages, queries, results, scores, tops, acc, q_sems, page_sems, out_sems = scratch
    slots = own.shape[0]
    columns = pl.ds(head * HD, HD)
    extra = pages.shape[1] - 1

    def request_of(t):
        return lax.rem(mine[0] - t + lines, lines)

    def q_copy(t, h):
        origin = q_all.at[request_of(t), pl.ds(0, PAGE), pl.ds((q_head * GQ + h) * HD, HD)]
        return pltpu.make_async_copy(origin, queries.at[t, h], q_sems.at[t, h])

    def out_copy(t):
        return pltpu.make_async_copy(results.at[t], out.at[request_of(t)], out_sems.at[t])

    def page_copy(source, slot, buffer, place):
        if source.shape[-1] == HD:
            origin = source.at[slot]
        else:
            origin = source.at[slot, :, :, columns]
        return pltpu.make_async_copy(origin, pages.at[buffer, place], page_sems.at[buffer, place])

    def fetch(t):
        request = request_of(t)
        buffer = lax.rem(t, 2)

        @pl.loop(0, counts[request])
        def _(place):
            code = picks[request, place]
            rank = lax.div(code, slots)
            slot = lax.rem(code, slots)
            for index, source in enumerate((own, twin, side, both)):
                @pl.when(rank == index)
                def _():
                    page_copy(source, slot, buffer, place).start()

    def arrive(t):
        buffer = lax.rem(t, 2)

        @pl.loop(0, counts[request_of(t)])
        def _(place):
            page_copy(own, 0, buffer, place).wait()

    def store_copy(slot):
        return pltpu.make_async_copy(pool.at[slot], pool_out.at[slot], store_sems.at[slot])

    fresh_copy = pltpu.make_async_copy(fresh.at[:, :, columns], pages.at[0, extra], page_sems.at[0, extra])
    for t in range(lines):
        for h in range(GQ):
            q_copy(t, h).start()
    for buffer in range(2):
        pages[buffer, :extra] = jnp.zeros((extra,) + pages.shape[2:], pages.dtype)
    fresh_copy.start()
    fetch(0)
    if lines > 1:
        fetch(1)
    if stores:
        @pl.loop(0, pool.shape[0])
        def _(slot):
            @pl.when(slot != store[0])
            def _():
                store_copy(slot).start()

        pltpu.make_async_copy(incoming.at[0], pool_out.at[store[0]], store_sems.at[store[0]]).start()

    def soften(h, scored, values):
        factor = SCALE * LOG2E
        old = tops[h]
        new = jnp.maximum(old, jnp.max(scored(), axis=1, keepdims=True))
        tops[h] = new
        fade = jnp.exp2((old - new) * factor)
        s = scored()
        wide = jnp.concatenate([new] * (s.shape[1] // PAGE), axis=1)
        expo = jnp.exp2((s - wide) * factor).astype(jnp.bfloat16)
        added = jnp.dot(expo, values, preferred_element_type=jnp.float32)
        acc[h] = acc[h] * jnp.concatenate([fade, fade], axis=1) + added

    def with_ones(values):
        return jnp.concatenate([values, jnp.ones_like(values)], axis=1)

    def score(t, h, keys):
        return lax.dot_general(queries[t, h], keys, CONTRACT_LAST, preferred_element_type=jnp.float32)

    def seen_of(t, index):
        request = request_of(t)
        return (counts[request] - 1 - index * BLOCK) * PAGE + lasts[request]

    def score_block(t, index, h, keys):
        column = lax.broadcasted_iota(jnp.int32, (PAGE, BLOCK * PAGE), 1)
        scores[h] = jnp.where(column < seen_of(t, index), score(t, h, keys), LOW)

    def keys_of(t, index):
        return pages[lax.rem(t, 2), pl.ds(index * BLOCK, BLOCK), 0].reshape(BLOCK * PAGE, HD)

    def values_of(t, index):
        return with_ones(pages[lax.rem(t, 2), pl.ds(index * BLOCK, BLOCK), 1].reshape(BLOCK * PAGE, HD))

    def blocks_of(t):
        return jnp.maximum(lax.div(counts[request_of(t)] + BLOCK - 1, BLOCK), 1)

    def reset():
        tops[...] = jnp.full(tops.shape, LOW, jnp.float32)
        acc[...] = jnp.zeros(acc.shape, jnp.float32)

    def finish(t):
        some = (counts[request_of(t)] > 0) | (t == 0)
        lane = lax.broadcasted_iota(jnp.int32, (PAGE, PAGE), 1)
        sums = jnp.ones((PAGE, PAGE), jnp.float32)
        heights = jnp.zeros((PAGE, PAGE), jnp.float32)
        for h in range(GQ):
            total = acc[h, :, HD:]
            results[t, h * PAGE:(h + 1) * PAGE, :] = (acc[h, :, :HD] * (1.0 / total)).astype(jnp.bfloat16)
            sums = jnp.where(lane == h, total, sums)
            heights = jnp.where(lane == h, tops[h], heights)
        level = heights.T[:8] * SCALE + jnp.log(sums.T[:8])
        level = jnp.where(some, level, LOW)
        high = level.astype(jnp.bfloat16).astype(jnp.float32)
        middle = (level - high).astype(jnp.bfloat16).astype(jnp.float32)
        low = level - high - middle
        stat = jnp.concatenate([high, middle, low, jnp.zeros_like(low)], axis=0)
        results[t, GQ * PAGE:, :] = stat.astype(jnp.bfloat16)
        out_copy(t).start()

    for t in range(lines):
        for h in range(GQ):
            q_copy(t, h).wait()
    fresh_copy.wait()
    reset()
    span_values = with_ones(pages[0, extra, 1])
    seen = lax.broadcasted_iota(jnp.int32, (PAGE, PAGE), 1) <= lax.broadcasted_iota(jnp.int32, (PAGE, PAGE), 0)
    for h in range(GQ):
        s = jnp.where(seen, score(0, h, pages[0, extra, 0]), LOW)
        soften(h, lambda: s, span_values)
    arrive(0)
    first = keys_of(0, 0)
    for h in range(GQ):
        score_block(0, 0, h, first)

    def step(_, carry):
        t, index = carry
        ends = index + 1 >= blocks_of(t)
        later_t = jnp.where(ends, t + 1, t)
        later_index = jnp.where(ends, 0, index + 1)
        ahead_t = jnp.minimum(later_t, lines - 1)

        @pl.when(ends & (t + 1 < lines))
        def _():
            arrive(t + 1)

        values = values_of(t, index)
        keys = keys_of(ahead_t, later_index)
        for h in range(GQ):
            soften(h, lambda: scores[h], values)
            score_block(ahead_t, later_index, h, keys)

        @pl.when(ends)
        def _():
            finish(t)
            reset()

            @pl.when(t + 2 < lines)
            def _():
                fetch(t + 2)

        return later_t, later_index

    steps = blocks_of(0)
    for t in range(1, lines):
        steps += blocks_of(t)
    lax.fori_loop(0, steps, step, (jnp.int32(0), jnp.int32(0)))
    for t in range(lines):
        out_copy(t).wait()
    if stores:
        @pl.loop(0, pool.shape[0])
        def _(slot):
            store_copy(slot).wait()


def attend(head, q_head, tables, q_all, pools, fresh, pool=None, incoming=None):
    picks, counts, lasts, mine, store = tables
    lines = q_all.shape[0]
    places = picks.shape[1]
    out_shape = [jax.ShapeDtypeStruct((lines, ROWS, HD), jnp.bfloat16)]
    scratch = [
        pltpu.VMEM((2, places + 1, 2, PAGE, HD), jnp.bfloat16),
        pltpu.VMEM((lines, GQ, PAGE, HD), jnp.bfloat16),
        pltpu.VMEM((lines, ROWS, HD), jnp.bfloat16),
        pltpu.VMEM((GQ, PAGE, BLOCK * PAGE), jnp.float32),
        pltpu.VMEM((GQ, PAGE, PAGE), jnp.float32),
        pltpu.VMEM((GQ, PAGE, 2 * HD), jnp.float32),
        pltpu.SemaphoreType.DMA((lines, GQ)),
        pltpu.SemaphoreType.DMA((2, places + 1)),
        pltpu.SemaphoreType.DMA((lines,)),
    ]
    operands = [q_all, *pools, fresh]
    if incoming is not None:
        operands += [pool, incoming]
        out_shape.append(jax.ShapeDtypeStruct(pool.shape, pool.dtype))
        scratch.append(pltpu.SemaphoreType.DMA((pool.shape[0],)))
    grid_spec = pltpu.PrefetchScalarGridSpec(
        num_scalar_prefetch=5,
        grid=(),
        in_specs=[pl.BlockSpec(memory_space=pl.ANY)] * len(operands),
        out_specs=[pl.BlockSpec(memory_space=pltpu.HBM)] * len(out_shape),
        scratch_shapes=scratch,
    )
    return pl.pallas_call(
        functools.partial(attend_kernel, lines, head, q_head),
        grid_spec=grid_spec,
        out_shape=out_shape,
        compiler_params=pltpu.CompilerParams(vmem_limit_bytes=24 * 2**20),
        cost_estimate=pl.CostEstimate(flops=1, bytes_accessed=1, transcendentals=0),
    )(picks, counts, lasts, mine, store, *operands)


def merge_kernel(head, parts, *refs):
    lines = parts.shape[0]
    out, result, sem = refs[-3:]
    levels = []
    for i in range(lines):
        block = parts[i, GQ * PAGE:, :].astype(jnp.float32)
        levels.append(block[:8] + block[8:16] + block[16:24])
    top = functools.reduce(jnp.maximum, levels)
    weights = [jnp.exp(level - top) for level in levels]
    total = functools.reduce(jnp.add, weights)
    weights = [weight / total for weight in weights]
    filler = PAGE - lines * 8
    if filler:
        weights.append(jnp.zeros((filler, PAGE), jnp.float32))
    table = jnp.concatenate(weights, axis=0).T
    for h in range(GQ):
        merged = jnp.zeros((PAGE, HD), jnp.float32)
        for i in range(lines):
            column = i * 8 + h
            merged += table[:, column:column + 1] * parts[i, h * PAGE:(h + 1) * PAGE, :].astype(jnp.float32)
        result[:, h * HD:(h + 1) * HD] = merged.astype(jnp.bfloat16)
    copy = pltpu.make_async_copy(result, out.at[:, pl.ds(head * CHUNK, CHUNK)], sem)
    copy.start()
    copy.wait()


def merge(head, parts, whole):
    before = [] if whole is None else [whole]
    return pl.pallas_call(
        functools.partial(merge_kernel, head),
        in_specs=[pl.BlockSpec(memory_space=pltpu.VMEM)] + [pl.BlockSpec(memory_space=pl.ANY)] * len(before),
        out_specs=pl.BlockSpec(memory_space=pl.ANY),
        out_shape=jax.ShapeDtypeStruct((PAGE, KVH * CHUNK), jnp.bfloat16),
        scratch_shapes=[pltpu.VMEM((PAGE, CHUNK), jnp.bfloat16), pltpu.SemaphoreType.DMA],
        input_output_aliases={1: 0} if before else {},
        cost_estimate=pl.CostEstimate(flops=1, bytes_accessed=1, transcendentals=0),
    )(parts, *before)


def page_rows(me, lines, limit, slots, page_owner, page_slot, prefix_len):
    owners = page_owner[0]
    length = prefix_len[0]
    used = (length + PAGE - 1) // PAGE
    spot = jnp.arange(MAXP)
    here = (spot < used)[None] & (owners[None] // CLUSTER == jnp.arange(lines)[:, None])
    before = jnp.sum(here[:, None, :] & (spot[None, None, :] < spot[None, :, None]), axis=2)
    local = ((owners % CLUSTER) ^ (me % CLUSTER)) * slots + page_slot[0]
    chosen = here[:, :, None] & (before[:, :, None] == jnp.arange(limit)[None, None, :])
    picks = jnp.sum(jnp.where(chosen, local[None, :, None], 0), axis=1)
    counts = jnp.sum(here, axis=1)
    tail = jnp.any(here & (spot == used - 1)[None], axis=1)
    lasts = jnp.where(tail, length - (used - 1) * PAGE, PAGE)
    return jnp.concatenate([picks, counts[:, None], lasts[:, None]], axis=1)


def exchanged(array, groups):
    return lax.all_to_all(array, "serve", 0, 0, axis_index_groups=groups, tiled=True)


def after(array, *others):
    return lax.optimization_barrier((array, *others))[0]


def per_device(queries, new_kv, pool, page_owner, page_slot, prefix_len, store_slot):
    width = lax.axis_size("serve")
    lines = width // CLUSTER
    groups = [[c * CLUSTER + i for c in range(lines)] for i in range(CLUSTER)]
    me = lax.axis_index("serve")
    slots = pool.shape[0]
    capacity = (MAXP + width - 2) // (width - 1)
    limit = min(MAXP, CLUSTER * capacity)
    incoming = shifted(new_kv[0], "serve", 1)
    owns = [pool[:, :, :, :HD]]
    rest = after(pool, owns[0])
    owns += [rest[:, :, :, g * HD:(g + 1) * HD] for g in range(1, KVH)]
    sides = [swapped(own, "serve", 2) for own in owns]
    twin = swapped(rest, "serve", 1)
    rows = page_rows(me, lines, limit, slots, page_owner, page_slot, prefix_len).astype(queries.dtype)
    rows = jnp.pad(rows[:, None], ((0, 0), (0, PAGE - 1), (0, PAGE - limit - 2)))
    half = KVH // 2 * CHUNK
    early = jnp.broadcast_to(after(queries, incoming)[None, :, :half], (lines, PAGE, half))
    early = exchanged(jnp.concatenate([early, rows], axis=2), groups)
    later = after(queries, sides[0], owns[1])[None, :, half:]
    later = exchanged(jnp.broadcast_to(later, (lines, PAGE, KVH * CHUNK - half)), groups)
    numbers = early[:, 0, half:half + limit + 2].astype(jnp.int32)
    tables = (numbers[:, :limit], numbers[:, limit], numbers[:, limit + 1], (me // CLUSTER)[None], store_slot[0])
    fresh = new_kv[0, 0]
    attended = None
    parts = []
    for g in range(KVH):
        side = sides[g]
        if g > 0:
            side = after(side, parts[g - 1])
        q_all, q_head = (early, g) if g < KVH // 2 else (later, g - KVH // 2)
        both = swapped(side, "serve", 1)
        pools = (owns[g], twin, side, both)
        if g == 0:
            part, pool_out = attend(g, q_head, tables, q_all, pools, fresh, pool, incoming)
        else:
            part = attend(g, q_head, tables, q_all, pools, fresh)[0]
        parts.append(part)
        attended = merge(g, exchanged(part, groups), attended)
    return (attended, pool_out)


def solution(mesh):
    return jax.shard_map(
        per_device,
        mesh=mesh,
        in_specs=(
            P(("groups", "serve"), None),
            P(("groups", "serve"), None, None, None, None),
            P(("groups", "serve"), None, None, None),
            P(("groups", "serve"), None),
            P(("groups", "serve"), None),
            P(("groups", "serve")),
            P(("groups", "serve"), None),
        ),
        out_specs=(P(("groups", "serve"), None), P(("groups", "serve"), None, None, None)),
        check_vma=False,
    )
```

```python
import functools

import jax
import jax.numpy as jnp
from jax import lax
from jax.experimental import pallas as pl
from jax.experimental.pallas import tpu as pltpu
from jax.sharding import PartitionSpec as P

PAGE = 128
KVH = 4
GQ = 5
HD = 128
MAXP = 48
SCALE = HD ** (-0.5)
LOG2E = 1.4426950408889634
LOW = -1e30
CLUSTER = 4
BLOCK = 4
STAT = 32
ROWS = GQ * PAGE + STAT
CHUNK = GQ * HD
CONTRACT_LAST = (((1,), (1,)), ((), ()))


def swapped(array, axis, bit):
    size = lax.axis_size(axis)
    return lax.ppermute(array, axis, [(i, i ^ bit) for i in range(size)])


def shifted(array, axis, by):
    size = lax.axis_size(axis)
    return lax.ppermute(array, axis, [(i, (i + by) % size) for i in range(size)])


def attend_kernel(lines, head, q_head, picks, counts, lasts, mine, store, *refs):
    q_all, own, twin, side, both, fresh = refs[:6]
    stores = len(refs) == 20
    if stores:
        pool, incoming, out, pool_out = refs[6:10]
        store_sems = refs[-1]
        scratch = refs[10:-1]
    else:
        out = refs[6]
        scratch = refs[7:]
    pages, queries, results, scores, tops, acc, q_sems, page_sems, out_sems = scratch
    slots = own.shape[0]
    columns = pl.ds(head * HD, HD)
    extra = pages.shape[1] - 1

    def request_of(t):
        return lax.rem(mine[0] - t + lines, lines)

    def q_copy(t, h):
        origin = q_all.at[request_of(t), pl.ds(0, PAGE), pl.ds((q_head * GQ + h) * HD, HD)]
        return pltpu.make_async_copy(origin, queries.at[t, h], q_sems.at[t, h])

    def out_copy(t):
        return pltpu.make_async_copy(results.at[t], out.at[request_of(t)], out_sems.at[t])

    def page_copy(source, slot, buffer, place):
        if source.shape[-1] == HD:
            origin = source.at[slot]
        else:
            origin = source.at[slot, :, :, columns]
        return pltpu.make_async_copy(origin, pages.at[buffer, place], page_sems.at[buffer, place])

    def fetch(t):
        request = request_of(t)
        buffer = lax.rem(t, 2)

        @pl.loop(0, counts[request])
        def _(place):
            code = picks[request, place]
            rank = lax.div(code, slots)
            slot = lax.rem(code, slots)
            for index, source in enumerate((own, twin, side, both)):
                @pl.when(rank == index)
                def _():
                    page_copy(source, slot, buffer, place).start()

    def arrive(t):
        buffer = lax.rem(t, 2)

        @pl.loop(0, counts[request_of(t)])
        def _(place):
            page_copy(own, 0, buffer, place).wait()

    def store_copy(slot):
        return pltpu.make_async_copy(pool.at[slot], pool_out.at[slot], store_sems.at[slot])

    fresh_copy = pltpu.make_async_copy(fresh.at[:, :, columns], pages.at[0, extra], page_sems.at[0, extra])
    for t in range(lines):
        for h in range(GQ):
            q_copy(t, h).start()
    for buffer in range(2):
        pages[buffer, :extra] = jnp.zeros((extra,) + pages.shape[2:], pages.dtype)
    fresh_copy.start()
    fetch(0)
    if lines > 1:
        fetch(1)
    if stores:
        @pl.loop(0, pool.shape[0])
        def _(slot):
            @pl.when(slot != store[0])
            def _():
                store_copy(slot).start()

        pltpu.make_async_copy(incoming.at[0], pool_out.at[store[0]], store_sems.at[store[0]]).start()

    def soften(h, scored, values):
        factor = SCALE * LOG2E
        old = tops[h]
        new = jnp.maximum(old, jnp.max(scored(), axis=1, keepdims=True))
        tops[h] = new
        fade = jnp.exp2((old - new) * factor)
        s = scored()
        wide = jnp.concatenate([new] * (s.shape[1] // PAGE), axis=1)
        expo = jnp.exp2((s - wide) * factor).astype(jnp.bfloat16)
        added = jnp.dot(expo, values, preferred_element_type=jnp.float32)
        acc[h] = acc[h] * jnp.concatenate([fade, fade], axis=1) + added

    def with_ones(values):
        return jnp.concatenate([values, jnp.ones_like(values)], axis=1)

    def score(t, h, keys):
        return lax.dot_general(queries[t, h], keys, CONTRACT_LAST, preferred_element_type=jnp.float32)

    def seen_of(t, index):
        request = request_of(t)
        return (counts[request] - 1 - index * BLOCK) * PAGE + lasts[request]

    def score_block(t, index, h, keys):
        column = lax.broadcasted_iota(jnp.int32, (PAGE, BLOCK * PAGE), 1)
        scores[h] = jnp.where(column < seen_of(t, index), score(t, h, keys), LOW)

    def keys_of(t, index):
        return pages[lax.rem(t, 2), pl.ds(index * BLOCK, BLOCK), 0].reshape(BLOCK * PAGE, HD)

    def values_of(t, index):
        return with_ones(pages[lax.rem(t, 2), pl.ds(index * BLOCK, BLOCK), 1].reshape(BLOCK * PAGE, HD))

    def blocks_of(t):
        return jnp.maximum(lax.div(counts[request_of(t)] + BLOCK - 1, BLOCK), 1)

    def reset():
        tops[...] = jnp.full(tops.shape, LOW, jnp.float32)
        acc[...] = jnp.zeros(acc.shape, jnp.float32)

    def finish(t):
        some = (counts[request_of(t)] > 0) | (t == 0)
        lane = lax.broadcasted_iota(jnp.int32, (PAGE, PAGE), 1)
        sums = jnp.ones((PAGE, PAGE), jnp.float32)
        heights = jnp.zeros((PAGE, PAGE), jnp.float32)
        for h in range(GQ):
            total = acc[h, :, HD:]
            results[t, h * PAGE:(h + 1) * PAGE, :] = (acc[h, :, :HD] * (1.0 / total)).astype(jnp.bfloat16)
            sums = jnp.where(lane == h, total, sums)
            heights = jnp.where(lane == h, tops[h], heights)
        level = heights.T[:8] * SCALE + jnp.log(sums.T[:8])
        level = jnp.where(some, level, LOW)
        high = level.astype(jnp.bfloat16).astype(jnp.float32)
        middle = (level - high).astype(jnp.bfloat16).astype(jnp.float32)
        low = level - high - middle
        stat = jnp.concatenate([high, middle, low, jnp.zeros_like(low)], axis=0)
        results[t, GQ * PAGE:, :] = stat.astype(jnp.bfloat16)
        out_copy(t).start()

    for t in range(lines):
        for h in range(GQ):
            q_copy(t, h).wait()
    fresh_copy.wait()
    reset()
    span_values = with_ones(pages[0, extra, 1])
    seen = lax.broadcasted_iota(jnp.int32, (PAGE, PAGE), 1) <= lax.broadcasted_iota(jnp.int32, (PAGE, PAGE), 0)
    for h in range(GQ):
        s = jnp.where(seen, score(0, h, pages[0, extra, 0]), LOW)
        soften(h, lambda: s, span_values)
    arrive(0)
    first = keys_of(0, 0)
    for h in range(GQ):
        score_block(0, 0, h, first)

    def step(_, carry):
        t, index = carry
        ends = index + 1 >= blocks_of(t)
        later_t = jnp.where(ends, t + 1, t)
        later_index = jnp.where(ends, 0, index + 1)
        ahead_t = jnp.minimum(later_t, lines - 1)

        @pl.when(ends & (t + 1 < lines))
        def _():
            arrive(t + 1)

        values = values_of(t, index)
        keys = keys_of(ahead_t, later_index)
        for h in range(GQ):
            soften(h, lambda: scores[h], values)
            score_block(ahead_t, later_index, h, keys)

        @pl.when(ends)
        def _():
            finish(t)
            reset()

            @pl.when(t + 2 < lines)
            def _():
                fetch(t + 2)

        return later_t, later_index

    steps = blocks_of(0)
    for t in range(1, lines):
        steps += blocks_of(t)
    lax.fori_loop(0, steps, step, (jnp.int32(0), jnp.int32(0)))
    for t in range(lines):
        out_copy(t).wait()
    if stores:
        @pl.loop(0, pool.shape[0])
        def _(slot):
            store_copy(slot).wait()


def attend(head, q_head, tables, q_all, pools, fresh, pool=None, incoming=None):
    picks, counts, lasts, mine, store = tables
    lines = q_all.shape[0]
    places = picks.shape[1]
    out_shape = [jax.ShapeDtypeStruct((lines, ROWS, HD), jnp.bfloat16)]
    scratch = [
        pltpu.VMEM((2, places + 1, 2, PAGE, HD), jnp.bfloat16),
        pltpu.VMEM((lines, GQ, PAGE, HD), jnp.bfloat16),
        pltpu.VMEM((lines, ROWS, HD), jnp.bfloat16),
        pltpu.VMEM((GQ, PAGE, BLOCK * PAGE), jnp.float32),
        pltpu.VMEM((GQ, PAGE, PAGE), jnp.float32),
        pltpu.VMEM((GQ, PAGE, 2 * HD), jnp.float32),
        pltpu.SemaphoreType.DMA((lines, GQ)),
        pltpu.SemaphoreType.DMA((2, places + 1)),
        pltpu.SemaphoreType.DMA((lines,)),
    ]
    operands = [q_all, *pools, fresh]
    if incoming is not None:
        operands += [pool, incoming]
        out_shape.append(jax.ShapeDtypeStruct(pool.shape, pool.dtype))
        scratch.append(pltpu.SemaphoreType.DMA((pool.shape[0],)))
    grid_spec = pltpu.PrefetchScalarGridSpec(
        num_scalar_prefetch=5,
        grid=(),
        in_specs=[pl.BlockSpec(memory_space=pl.ANY)] * len(operands),
        out_specs=[pl.BlockSpec(memory_space=pltpu.HBM)] * len(out_shape),
        scratch_shapes=scratch,
    )
    return pl.pallas_call(
        functools.partial(attend_kernel, lines, head, q_head),
        grid_spec=grid_spec,
        out_shape=out_shape,
        compiler_params=pltpu.CompilerParams(vmem_limit_bytes=24 * 2**20),
        cost_estimate=pl.CostEstimate(flops=1, bytes_accessed=1, transcendentals=0),
    )(picks, counts, lasts, mine, store, *operands)


def merge_kernel(head, parts, *refs):
    lines = parts.shape[0]
    out, result, sem = refs[-3:]
    levels = []
    for i in range(lines):
        block = parts[i, GQ * PAGE:, :].astype(jnp.float32)
        levels.append(block[:8] + block[8:16] + block[16:24])
    top = functools.reduce(jnp.maximum, levels)
    weights = [jnp.exp(level - top) for level in levels]
    total = functools.reduce(jnp.add, weights)
    weights = [weight / total for weight in weights]
    filler = PAGE - lines * 8
    if filler:
        weights.append(jnp.zeros((filler, PAGE), jnp.float32))
    table = jnp.concatenate(weights, axis=0).T
    for h in range(GQ):
        merged = jnp.zeros((PAGE, HD), jnp.float32)
        for i in range(lines):
            column = i * 8 + h
            merged += table[:, column:column + 1] * parts[i, h * PAGE:(h + 1) * PAGE, :].astype(jnp.float32)
        result[:, h * HD:(h + 1) * HD] = merged.astype(jnp.bfloat16)
    copy = pltpu.make_async_copy(result, out.at[:, pl.ds(head * CHUNK, CHUNK)], sem)
    copy.start()
    copy.wait()


def merge(head, parts, whole):
    before = [] if whole is None else [whole]
    return pl.pallas_call(
        functools.partial(merge_kernel, head),
        in_specs=[pl.BlockSpec(memory_space=pltpu.VMEM)] + [pl.BlockSpec(memory_space=pl.ANY)] * len(before),
        out_specs=pl.BlockSpec(memory_space=pl.ANY),
        out_shape=jax.ShapeDtypeStruct((PAGE, KVH * CHUNK), jnp.bfloat16),
        scratch_shapes=[pltpu.VMEM((PAGE, CHUNK), jnp.bfloat16), pltpu.SemaphoreType.DMA],
        input_output_aliases={1: 0} if before else {},
        cost_estimate=pl.CostEstimate(flops=1, bytes_accessed=1, transcendentals=0),
    )(parts, *before)


def page_rows(me, lines, limit, slots, page_owner, page_slot, prefix_len):
    owners = page_owner[0]
    length = prefix_len[0]
    used = (length + PAGE - 1) // PAGE
    spot = jnp.arange(MAXP)
    here = (spot < used)[None] & (owners[None] // CLUSTER == jnp.arange(lines)[:, None])
    before = jnp.sum(here[:, None, :] & (spot[None, None, :] < spot[None, :, None]), axis=2)
    local = ((owners % CLUSTER) ^ (me % CLUSTER)) * slots + page_slot[0]
    chosen = here[:, :, None] & (before[:, :, None] == jnp.arange(limit)[None, None, :])
    picks = jnp.sum(jnp.where(chosen, local[None, :, None], 0), axis=1)
    counts = jnp.sum(here, axis=1)
    tail = jnp.any(here & (spot == used - 1)[None], axis=1)
    lasts = jnp.where(tail, length - (used - 1) * PAGE, PAGE)
    return jnp.concatenate([picks, counts[:, None], lasts[:, None]], axis=1)


def exchanged(array, groups):
    return lax.all_to_all(array, "serve", 0, 0, axis_index_groups=groups, tiled=True)


def after(array, *others):
    return lax.optimization_barrier((array, *others))[0]


def per_device(queries, new_kv, pool, page_owner, page_slot, prefix_len, store_slot):
    width = lax.axis_size("serve")
    lines = width // CLUSTER
    groups = [[c * CLUSTER + i for c in range(lines)] for i in range(CLUSTER)]
    me = lax.axis_index("serve")
    slots = pool.shape[0]
    capacity = (MAXP + width - 2) // (width - 1)
    limit = min(MAXP, CLUSTER * capacity)
    incoming = shifted(new_kv[0], "serve", 1)
    owns = [pool[:, :, :, :HD]]
    rest = after(pool, owns[0])
    owns += [rest[:, :, :, g * HD:(g + 1) * HD] for g in range(1, KVH)]
    sides = [swapped(own, "serve", 2) for own in owns]
    twin = swapped(rest, "serve", 1)
    rows = page_rows(me, lines, limit, slots, page_owner, page_slot, prefix_len).astype(queries.dtype)
    rows = jnp.pad(rows[:, None], ((0, 0), (0, PAGE - 1), (0, PAGE - limit - 2)))
    half = CHUNK
    early = jnp.broadcast_to(after(queries, incoming)[None, :, :half], (lines, PAGE, half))
    early = exchanged(jnp.concatenate([early, rows], axis=2), groups)
    later = after(queries, sides[0], owns[1])[None, :, half:]
    later = exchanged(jnp.broadcast_to(later, (lines, PAGE, KVH * CHUNK - half)), groups)
    numbers = early[:, 0, half:half + limit + 2].astype(jnp.int32)
    tables = (numbers[:, :limit], numbers[:, limit], numbers[:, limit + 1], (me // CLUSTER)[None], store_slot[0])
    fresh = new_kv[0, 0]
    attended = None
    parts = []
    for g in range(KVH):
        side = sides[g]
        if g > 0:
            side = after(side, parts[g - 1])
        q_all, q_head = (early, 0) if g == 0 else (later, g - 1)
        both = swapped(side, "serve", 1)
        pools = (owns[g], twin, side, both)
        if g == 0:
            part, pool_out = attend(g, q_head, tables, q_all, pools, fresh, pool, incoming)
        else:
            part = attend(g, q_head, tables, q_all, pools, fresh)[0]
        parts.append(part)
        attended = merge(g, exchanged(part, groups), attended)
    return (attended, pool_out)


def solution(mesh):
    return jax.shard_map(
        per_device,
        mesh=mesh,
        in_specs=(
            P(("groups", "serve"), None),
            P(("groups", "serve"), None, None, None, None),
            P(("groups", "serve"), None, None, None),
            P(("groups", "serve"), None),
            P(("groups", "serve"), None),
            P(("groups", "serve")),
            P(("groups", "serve"), None),
        ),
        out_specs=(P(("groups", "serve"), None), P(("groups", "serve"), None, None, None)),
        check_vma=False,
    )
```
